32 devices in a mesh: ctx: 4 (over y, core), tp: 4 (over z), fsdp: 2 (over x).
Axes of the slice: x: 2, y: 2, z: 4, core: 2. Of those that a mesh axis runs over, the one named last changes fastest.
Arguments:
- tokens: bfloat16 [2, 512, 2048], P('fsdp', 'ctx'), may hold values from -6 to 6
- out_grad: bfloat16 [2, 512, 2048], P('fsdp', 'ctx'), may hold values from -6 to 6
- segment_start: int32 [2, 512], P('fsdp'), may hold values from 0 to 511, as said below
- norm_attn: bfloat16 [2048], P('fsdp'), may hold values from 0.5 to 1.5
- norm_mlp: bfloat16 [2048], P('fsdp'), may hold values from 0.5 to 1.5
- w_query: bfloat16 [2048, 2048], P('fsdp', 'tp'), may hold values from -0.125 to 0.125
- w_key: bfloat16 [2048, 2048], P('fsdp', 'tp'), may hold values from -0.125 to 0.125
- w_value: bfloat16 [2048, 2048], P('fsdp', 'tp'), may hold values from -0.125 to 0.125
- w_out: bfloat16 [2048, 2048], P('tp', 'fsdp'), may hold values from -1 to 1
- w_gate: bfloat16 [2048, 8192], P('fsdp', 'tp'), may hold values from -0.125 to 0.125
- w_up: bfloat16 [2048, 8192], P('fsdp', 'tp'), may hold values from -0.125 to 0.125
- w_down: bfloat16 [8192, 2048], P('tp', 'fsdp'), may hold values from -0.0625 to 0.0625
- mom_query: float32 [2048, 2048], P('fsdp', 'tp'), may hold values from -160 to 160
- mom_key: float32 [2048, 2048], P('fsdp', 'tp'), may hold values from -160 to 160
- mom_value: float32 [2048, 2048], P('fsdp', 'tp'), may hold values from -160 to 160
- mom_out: float32 [2048, 2048], P('tp', 'fsdp'), may hold values from -160 to 160
- mom_gate: float32 [2048, 8192], P('fsdp', 'tp'), may hold values from -160 to 160
- mom_up: float32 [2048, 8192], P('fsdp', 'tp'), may hold values from -160 to 160
- mom_down: float32 [8192, 2048], P('tp', 'fsdp'), may hold values from -160 to 160
Outputs:
- output: bfloat16 [2, 512, 2048], P('fsdp', 'ctx')
- input_grad: float32 [2, 512, 2048], P('fsdp', 'ctx')
- grad_norm_attn: float32 [2048], P('fsdp')
- grad_norm_mlp: float32 [2048], P('fsdp')
- grad_query: float32 [2048, 2048], P('fsdp', 'tp')
- grad_key: float32 [2048, 2048], P('fsdp', 'tp')
- grad_value: float32 [2048, 2048], P('fsdp', 'tp')
- grad_out: float32 [2048, 2048], P('tp', 'fsdp')
- grad_gate: float32 [2048, 8192], P('fsdp', 'tp')
- grad_up: float32 [2048, 8192], P('fsdp', 'tp')
- grad_down: float32 [8192, 2048], P('tp', 'fsdp')
- new_mom_query: float32 [2048, 2048], P('fsdp', 'tp')
- new_mom_key: float32 [2048, 2048], P('fsdp', 'tp')
- new_mom_value: float32 [2048, 2048], P('fsdp', 'tp')
- new_mom_out: float32 [2048, 2048], P('tp', 'fsdp')
- new_mom_gate: float32 [2048, 8192], P('fsdp', 'tp')
- new_mom_up: float32 [2048, 8192], P('fsdp', 'tp')
- new_mom_down: float32 [8192, 2048], P('tp', 'fsdp')
- new_query: float32 [2048, 2048], P('fsdp', 'tp')
- new_key: float32 [2048, 2048], P('fsdp', 'tp')
- new_value: float32 [2048, 2048], P('fsdp', 'tp')
- new_out: float32 [2048, 2048], P('tp', 'fsdp')
- new_gate: float32 [2048, 8192], P('fsdp', 'tp')
- new_up: float32 [2048, 8192], P('fsdp', 'tp')
- new_down: float32 [8192, 2048], P('tp', 'fsdp')
The draws below stay inside these ranges and needn't reach their ends.
Inputs may be any that keep to these rules, and one draw needn't show every extreme that they name: segment_start[g, i] is the first index in group g of the sequence that holds token i; a group's sequences are consecutive runs of 1 to 256 tokens, each group has one of exactly 256, and the last token of each group is a sequence of its own.
All inputs are finite; a program needn't handle non-finite values.
Results may differ from the reference program's by a relative error of at most 0.013.
Values may be sent and summed in bfloat16 or wider, within the bound.
No kernel may reach another device: no remote copies, remote signals or barrier semaphores. Data moves between devices by JAX's collectives and lax.ppermute only.
A program may use at most 448 MiB of HBM per device.

```python
import math
import jax
import jax.numpy as jnp
from jax import lax

D = 2048
HEADS = 32
HEAD_DIM = 64
FF = 8192
NS_STEPS = 5
GROUPS = 2
GROUP_TOK = 512
SEQ_MAX = 256
TOKENS = 1024
BLK = 512
UNITS = 16
N_TP = 4


def draw_segment_start(key, part):
    keys = jax.random.split(key, 2)
    index = jnp.arange(GROUP_TOK, dtype=jnp.int32)[None, :]
    first = jax.random.randint(keys[0], (GROUPS, 1), 0, GROUP_TOK - SEQ_MAX)
    cuts = jax.random.randint(keys[1], (GROUPS, GROUP_TOK), 0, GROUP_TOK) < 6
    inside = (index > first) & (index < first + SEQ_MAX)
    begin = cuts & jnp.logical_not(inside) | (index == 0) | (index == first) | (index == first + SEQ_MAX) | (index == GROUP_TOK - 1)
    marks = jnp.where(begin, index, 0)
    return lax.cummax(marks, axis=1).astype(jnp.int32)


def block_scale(stream_key, shape, shards, low, top_value):
    def one(dim, parts):
        draws = jax.random.uniform(jax.random.fold_in(jax.random.fold_in(stream_key, 6), dim), (parts,), jnp.float32, low / len(shards), top_value / len(shards))
        return jnp.repeat(jnp.exp(draws), shape[dim] // parts).reshape((-1,) + (1,) * (len(shape) - dim - 1))

    loudness = one(*shards[0])
    for cut in shards[1:]:
        loudness = loudness * one(*cut)
    return loudness


def bell_draw(stream_key, extent, deviation, most, shards=(), kind=jnp.bfloat16):
    gain = block_scale(stream_key, extent, shards, -0.22, 0.18) if shards else 1.0
    entries = jax.random.normal(stream_key, extent, jnp.float32) * deviation * gain
    return jnp.minimum(jnp.maximum(entries, -most), most).astype(kind)


def setup_inputs(seed: int = 0) -> dict:
    seeds = jax.random.split(jax.random.key(seed), 20)
    tokens = bell_draw(seeds[0], (GROUPS, GROUP_TOK, D), 1.0, 6.0, ((0, 2), (1, 4)))
    out_grad = bell_draw(seeds[1], (GROUPS, GROUP_TOK, D), 1.0, 6.0, ((0, 2), (1, 4)))
    segment_start = draw_segment_start(jax.random.fold_in(seeds[19], 71), 0)
    norm_attn = jnp.clip(1.0 + 0.1 * jax.random.normal(seeds[3], (D,), jnp.float32), 0.5, 1.5).astype(jnp.bfloat16)
    norm_mlp = jnp.clip(1.0 + 0.1 * jax.random.normal(seeds[4], (D,), jnp.float32), 0.5, 1.5).astype(jnp.bfloat16)
    w_query = bell_draw(seeds[5], (D, D), D ** -0.5, 0.125, ((0, 2), (1, 4)))
    w_key = bell_draw(seeds[6], (D, D), D ** -0.5, 0.125, ((0, 2), (1, 4)))
    w_value = bell_draw(seeds[7], (D, D), D ** -0.5, 0.125, ((0, 2), (1, 4)))
    w_out = bell_draw(seeds[8], (D, D), (D // 48) ** -0.5, 1.0, ((0, 4), (1, 2)))
    w_gate = bell_draw(seeds[9], (D, FF), D ** -0.5, 0.125, ((0, 2), (1, 4)))
    w_up = bell_draw(seeds[10], (D, FF), D ** -0.5, 0.125, ((0, 2), (1, 4)))
    w_down = bell_draw(seeds[11], (FF, D), FF ** -0.5, 0.0625, ((0, 4), (1, 2)))
    mom_query = bell_draw(seeds[12], (D, D), (0.8 * TOKENS ** 0.5), 160.0, ((0, 2), (1, 4)), jnp.float32)
    mom_key = bell_draw(seeds[13], (D, D), (0.8 * TOKENS ** 0.5), 160.0, ((0, 2), (1, 4)), jnp.float32)
    mom_value = bell_draw(seeds[14], (D, D), (0.8 * TOKENS ** 0.5), 160.0, ((0, 2), (1, 4)), jnp.float32)
    mom_out = bell_draw(seeds[15], (D, D), (0.8 * TOKENS ** 0.5), 160.0, ((0, 4), (1, 2)), jnp.float32)
    mom_gate = bell_draw(seeds[16], (D, FF), (0.8 * TOKENS ** 0.5), 160.0, ((0, 2), (1, 4)), jnp.float32)
    mom_up = bell_draw(seeds[17], (D, FF), (0.8 * TOKENS ** 0.5), 160.0, ((0, 2), (1, 4)), jnp.float32)
    mom_down = bell_draw(seeds[18], (FF, D), (0.8 * TOKENS ** 0.5), 160.0, ((0, 4), (1, 2)), jnp.float32)
    return dict(tokens=tokens, out_grad=out_grad, segment_start=segment_start, norm_attn=norm_attn, norm_mlp=norm_mlp, w_query=w_query, w_key=w_key, w_value=w_value, w_out=w_out, w_gate=w_gate, w_up=w_up, w_down=w_down, mom_query=mom_query, mom_key=mom_key, mom_value=mom_value, mom_out=mom_out, mom_gate=mom_gate, mom_up=mom_up, mom_down=mom_down)


@jax.custom_vjp
def low(v):
    return lax.optimization_barrier(v.astype(jnp.bfloat16)).astype(jnp.float32)

@jax.custom_vjp
def low_back(v):
    return v

def low_keep(v):
    return (low(v), None)

def low_pass(kept, grad):
    return (grad,)

def back_keep(v):
    return (v, None)

def back_low(kept, grad):
    return (low(grad),)
low.defvjp(low_keep, low_pass)
low_back.defvjp(back_keep, back_low)
EPS = 1e-05
THETA = 130000.0
MOMENTUM = 0.95
COEF_A = 3.4445
COEF_B = -4.775
COEF_C = 2.0315
RATE = 0.5
HIGH = lax.Precision.HIGHEST

def matmul(a, b):
    return jnp.dot(a, b, precision=HIGH, preferred_element_type=jnp.float32)

def rope_tables(position):
    half = HEAD_DIM // 2
    freq = THETA ** (-(jnp.arange(half, dtype=jnp.float32) * 2.0 / HEAD_DIM))
    angle = position[:, None] * freq[None, :]
    cosine = jnp.concatenate([jnp.cos(angle), jnp.cos(angle)], axis=1)
    sine = jnp.concatenate([jnp.sin(angle), jnp.sin(angle)], axis=1)
    return (cosine, sine)

def rotate(values, cosine, sine):
    half = HEAD_DIM // 2
    turned = jnp.concatenate([-values[..., half:], values[..., :half]], axis=-1)
    return values * cosine[:, None, :] + turned * sine[:, None, :]

def one_group(params, group_x, group_start):
    gain_one, gain_two, wquery, wkey, wvalue, wout, wgate, wup, wdown = params
    count = group_x.shape[0]
    index = jnp.arange(count, dtype=jnp.int32)
    cosine, sine = rope_tables((index - group_start).astype(jnp.float32))
    normed = low(group_x * lax.rsqrt(lax.optimization_barrier(jnp.mean(group_x * group_x, axis=1, keepdims=True)) + EPS) * gain_one)
    query = low(rotate(low_back(matmul(normed, wquery)).reshape(count, HEADS, HEAD_DIM), cosine, sine))
    keys = low(rotate(low_back(matmul(normed, wkey)).reshape(count, HEADS, HEAD_DIM), cosine, sine))
    values = low(low_back(matmul(normed, wvalue))).reshape(count, HEADS, HEAD_DIM)
    block = min(512, count)

    def attend(piece):
        query_block, query_index, query_start = piece
        scores = jnp.einsum('qhd,khd->hqk', query_block, keys, precision=HIGH) / math.sqrt(HEAD_DIM)
        allowed = (group_start[None, :] == query_start[:, None]) & (index[None, :] <= query_index[:, None])
        scores = low_back(jnp.where(allowed[None], scores, -1e+30))
        top = lax.optimization_barrier(jnp.max(scores, axis=2, keepdims=True))
        expo = jnp.exp(scores - top)
        prob = low(expo / lax.optimization_barrier(jnp.sum(expo, axis=2, keepdims=True)))
        return jnp.einsum('hqk,khd->qhd', prob, values, precision=HIGH)
    pieces = (query.reshape(count // block, block, HEADS, HEAD_DIM), index.reshape(count // block, block), group_start.reshape(count // block, block))
    attn = lax.map(jax.checkpoint(attend), pieces).reshape(count, D)
    attn = low(low_back(attn))
    middle = group_x + low_back(matmul(attn, wout))
    normed_two = low(middle * lax.rsqrt(lax.optimization_barrier(jnp.mean(middle * middle, axis=1, keepdims=True)) + EPS) * gain_two)
    gate = low_back(matmul(normed_two, wgate))
    upper = low_back(matmul(normed_two, wup))
    hidden = low(gate * jax.nn.sigmoid(gate) * upper)
    return middle + low_back(matmul(hidden, wdown))

def to_blocks(looks):
    lquery, lkey, lvalue, lout, lgate, lup, ldown = looks
    mult = FF // D

    def columns(matrix):
        return jnp.transpose(matrix.reshape(D, N_TP, BLK), (1, 2, 0))[:, None]

    def wide_columns(matrix):
        return jnp.transpose(matrix.reshape(D, N_TP, mult, BLK), (1, 2, 3, 0))
    return jnp.concatenate([columns(lquery), columns(lkey), columns(lvalue), lout.reshape(N_TP, 1, BLK, D), wide_columns(lgate), wide_columns(lup), ldown.reshape(N_TP, mult, BLK, D)], axis=1)

def from_blocks(blocks):
    mult = FF // D

    def columns(part):
        return jnp.transpose(part, (2, 0, 1)).reshape(D, D)

    def wide_columns(part):
        return jnp.transpose(part, (3, 0, 1, 2)).reshape(D, FF)
    return (columns(blocks[:, 0]), columns(blocks[:, 1]), columns(blocks[:, 2]), blocks[:, 3].reshape(D, D), wide_columns(blocks[:, 4:4 + mult]), wide_columns(blocks[:, 4 + mult:4 + 2 * mult]), blocks[:, 4 + 2 * mult:].reshape(FF, D))

def newton(unit):
    state = unit / (jnp.sqrt(jnp.sum(unit * unit)) + 1e-07)
    for step in range(NS_STEPS):
        gram = matmul(state, state.T)
        mixed = COEF_B * gram + COEF_C * matmul(gram, gram)
        state = COEF_A * state + matmul(mixed, state)
    return state

def reference(tokens, out_grad, segment_start, norm_attn, norm_mlp, w_query, w_key, w_value, w_out, w_gate, w_up, w_down, mom_query, mom_key, mom_value, mom_out, mom_gate, mom_up, mom_down):
    params = tuple((p.astype(jnp.float32) for p in (norm_attn, norm_mlp, w_query, w_key, w_value, w_out, w_gate, w_up, w_down)))
    inputs = tokens.astype(jnp.float32)

    def forward(xs, weights):
        return lax.map(lambda pair: one_group(weights, pair[0], pair[1]), (xs, segment_start))
    result, pullback = jax.vjp(forward, inputs, params)
    input_grad, grads = pullback(out_grad.astype(jnp.float32))
    moments = (mom_query, mom_key, mom_value, mom_out, mom_gate, mom_up, mom_down)
    matrix_grads = grads[2:]
    new_moms = tuple((MOMENTUM * m + g for m, g in zip(moments, matrix_grads)))
    looks = tuple((g + MOMENTUM * m for m, g in zip(new_moms, matrix_grads)))
    blocks = to_blocks(looks)
    flat = blocks.reshape(N_TP * UNITS, BLK, D)
    ortho = lax.map(newton, flat).reshape(N_TP, UNITS, BLK, D)
    steps = from_blocks(ortho)
    news = tuple((w - RATE * s for w, s in zip(params[2:], steps)))
    return (result.astype(jnp.bfloat16), input_grad, grads[0], grads[1], matrix_grads[0], matrix_grads[1], matrix_grads[2], matrix_grads[3], matrix_grads[4], matrix_grads[5], matrix_grads[6], new_moms[0], new_moms[1], new_moms[2], new_moms[3], new_moms[4], new_moms[5], new_moms[6], news[0], news[1], news[2], news[3], news[4], news[5], news[6])
```

```python
import functools
import math

import jax
import jax.numpy as jnp
from jax import lax
from jax.experimental import pallas as pl
from jax.experimental.pallas import tpu as pltpu
from jax.sharding import PartitionSpec as P

HEAD_DIM = 64
NS_STEPS = 5
EPS = 1e-05
THETA = 130000.0
MOMENTUM = 0.95
COEF_A = 3.4445
COEF_B = -4.775
COEF_C = 2.0315
RATE = 0.5
BF = jnp.bfloat16
F32 = jnp.float32
VMEM_LIMIT = 56 * 1024 * 1024


def dot(left, right, ldim=1, rdim=0):
    return lax.dot_general(
        left, right, (((ldim,), (rdim,)), ((), ())), preferred_element_type=F32
    )


def params():
    return pltpu.CompilerParams(vmem_limit_bytes=VMEM_LIMIT)


def cost(flops, nbytes):
    return pl.CostEstimate(flops=int(flops), bytes_accessed=int(nbytes), transcendentals=0)


def swap(value, axis, bit):
    size = lax.axis_size(axis)
    return lax.ppermute(value, axis, [(i, i ^ bit) for i in range(size)])


def ctx_parts(value):
    two = swap(value, "ctx", 2)
    return [value, swap(value, "ctx", 1), two, swap(two, "ctx", 1)]


def pair():
    return lax.axis_size("fsdp") == 2


def f_scatter_cols(value):
    size = lax.axis_size("fsdp")
    rows, width = value.shape
    part = width // size
    if size == 2:
        own = lax.axis_index("fsdp")
        mine = lax.dynamic_slice_in_dim(value, own * part, part, 1)
        other = lax.dynamic_slice_in_dim(value, (1 - own) * part, part, 1)
        return jnp.concatenate([mine, swap(other, "fsdp", 1)], axis=0)
    cut = jnp.swapaxes(value.reshape(rows, size, part), 0, 1)
    return lax.all_to_all(cut, "fsdp", 0, 0, tiled=True).reshape(size * rows, part)


def f_gather_cols(value):
    size = lax.axis_size("fsdp")
    rows = value.shape[0] // size
    if size == 2:
        own = lax.axis_index("fsdp")
        mine, other = value[:rows], swap(value[rows:], "fsdp", 1)
        return jnp.concatenate(
            [jnp.where(own == 0, mine, other), jnp.where(own == 0, other, mine)], axis=1
        )
    cut = lax.all_to_all(value.reshape(size, rows, -1), "fsdp", 0, 0, tiled=True)
    return jnp.swapaxes(cut, 0, 1).reshape(rows, -1)


def f_gather_rows(value):
    if pair():
        return jnp.concatenate([value, swap(value, "fsdp", 1)], axis=0)
    return lax.all_gather(value, "fsdp", axis=0, tiled=True)


def f_reduce_rows(value):
    size = lax.axis_size("fsdp")
    rows = value.shape[0] // size
    if size == 2:
        return value[:rows].astype(F32) + swap(value[rows:], "fsdp", 1).astype(F32)
    return lax.psum_scatter(value.astype(F32), "fsdp", scatter_dimension=0, tiled=True)


def f_gather_weight(weight, axis):
    if not pair():
        return lax.all_gather(weight, "fsdp", axis=axis, tiled=True)
    own, me = lax.axis_index("fsdp"), lax.axis_index("ctx")
    half = weight.shape[axis]
    part = half // lax.axis_size("ctx")
    piece = lax.dynamic_slice_in_dim(weight, me * part, part, axis)
    pieces = ctx_parts(swap(piece, "fsdp", 1))
    shape = list(weight.shape)
    shape[axis] = 2 * half
    full = jnp.zeros(shape, weight.dtype)
    full = lax.dynamic_update_slice_in_dim(full, weight, own * half, axis)
    for j, received in enumerate(pieces):
        full = lax.dynamic_update_slice_in_dim(
            full, received, (1 - own) * half + (me ^ j) * part, axis
        )
    return full


def f_gather_vector(vector):
    if not pair():
        return lax.all_gather(vector, "fsdp", axis=0, tiled=True)
    own = lax.axis_index("fsdp")
    other = swap(vector, "fsdp", 1)
    return jnp.where(
        own == 0, jnp.concatenate([vector, other]), jnp.concatenate([other, vector])
    )


def z_reduce(value):
    size = lax.axis_size("tp")
    rows, width = value.shape
    cut = value.astype(BF).reshape(size, rows // size, width)
    return jnp.sum(lax.all_to_all(cut, "tp", 0, 0, tiled=True).astype(F32), axis=0)


def z_gather(value):
    return lax.all_gather(value, "tp", axis=0, tiled=True)


def rope_tables(position, width):
    half = HEAD_DIM // 2
    freq = THETA ** (-(jnp.arange(half, dtype=F32) * 2.0 / HEAD_DIM))
    angle = position[:, None] * freq[None, :]
    repeat = width // half
    return jnp.tile(jnp.cos(angle), (1, repeat)), jnp.tile(jnp.sin(angle), (1, repeat))


def first_half(shape):
    lane = lax.broadcasted_iota(jnp.int32, shape, 1)
    return (lane & (HEAD_DIM - 1)) < HEAD_DIM // 2


def rotate(values, cosine, sine):
    half = HEAD_DIM // 2
    turned = jnp.where(
        first_half(values.shape), -jnp.roll(values, -half, 1), jnp.roll(values, half, 1)
    )
    return values * cosine + turned * sine


def unrotate(grads, cosine, sine):
    half = HEAD_DIM // 2
    scaled = grads * sine
    back = jnp.where(
        first_half(grads.shape), jnp.roll(scaled, -half, 1), -jnp.roll(scaled, half, 1)
    )
    return grads * cosine + back


def head_probs(query, keys, allowed, scale):
    scores = jnp.where(allowed, dot(query, keys, 1, 1) * scale, -1e30)
    top = jnp.max(scores, axis=1, keepdims=True)
    expo = jnp.exp(scores - top)
    return expo / jnp.sum(expo, axis=1, keepdims=True)


def attention_kernel(scale, q_ref, k_ref, v_ref, qi_ref, qs_ref, ki_ref, ks_ref, o_ref):
    allowed = (ks_ref[...] == qs_ref[...]) & (ki_ref[...] <= qi_ref[...])
    query, keys, values = q_ref[...], k_ref[...], v_ref[...]
    lane = lax.broadcasted_iota(jnp.int32, query.shape, 1)
    outs = []
    for head in range(2):
        mine = (lane >= HEAD_DIM) == (head == 1)
        prob = head_probs(jnp.where(mine, query, 0), keys, allowed, scale)
        outs.append(dot(prob.astype(BF), values))
    o_ref[...] = jnp.where(lane < HEAD_DIM, outs[0], outs[1]).astype(BF)


def attention_grad_kernel(
    scale, q_ref, k_ref, v_ref, g_ref, qi_ref, qs_ref, ki_ref, ks_ref, dq_ref, dk_ref, dv_ref
):
    allowed = (ks_ref[...] == qs_ref[...]) & (ki_ref[...] <= qi_ref[...])
    query, keys, values, grads = q_ref[...], k_ref[...], v_ref[...], g_ref[...]
    lane = lax.broadcasted_iota(jnp.int32, query.shape, 1)
    wide = lax.broadcasted_iota(jnp.int32, keys.shape, 1)
    dqs, dks, dvs = [], [], []
    for head in range(2):
        mine = (lane >= HEAD_DIM) == (head == 1)
        prob = head_probs(jnp.where(mine, query, 0), keys, allowed, scale)
        dprob = dot(jnp.where(mine, grads, 0), values, 1, 1)
        delta = jnp.sum(prob * dprob, axis=1, keepdims=True)
        dscore = (prob * (dprob - delta)).astype(BF)
        dqs.append(dot(dscore, keys))
        dks.append(dot(dscore, query, 0, 0))
        dvs.append(dot(prob.astype(BF), grads, 0, 0))
    low, wlow = lane < HEAD_DIM, wide < HEAD_DIM
    dq_ref[...] = jnp.where(low, dqs[0], dqs[1]) * scale
    dk_ref[...] = (jnp.where(wlow, dks[0], dks[1]) * scale).astype(BF)
    dv_ref[...] = jnp.where(wlow, dvs[0], dvs[1]).astype(BF)


def attention_specs(rows, keys):
    def col(n):
        return pl.BlockSpec((n, 2 * HEAD_DIM), lambda h: (0, h))

    def whole(shape):
        return pl.BlockSpec(shape, lambda h: (0, 0))

    marks = [whole((rows, 1)), whole((rows, 1)), whole((1, keys)), whole((1, keys))]
    return col, marks


def attention(query, keys, values, marks):
    rows, width = query.shape
    count = keys.shape[0]
    col, mark_specs = attention_specs(rows, count)
    return pl.pallas_call(
        functools.partial(attention_kernel, 1.0 / math.sqrt(HEAD_DIM)),
        grid=(width // (2 * HEAD_DIM),),
        in_specs=[col(rows), col(count), col(count)] + mark_specs,
        out_specs=col(rows),
        out_shape=jax.ShapeDtypeStruct((rows, width), BF),
        compiler_params=params(),
        cost_estimate=cost(8 * rows * count * width, 4 * count * width),
        name="attention",
    )(query, keys, values, *marks)


def attention_grad(query, keys, values, grads, marks):
    rows, width = query.shape
    count = keys.shape[0]
    col, mark_specs = attention_specs(rows, count)
    return pl.pallas_call(
        functools.partial(attention_grad_kernel, 1.0 / math.sqrt(HEAD_DIM)),
        grid=(width // (2 * HEAD_DIM),),
        in_specs=[col(rows), col(count), col(count), col(rows)] + mark_specs,
        out_specs=[col(rows), col(count), col(count)],
        out_shape=[
            jax.ShapeDtypeStruct((rows, width), F32),
            jax.ShapeDtypeStruct((count, width), BF),
            jax.ShapeDtypeStruct((count, width), BF),
        ],
        compiler_params=params(),
        cost_estimate=cost(20 * rows * count * width, 8 * count * width),
        name="attention_grad",
    )(query, keys, values, grads, *marks)


def mlp_kernel(
    x_ref, dy_ref, wg_ref, wu_ref, wd_ref, hid_ref, dg_ref, du_ref, out_ref, dx_ref, acc_o, acc_d
):
    step = pl.program_id(0)
    gate = dot(x_ref[...], wg_ref[...])
    upper = dot(x_ref[...], wu_ref[...])
    dhid = dot(dy_ref[...], wd_ref[...], 1, 1)
    sigma = jax.nn.sigmoid(gate)
    silu = gate * sigma
    hidden = (silu * upper).astype(BF)
    dgate = (dhid * upper * sigma * (1.0 + gate * (1.0 - sigma))).astype(BF)
    dup = (dhid * silu).astype(BF)
    hid_ref[...] = hidden
    dg_ref[...] = dgate
    du_ref[...] = dup
    out = dot(hidden, wd_ref[...])
    grad = dot(dgate, wg_ref[...], 1, 1) + dot(dup, wu_ref[...], 1, 1)

    @pl.when(step == 0)
    def _():
        acc_o[...] = out
        acc_d[...] = grad

    @pl.when(step > 0)
    def _():
        acc_o[...] += out
        acc_d[...] += grad

    @pl.when(step == pl.num_programs(0) - 1)
    def _():
        out_ref[...] = acc_o[...].astype(BF)
        dx_ref[...] = acc_d[...].astype(BF)


def mlp(normed, grads, wgate, wup, wdown, tile=512):
    rows, width = normed.shape
    hidden = wgate.shape[1]
    whole = pl.BlockSpec((rows, width), lambda n: (0, 0))
    cols = pl.BlockSpec((width, tile), lambda n: (0, n))
    lanes = pl.BlockSpec((rows, tile), lambda n: (0, n))
    mid = jax.ShapeDtypeStruct((rows, hidden), BF)
    res = jax.ShapeDtypeStruct((rows, width), BF)
    return pl.pallas_call(
        mlp_kernel,
        grid=(hidden // tile,),
        in_specs=[whole, whole, cols, cols, pl.BlockSpec((tile, width), lambda n: (n, 0))],
        out_specs=[lanes, lanes, lanes, whole, whole],
        out_shape=[mid, mid, mid, res, res],
        scratch_shapes=[pltpu.VMEM((rows, width), F32), pltpu.VMEM((rows, width), F32)],
        compiler_params=params(),
        cost_estimate=cost(12 * rows * width * hidden, 6 * width * hidden),
        name="mlp",
    )(normed, grads, wgate, wup, wdown)


def weight_grad_kernel(count, gained, *refs):
    lefts, rights = refs[:count], refs[count : 2 * count]
    mom_ref = refs[2 * count]
    rest = refs[2 * count + 1 :]
    total = dot(lefts[0][...], rights[0][...], 0, 0)
    for left, right in zip(lefts[1:], rights[1:]):
        total += dot(left[...], right[...], 0, 0)
    mom = MOMENTUM * mom_ref[...] + total
    if gained:
        w_ref, g_ref, m_ref, l_ref, s_ref = rest
        prod = total * w_ref[...].astype(F32)
        lanes = prod[:, :128]
        for k in range(1, prod.shape[1] // 128):
            lanes += prod[:, 128 * k : 128 * (k + 1)]

        @pl.when(pl.program_id(1) == 0)
        def _():
            s_ref[...] = lanes

        @pl.when(pl.program_id(1) > 0)
        def _():
            s_ref[...] += lanes
    else:
        g_ref, m_ref, l_ref = rest
    g_ref[...] = total
    m_ref[...] = mom
    l_ref[...] = (total + MOMENTUM * mom).astype(BF)


def weight_grad(lefts, rights, mom, weight=None, tile=(512, 512)):
    count = len(lefts)
    tok = lefts[0].shape[0]
    height, width = mom.shape
    tm, tn = min(tile[0], height), min(tile[1], width)
    out = pl.BlockSpec((tm, tn), lambda i, j: (i, j))
    in_specs = [pl.BlockSpec((tok, tm), lambda i, j: (0, i))] * count
    in_specs += [pl.BlockSpec((tok, tn), lambda i, j: (0, j))] * count + [out]
    out_specs = [out, out, out]
    out_shape = [
        jax.ShapeDtypeStruct((height, width), F32),
        jax.ShapeDtypeStruct((height, width), F32),
        jax.ShapeDtypeStruct((height, width), BF),
    ]
    args = list(lefts) + list(rights) + [mom]
    if weight is not None:
        in_specs.append(out)
        args.append(weight)
        out_specs.append(pl.BlockSpec((tm, 128), lambda i, j: (i, 0)))
        out_shape.append(jax.ShapeDtypeStruct((height, 128), F32))
    return pl.pallas_call(
        functools.partial(weight_grad_kernel, count, weight is not None),
        grid=(height // tm, width // tn),
        in_specs=in_specs,
        out_specs=out_specs,
        out_shape=out_shape,
        compiler_params=params(),
        cost_estimate=cost(2 * count * tok * height * width, 16 * height * width),
        name="weight_grad",
    )(*args)


def polynomial_kernel(a_ref, b_ref, out_ref):
    size = a_ref.shape[0]
    row = lax.broadcasted_iota(jnp.int32, (size, size), 0)
    column = lax.broadcasted_iota(jnp.int32, (size, size), 1)
    eye = row == column

    def split(full):
        only = jnp.where(eye, full, 0.0)
        return (
            jnp.where(eye, 0.0, full),
            jnp.sum(only, axis=1, keepdims=True),
            jnp.sum(only, axis=0, keepdims=True),
        )

    def times(left, right):
        loff, lcol, lrow = left
        roff, rcol, rrow = right
        full = dot(loff.astype(BF), roff.astype(BF)) + lcol * roff + loff * rrow
        off, dcol, drow = split(full)
        return off, dcol + lcol * rcol, drow + lrow * rrow

    def mix(coefs, first, second, shift):
        off = coefs[0] * first[0] + coefs[1] * second[0]
        dcol = coefs[0] * first[1] + coefs[1] * second[1] + shift
        drow = coefs[0] * first[2] + coefs[1] * second[2] + shift
        return off, dcol, drow

    gram = split(a_ref[...] + b_ref[...])
    norm = jnp.sqrt(jnp.sum(gram[2])) + 1e-07
    inverse = 1.0 / (norm * norm)
    gram = tuple(part * inverse for part in gram)
    total = None
    for step in range(NS_STEPS):
        square = times(gram, gram)
        factor = mix((COEF_B, COEF_C), gram, square, COEF_A)
        total = factor if total is None else times(factor, total)
        if step < NS_STEPS - 1:
            gram = times(factor, times(factor, gram))
    weight = -RATE / norm
    out_ref[0:size, :] = (total[0] * weight).astype(BF)
    diagonal = total[2] * weight
    high = diagonal.astype(BF)
    low = (diagonal - high.astype(F32)).astype(BF)
    line = lax.broadcasted_iota(jnp.int32, (16, size), 0)
    tail = jnp.where(line == 0, high.astype(F32), jnp.where(line == 1, low.astype(F32), 0.0))
    out_ref[size : size + 16, :] = tail.astype(BF)


def polynomial(a, b):
    size = a.shape[0]
    return pl.pallas_call(
        polynomial_kernel,
        in_specs=[pl.BlockSpec(memory_space=pltpu.VMEM)] * 2,
        out_specs=pl.BlockSpec(memory_space=pltpu.VMEM),
        out_shape=jax.ShapeDtypeStruct((size + 16, size), BF),
        compiler_params=params(),
        cost_estimate=cost(34 * size**3, 10 * size * size),
        name="polynomial",
    )(a, b)


def update_kernel(by_columns, me_ref, q_ref, l_ref, w_ref, o_ref):
    size = q_ref.shape[2]
    look = l_ref[...]
    factor = q_ref[0, :size]
    ends = q_ref[0, size:].astype(F32)
    line = ends[0:1] + ends[1:2]
    if by_columns:
        step = dot(look, factor) + look.astype(F32) * line
    else:
        eye = lax.broadcasted_iota(jnp.int32, (size, size), 0) == lax.broadcasted_iota(
            jnp.int32, (size, size), 1
        )
        column = jnp.sum(jnp.where(eye, line, 0.0), axis=1, keepdims=True)
        step = dot(factor, look) + look.astype(F32) * column
    o_ref[...] = w_ref[...].astype(F32) + step


def update(factors, look, weight, by_columns, me):
    count, _, size = factors.shape
    height, width = weight.shape
    if by_columns:
        tile = min(512, height)
        grid = (width // size, height // tile)
        spec = pl.BlockSpec((tile, size), lambda b, i, me_ref: (i, b))
    else:
        tile = min(512, width)
        grid = (height // size, width // tile)
        spec = pl.BlockSpec((size, tile), lambda b, i, me_ref: (b, i))
    return pl.pallas_call(
        functools.partial(update_kernel, by_columns),
        grid_spec=pltpu.PrefetchScalarGridSpec(
            num_scalar_prefetch=1,
            grid=grid,
            in_specs=[
                pl.BlockSpec((1, size + 16, size), lambda b, i, me_ref: (b ^ me_ref[0], 0, 0)),
                spec,
                spec,
            ],
            out_specs=spec,
        ),
        out_shape=jax.ShapeDtypeStruct(weight.shape, F32),
        compiler_params=params(),
        cost_estimate=cost(2 * size * height * width, 8 * height * width),
        name="update",
    )(me, factors, look, weight)


def gram_of(block):
    return dot(block, block, 0, 0)


def body(
    tokens,
    out_grad,
    segment_start,
    norm_attn,
    norm_mlp,
    w_query,
    w_key,
    w_value,
    w_out,
    w_gate,
    w_up,
    w_down,
    mom_query,
    mom_key,
    mom_value,
    mom_out,
    mom_gate,
    mom_up,
    mom_down,
):
    rows = tokens.shape[1]
    me = lax.axis_index("ctx")
    my_t = lax.axis_index("tp")
    my_f = lax.axis_index("fsdp")
    n_tp = lax.axis_size("tp")
    width = w_query.shape[1]
    share = w_query.shape[0]
    low_in = tokens[0]
    inputs = low_in.astype(F32)
    grad_low = out_grad[0]

    gain_one = f_gather_vector(norm_attn).astype(F32)
    gain_two = f_gather_vector(norm_mlp).astype(F32)
    inv_one = lax.rsqrt(jnp.mean(inputs * inputs, axis=1, keepdims=True) + EPS)

    spread = f_scatter_cols(low_in)
    scaled = (spread.astype(F32) * norm_attn.astype(F32)).astype(BF)
    partial = jnp.concatenate(
        [dot(scaled, w).astype(BF) for w in (w_query, w_key, w_value)], axis=1
    )
    qkv = f_reduce_rows(partial) * inv_one

    starts = segment_start[0]
    chunks = [(me ^ j) * rows for j in range(lax.axis_size("ctx"))]
    key_start = jnp.concatenate([lax.dynamic_slice_in_dim(starts, o, rows) for o in chunks])
    key_index = jnp.concatenate([o + jnp.arange(rows, dtype=jnp.int32) for o in chunks])
    query_start, query_index = key_start[:rows], key_index[:rows]
    cosine, sine = rope_tables((query_index - query_start).astype(F32), width)
    marks = (query_index[:, None], query_start[:, None], key_index[None], key_start[None])

    query = rotate(qkv[:, :width], cosine, sine).astype(BF)
    kv_own = jnp.concatenate(
        [rotate(qkv[:, width : 2 * width], cosine, sine), qkv[:, 2 * width :]], axis=1
    ).astype(BF)
    kv = jnp.concatenate(ctx_parts(kv_own), axis=0)
    keys, values = kv[:, :width], kv[:, width:]
    attn = attention(query, keys, values, marks)

    wout = f_gather_weight(w_out, 1)
    wgate = f_gather_weight(w_gate, 0)
    wup = f_gather_weight(w_up, 0)
    wdown = f_gather_weight(w_down, 1)

    piece = rows // n_tp
    own_in = lax.dynamic_slice_in_dim(inputs, my_t * piece, piece, 0)
    own_inv = lax.dynamic_slice_in_dim(inv_one, my_t * piece, piece, 0)
    own_dy = lax.dynamic_slice_in_dim(grad_low, my_t * piece, piece, 0).astype(F32)

    middle = own_in + z_reduce(dot(attn, wout))
    inv_two = lax.rsqrt(jnp.mean(middle * middle, axis=1, keepdims=True) + EPS)
    normed_two = z_gather((middle * inv_two * gain_two).astype(BF))

    hidden, dgate, dup, out_part, dx_part = mlp(normed_two, grad_low, wgate, wup, wdown)

    grad_two = z_reduce(dx_part)
    scaled_two = middle * inv_two
    weighted = grad_two * gain_two
    grad_middle = own_dy + inv_two * (
        weighted - scaled_two * jnp.mean(weighted * scaled_two, axis=1, keepdims=True)
    )
    middle_low = z_gather(grad_middle.astype(BF))
    grad_attn = dot(middle_low, wout, 1, 1).astype(BF)

    result = z_gather((middle + z_reduce(out_part)).astype(BF))

    dquery, dkeys, dvalues = attention_grad(query, keys, values, grad_attn, marks)
    dkv = jnp.concatenate([dkeys, dvalues], axis=1)
    far = dkv[: 2 * rows].astype(F32) + swap(dkv[2 * rows :], "ctx", 2).astype(F32)
    near = far[:rows] + swap(far[rows:].astype(BF), "ctx", 1).astype(F32)
    dqkv = jnp.concatenate(
        [
            unrotate(dquery, cosine, sine),
            unrotate(near[:, :width], cosine, sine),
            near[:, width:],
        ],
        axis=1,
    ).astype(BF)

    dqkv_rows = f_gather_rows(dqkv)
    dx_one = (
        dot(dqkv_rows[:, :width], w_query, 1, 1)
        + dot(dqkv_rows[:, width : 2 * width], w_key, 1, 1)
        + dot(dqkv_rows[:, 2 * width :], w_value, 1, 1)
    )
    groups = lax.axis_size("fsdp")
    cut = jnp.swapaxes(dx_one.reshape(groups, n_tp, piece, share), 0, 1)
    grad_one = f_gather_cols(z_reduce(cut.reshape(groups * rows, share)).astype(BF)).astype(F32)
    scaled_one = own_in * own_inv
    weighted = grad_one * gain_one
    input_grad = grad_middle + own_inv * (
        weighted - scaled_one * jnp.mean(weighted * scaled_one, axis=1, keepdims=True)
    )
    input_grad = z_gather(input_grad.astype(BF)).astype(F32)

    def all_rows(value):
        return ctx_parts(f_gather_rows(value))

    def all_rows_own_cols(value):
        return ctx_parts(f_scatter_cols(value))

    normed = (inputs * inv_one * gain_one).astype(BF)
    dy_all = all_rows_own_cols(grad_low)
    two_all = all_rows_own_cols(normed_two)
    hidden_all, dgate_all, dup_all = all_rows(hidden), all_rows(dgate), all_rows(dup)
    g_down, m_down, l_down = weight_grad(hidden_all, dy_all, mom_down)
    g_gate, m_gate, l_gate, s_gate = weight_grad(two_all, dgate_all, mom_gate, w_gate)
    g_up, m_up, l_up, s_up = weight_grad(two_all, dup_all, mom_up, w_up)

    one_all = all_rows_own_cols(normed)
    attn_all = all_rows(attn)
    mid_all = all_rows_own_cols(middle_low)
    dqkv_all = ctx_parts(dqkv_rows)
    g_out, m_out, l_out = weight_grad(attn_all, mid_all, mom_out)
    parts = [
        [d[:, k * width : (k + 1) * width] for d in dqkv_all] for k in range(3)
    ]
    g_query, m_query, l_query, s_query = weight_grad(one_all, parts[0], mom_query, w_query)
    g_key, m_key, l_key, s_key = weight_grad(one_all, parts[1], mom_key, w_key)
    g_value, m_value, l_value, s_value = weight_grad(one_all, parts[2], mom_value, w_value)

    gains = jnp.stack([jnp.sum(s_query + s_key + s_value, axis=1), jnp.sum(s_gate + s_up, axis=1)])
    gains = jnp.sum(lax.all_gather(gains, "tp", axis=0), axis=0)
    grad_gain_one = gains[0] / norm_attn.astype(F32)
    grad_gain_two = gains[1] / norm_mlp.astype(F32)

    size = width

    def column_block(look):
        return lax.dynamic_slice_in_dim(look, me * size, size, 1)

    gram_down = dot(
        lax.dynamic_slice_in_dim(l_down, me * size, size, 0),
        lax.dynamic_slice_in_dim(l_down, me * size, size, 0),
        1,
        1,
    )
    gram_gate = gram_of(column_block(l_gate))
    gram_up = gram_of(column_block(l_up))
    four = jnp.stack([l_query, l_key, l_value, l_out.T])
    gram_attn = gram_of(lax.dynamic_index_in_dim(four, me, 0, keepdims=False))

    if pair():
        even = my_f == 0
        q_own = polynomial(
            jnp.where(even, gram_down, gram_gate),
            swap(jnp.where(even, gram_gate, gram_down), "fsdp", 1),
        )
        q_other = swap(q_own, "fsdp", 1)
        q_down = jnp.where(even, q_own, q_other)
        q_gate = jnp.where(even, q_other, q_own)
        q_up = polynomial(gram_up, swap(gram_up, "fsdp", 1))
        q_attn = polynomial(gram_attn, swap(gram_attn, "fsdp", 1))
    else:
        grams = lax.psum(jnp.stack([gram_down, gram_gate, gram_up, gram_attn]), "fsdp")
        none = jnp.zeros_like(gram_up)
        q_down, q_gate, q_up, q_attn = (polynomial(grams[k], none) for k in range(4))

    place = me.reshape(1).astype(jnp.int32)
    zero = jnp.zeros((1,), jnp.int32)
    q_down, q_gate, q_up, q_attn = (
        jnp.stack(ctx_parts(q)) for q in (q_down, q_gate, q_up, q_attn)
    )
    new_down = update(q_down, l_down, w_down, False, place)
    new_gate = update(q_gate, l_gate, w_gate, True, place)
    new_up = update(q_up, l_up, w_up, True, place)

    def attn_factor(k):
        return lax.dynamic_index_in_dim(q_attn, me ^ k, 0)

    new_query = update(attn_factor(0), l_query, w_query, True, zero)
    new_key = update(attn_factor(1), l_key, w_key, True, zero)
    new_value = update(attn_factor(2), l_value, w_value, True, zero)
    new_out = update(attn_factor(3), l_out, w_out, False, zero)

    return (
        result[None],
        input_grad[None],
        grad_gain_one,
        grad_gain_two,
        g_query,
        g_key,
        g_value,
        g_out,
        g_gate,
        g_up,
        g_down,
        m_query,
        m_key,
        m_value,
        m_out,
        m_gate,
        m_up,
        m_down,
        new_query,
        new_key,
        new_value,
        new_out,
        new_gate,
        new_up,
        new_down,
    )


def solution(mesh):
    act = P("fsdp", "ctx", None)
    col, row, vec = P("fsdp", "tp"), P("tp", "fsdp"), P("fsdp")
    seven = (col, col, col, row, col, col, row)
    in_specs = (act, act, P("fsdp", None), vec, vec) + seven + seven
    out_specs = (act, act, vec, vec) + seven + seven + seven
    return jax.shard_map(body, mesh=mesh, in_specs=in_specs, out_specs=out_specs, check_vma=False)
```

```python
import functools
import math

import jax
import jax.numpy as jnp
from jax import lax
from jax.experimental import pallas as pl
from jax.experimental.pallas import tpu as pltpu
from jax.sharding import PartitionSpec as P

HEAD_DIM = 64
NS_STEPS = 5
EPS = 1e-05
THETA = 130000.0
MOMENTUM = 0.95
COEF_A = 3.4445
COEF_B = -4.775
COEF_C = 2.0315
RATE = 0.5
BF = jnp.bfloat16
F32 = jnp.float32
VMEM_LIMIT = 56 * 1024 * 1024


def dot(left, right, ldim=1, rdim=0):
    return lax.dot_general(
        left, right, (((ldim,), (rdim,)), ((), ())), preferred_element_type=F32
    )


def params():
    return pltpu.CompilerParams(vmem_limit_bytes=VMEM_LIMIT)


def cost(flops, nbytes):
    return pl.CostEstimate(flops=int(flops), bytes_accessed=int(nbytes), transcendentals=0)


def swap(value, axis, bit):
    size = lax.axis_size(axis)
    return lax.ppermute(value, axis, [(i, i ^ bit) for i in range(size)])


def later(value, *others):
    return lax.optimization_barrier((value, others))[0]


def ctx_two(value):
    return [value, swap(value, "ctx", 2)]


def ctx_four(two):
    value, far = two
    return [value, swap(value, "ctx", 1), far, swap(far, "ctx", 1)]


def ctx_parts(value):
    return ctx_four(ctx_two(value))


def pair():
    return lax.axis_size("fsdp") == 2


def f_scatter_cols(value):
    size = lax.axis_size("fsdp")
    rows, width = value.shape
    part = width // size
    if size == 2:
        own = lax.axis_index("fsdp")
        mine = lax.dynamic_slice_in_dim(value, own * part, part, 1)
        other = lax.dynamic_slice_in_dim(value, (1 - own) * part, part, 1)
        return jnp.concatenate([mine, swap(other, "fsdp", 1)], axis=0)
    cut = jnp.swapaxes(value.reshape(rows, size, part), 0, 1)
    return lax.all_to_all(cut, "fsdp", 0, 0, tiled=True).reshape(size * rows, part)


def f_gather_cols(value):
    size = lax.axis_size("fsdp")
    rows = value.shape[0] // size
    if size == 2:
        own = lax.axis_index("fsdp")
        mine, other = value[:rows], swap(value[rows:], "fsdp", 1)
        return jnp.concatenate(
            [jnp.where(own == 0, mine, other), jnp.where(own == 0, other, mine)], axis=1
        )
    cut = lax.all_to_all(value.reshape(size, rows, -1), "fsdp", 0, 0, tiled=True)
    return jnp.swapaxes(cut, 0, 1).reshape(rows, -1)


def f_gather_rows(value):
    if pair():
        return jnp.concatenate([value, swap(value, "fsdp", 1)], axis=0)
    return lax.all_gather(value, "fsdp", axis=0, tiled=True)


def f_reduce_rows(value):
    size = lax.axis_size("fsdp")
    rows = value.shape[0] // size
    if size == 2:
        return value[:rows].astype(F32) + swap(value[rows:].astype(BF), "fsdp", 1).astype(F32)
    return lax.psum_scatter(value.astype(F32), "fsdp", scatter_dimension=0, tiled=True)


def flip(value):
    half = value.shape[0] // 2
    return jnp.concatenate([value[half:], value[:half]], axis=0)


def f_all(value):
    if pair():
        return value + flip(swap(value, "fsdp", 1))
    return lax.psum(value, "fsdp")


def f_reduce_list(parts):
    rows = parts[0].shape[0] // 2
    sent = jnp.concatenate([p[rows:].astype(BF) for p in parts], axis=1)
    return jnp.concatenate([p[:rows] for p in parts], axis=1) + swap(sent, "fsdp", 1).astype(F32)


def z_shift(value, k):
    size = lax.axis_size("tp")
    return lax.ppermute(value, "tp", [(i, (i + k) % size) for i in range(size)])


def z_shifts():
    size = lax.axis_size("tp")
    return sorted(range(1, size), key=lambda k: -min(k, size - k))


def by_quarter(value):
    size, groups = lax.axis_size("tp"), lax.axis_size("fsdp")
    rows, width = value.shape
    part = rows // (size * groups)
    cut = jnp.swapaxes(value.reshape(groups, size, part, width), 0, 1)
    return cut.reshape(size, groups * part, width)


def own_quarter(value):
    return lax.dynamic_index_in_dim(by_quarter(value), lax.axis_index("tp"), 0, keepdims=False)


def z_reduce(value):
    sent = by_quarter(value.astype(BF))
    return jnp.sum(lax.all_to_all(sent, "tp", 0, 0, tiled=True).astype(F32), axis=0)


def z_gather(value):
    size, groups = lax.axis_size("tp"), lax.axis_size("fsdp")
    rows, width = value.shape
    full = lax.all_gather(value, "tp", axis=0)
    full = jnp.swapaxes(full.reshape(size, groups, rows // groups, width), 0, 1)
    return full.reshape(size * rows, width)


def z_reduce_slow(value):
    size, me = lax.axis_size("tp"), lax.axis_index("tp")
    cut = by_quarter(value)
    total = lax.dynamic_index_in_dim(cut, me, 0, keepdims=False).astype(F32)
    for k in z_shifts():
        sent = lax.dynamic_index_in_dim(cut, (me + k) % size, 0, keepdims=False).astype(BF)
        total = total + z_shift(sent, k).astype(F32)
    return total


def z_gather_groups_slow(value, wait=()):
    size, groups = lax.axis_size("tp"), lax.axis_size("fsdp")
    rows, width = value.shape
    full = z_gather_slow(value, wait).reshape(size, groups, rows // groups, width)
    return jnp.swapaxes(full, 0, 1).reshape(size * rows, width)


def z_gather_slow(value, wait=()):
    size, me = lax.axis_size("tp"), lax.axis_index("tp")
    by_place = {k: later(z_shift(value, k), wait) for k in z_shifts()}
    by_place[0] = value
    ordered = []
    for at in range(size):
        chosen = value
        for k in z_shifts():
            chosen = jnp.where((me - k) % size == at, by_place[k], chosen)
        ordered.append(chosen)
    return jnp.concatenate(ordered, axis=0)


def all_sum(value, axes):
    for axis in axes:
        size = lax.axis_size(axis)
        if axis == "tp":
            value = value + sum(z_shift(value, k) for k in z_shifts())
        else:
            bit = 1
            while bit < size:
                value = value + swap(value, axis, bit)
                bit *= 2
    return value


def rope_tables(position, width):
    half = HEAD_DIM // 2
    freq = THETA ** (-(jnp.arange(half, dtype=F32) * 2.0 / HEAD_DIM))
    angle = position[:, None] * freq[None, :]
    repeat = width // half
    return jnp.tile(jnp.cos(angle), (1, repeat)), jnp.tile(jnp.sin(angle), (1, repeat))


def first_half(shape):
    lane = lax.broadcasted_iota(jnp.int32, shape, 1)
    return (lane & (HEAD_DIM - 1)) < HEAD_DIM // 2


def rotate(values, cosine, sine):
    half = HEAD_DIM // 2
    turned = jnp.where(
        first_half(values.shape), -jnp.roll(values, -half, 1), jnp.roll(values, half, 1)
    )
    return values * cosine + turned * sine


def unrotate(grads, cosine, sine):
    half = HEAD_DIM // 2
    scaled = grads * sine
    back = jnp.where(
        first_half(grads.shape), jnp.roll(scaled, -half, 1), -jnp.roll(scaled, half, 1)
    )
    return grads * cosine + back


def head_probs(query, keys, allowed, scale):
    scores = jnp.where(allowed, dot(query, keys, 1, 1) * scale, -1e30)
    top = jnp.max(scores, axis=1, keepdims=True)
    expo = jnp.exp(scores - top)
    return expo / jnp.sum(expo, axis=1, keepdims=True)


def attention_kernel(scale, q_ref, k_ref, v_ref, qi_ref, qs_ref, ki_ref, ks_ref, o_ref):
    allowed = (ks_ref[...] == qs_ref[...]) & (ki_ref[...] <= qi_ref[...])
    query, keys, values = q_ref[...], k_ref[...], v_ref[...]
    lane = lax.broadcasted_iota(jnp.int32, query.shape, 1)
    outs = []
    for head in range(2):
        mine = (lane >= HEAD_DIM) == (head == 1)
        prob = head_probs(jnp.where(mine, query, 0), keys, allowed, scale)
        outs.append(dot(prob.astype(BF), values))
    o_ref[...] = jnp.where(lane < HEAD_DIM, outs[0], outs[1]).astype(BF)


def attention_grad_kernel(
    scale, q_ref, k_ref, v_ref, g_ref, qi_ref, qs_ref, ki_ref, ks_ref, dq_ref, dk_ref, dv_ref
):
    allowed = (ks_ref[...] == qs_ref[...]) & (ki_ref[...] <= qi_ref[...])
    query, keys, values, grads = q_ref[...], k_ref[...], v_ref[...], g_ref[...]
    lane = lax.broadcasted_iota(jnp.int32, query.shape, 1)
    wide = lax.broadcasted_iota(jnp.int32, keys.shape, 1)
    dqs, dks, dvs = [], [], []
    for head in range(2):
        mine = (lane >= HEAD_DIM) == (head == 1)
        prob = head_probs(jnp.where(mine, query, 0), keys, allowed, scale)
        dprob = dot(jnp.where(mine, grads, 0), values, 1, 1)
        delta = jnp.sum(prob * dprob, axis=1, keepdims=True)
        dscore = (prob * (dprob - delta)).astype(BF)
        dqs.append(dot(dscore, keys))
        dks.append(dot(dscore, query, 0, 0))
        dvs.append(dot(prob.astype(BF), grads, 0, 0))
    low, wlow = lane < HEAD_DIM, wide < HEAD_DIM
    dq_ref[...] = jnp.where(low, dqs[0], dqs[1]) * scale
    dk_ref[...] = (jnp.where(wlow, dks[0], dks[1]) * scale).astype(BF)
    dv_ref[...] = jnp.where(wlow, dvs[0], dvs[1]).astype(BF)


def attention_specs(rows, keys):
    def col(n):
        return pl.BlockSpec((n, 2 * HEAD_DIM), lambda h: (0, h))

    def whole(shape):
        return pl.BlockSpec(shape, lambda h: (0, 0))

    marks = [whole((rows, 1)), whole((rows, 1)), whole((1, keys)), whole((1, keys))]
    return col, marks


def attention(query, keys, values, marks):
    rows, width = query.shape
    count = keys.shape[0]
    col, mark_specs = attention_specs(rows, count)
    return pl.pallas_call(
        functools.partial(attention_kernel, 1.0 / math.sqrt(HEAD_DIM)),
        grid=(width // (2 * HEAD_DIM),),
        in_specs=[col(rows), col(count), col(count)] + mark_specs,
        out_specs=col(rows),
        out_shape=jax.ShapeDtypeStruct((rows, width), BF),
        compiler_params=params(),
        cost_estimate=cost(8 * rows * count * width, 4 * count * width),
        name="attention",
    )(query, keys, values, *marks)


def attention_grad(query, keys, values, grads, marks):
    rows, width = query.shape
    count = keys.shape[0]
    col, mark_specs = attention_specs(rows, count)
    return pl.pallas_call(
        functools.partial(attention_grad_kernel, 1.0 / math.sqrt(HEAD_DIM)),
        grid=(width // (2 * HEAD_DIM),),
        in_specs=[col(rows), col(count), col(count), col(rows)] + mark_specs,
        out_specs=[col(rows), col(count), col(count)],
        out_shape=[
            jax.ShapeDtypeStruct((rows, width), F32),
            jax.ShapeDtypeStruct((count, width), BF),
            jax.ShapeDtypeStruct((count, width), BF),
        ],
        compiler_params=params(),
        cost_estimate=cost(20 * rows * count * width, 8 * count * width),
        name="attention_grad",
    )(query, keys, values, grads, *marks)


def smem():
    return pl.BlockSpec(memory_space=pltpu.SMEM)


def units_kernel(x_ref, wg_ref, wu_ref, own_ref, sent_ref):
    for k, w_ref in enumerate((wg_ref, wu_ref)):
        part = dot(x_ref[...], w_ref[...])
        own_ref[k] = part
        sent_ref[k] = part.astype(BF)


def units(x, wgate, wup, at, count, tile=512):
    rows, depth = x.shape
    steps = count // tile
    weight = pl.BlockSpec((depth, tile), lambda n: (0, at * steps + n))
    out = pl.BlockSpec((2, rows, tile), lambda n: (0, 0, n))
    return pl.pallas_call(
        units_kernel,
        grid=(steps,),
        in_specs=[pl.BlockSpec((rows, depth), lambda n: (0, 0)), weight, weight],
        out_specs=[out, out],
        out_shape=[
            jax.ShapeDtypeStruct((2, rows, count), F32),
            jax.ShapeDtypeStruct((2, rows, count), BF),
        ],
        compiler_params=params(),
        cost_estimate=cost(1, 1),
        name="units",
    )(x, wgate, wup)


def hidden_kernel(paired, first, own_ref, got_ref, dh_ref, dgot_ref, wg_ref, wu_ref, *refs):
    if first:
        out_ref, acc_ref = refs
    else:
        before_ref, out_ref, acc_ref = refs
    half = dh_ref.shape[0] // 2

    def total(own, got):
        if not paired:
            return own
        got = got.astype(F32)
        return own + jnp.concatenate([got[half:], got[:half]], axis=0)

    gate = total(own_ref[0], got_ref[0])
    upper = total(own_ref[1], got_ref[1])
    dhid = total(dh_ref[...], dgot_ref[...])
    sigma = jax.nn.sigmoid(gate)
    silu = gate * sigma
    dgate = (dhid * upper * sigma * (1.0 + gate * (1.0 - sigma))).astype(BF)
    dup = (dhid * silu).astype(BF)
    out_ref[0] = (silu * upper).astype(BF)
    out_ref[1] = dgate
    out_ref[2] = dup
    grad = dot(dgate, wg_ref[...], 1, 1) + dot(dup, wu_ref[...], 1, 1)

    @pl.when(pl.program_id(0) == 0)
    def _():
        acc_ref[...] = grad if first else grad + before_ref[...]

    @pl.when(pl.program_id(0) > 0)
    def _():
        acc_ref[...] += grad


def hidden_units(own, got, dhid, dgot, wgate, wup, at, before=None, tile=512):
    _, rows, count = own.shape
    depth = wgate.shape[0]
    steps = count // tile
    weight = pl.BlockSpec((depth, tile), lambda n: (0, at * steps + n))
    trio = pl.BlockSpec((2, rows, tile), lambda n: (0, 0, n))
    lanes = pl.BlockSpec((rows, tile), lambda n: (0, at * steps + n))
    total = pl.BlockSpec((rows, depth), lambda n: (0, 0))
    args = [own, got, dhid, dgot, wgate, wup] + ([] if before is None else [before])
    return pl.pallas_call(
        functools.partial(hidden_kernel, pair(), before is None),
        grid=(steps,),
        in_specs=[trio, trio, lanes, lanes, weight, weight] + [total] * (len(args) - 6),
        out_specs=[pl.BlockSpec((3, rows, tile), lambda n: (0, 0, n)), total],
        out_shape=[
            jax.ShapeDtypeStruct((3, rows, count), BF),
            jax.ShapeDtypeStruct((rows, depth), F32),
        ],
        compiler_params=params(),
        cost_estimate=cost(1, 1),
        name="hidden_units",
    )(*args)


def joined(parts):
    return jnp.concatenate([r[...].reshape(r.shape[-2:]) for r in parts], axis=0)


def moved(total, mom_ref, g_ref, m_ref, l_ref):
    mom = MOMENTUM * mom_ref[...] + total
    g_ref[...] = total
    m_ref[...] = mom
    l_ref[...] = (total + MOMENTUM * mom).astype(BF)


def add_gram(gram_ref, look_ref, by_columns, hit, first):
    half = gram_ref.shape[1]

    def three():
        if by_columns:
            low, high = look_ref[:, :half], look_ref[:, half:]
        else:
            low, high = look_ref[:half, :], look_ref[half:, :]
        dim = 0 if by_columns else 1
        return [dot(x, y, dim, dim) for x, y in ((low, low), (low, high), (high, high))]

    @pl.when(jnp.logical_and(hit, first))
    def _():
        for k, value in enumerate(three()):
            gram_ref[k] = value

    @pl.when(jnp.logical_and(hit, jnp.logical_not(first)))
    def _():
        for k, value in enumerate(three()):
            gram_ref[k] += value


def gram_spec(size):
    half = size // 2
    return (
        pl.BlockSpec((3, half, half), lambda *at: (0, 0, 0)),
        jax.ShapeDtypeStruct((3, half, half), F32),
    )


def weight_grad_kernel(nl, nr, by_columns, base, filled, place_ref, *refs):
    lefts, rights = refs[:nl], refs[nl : nl + nr]
    mom_ref, g_ref, m_ref, l_ref, gram_ref = refs[nl + nr], *refs[-4:]
    tall, wide = g_ref.shape
    moved(dot(joined(lefts), joined(rights), 0, 0), mom_ref, g_ref, m_ref, l_ref)
    i, j = pl.program_id(0), pl.program_id(1)
    outer, inner = (j, i) if by_columns else (i, j)
    size = 2 * gram_ref.shape[1]
    count = (wide if by_columns else tall) // size

    if filled:

        @pl.when(jnp.logical_and(i == 0, j == 0))
        def _():
            gram_ref[...] = refs[nl + nr + 4][...]

    for k in range(count):
        at = pl.ds(k * size, size)
        look = l_ref.at[:, at] if by_columns else l_ref.at[at, :]
        add_gram(gram_ref, look, by_columns, base + outer * count + k == place_ref[0], inner == 0)


def weight_grad(
    place, lefts, rights, mom, size, by_columns, tile, planes=(None, None), span=None, into=None
):
    height, width = mom.shape
    part, parts = span or (0, 1)
    tm, tn = min(tile[0], height), min(tile[1], width)
    grid = [height // tm, width // tn]
    axis = 1 if by_columns else 0
    grid[axis] //= parts
    start = [0, 0]
    start[axis] = part * grid[axis]
    out = pl.BlockSpec((tm, tn), lambda i, j: (start[0] + i, start[1] + j))
    tok = sum(v.shape[-2] for v in lefts)

    def specs(values, plane, lanes, place_of):
        if plane is None:
            return [pl.BlockSpec((v.shape[0], lanes), lambda i, j: (0, place_of(i, j))) for v in values]
        return [
            pl.BlockSpec((1, v.shape[1], lanes), lambda i, j: (plane, 0, place_of(i, j)))
            for v in values
        ]

    whole_gram, gram_shape = gram_spec(size)
    in_specs = [smem()]
    in_specs += specs(lefts, planes[0], tm, lambda i, j: i)
    in_specs += specs(rights, planes[1], tn, lambda i, j: j)
    in_specs += [out]
    args = [place, *lefts, *rights, mom]
    aliases = {}
    if into is not None:
        aliases = {len(args) + k: k for k in range(3)}
        in_specs += [pl.BlockSpec(memory_space=pl.ANY)] * 3 + [whole_gram]
        args += list(into)
    blocks = (width if by_columns else height) // size // parts
    return pl.pallas_call(
        functools.partial(
            weight_grad_kernel, len(lefts), len(rights), by_columns, part * blocks, into is not None
        ),
        grid=tuple(grid),
        in_specs=in_specs,
        out_specs=[out, out, out, whole_gram],
        out_shape=[
            jax.ShapeDtypeStruct((height, width), F32),
            jax.ShapeDtypeStruct((height, width), F32),
            jax.ShapeDtypeStruct((height, width), BF),
            gram_shape,
        ],
        input_output_aliases=aliases,
        compiler_params=params(),
        cost_estimate=cost(2 * tok * height * width // parts, 14 * height * width // parts),
        name="weight_grad",
    )(*args)


def attention_weights_kernel(count, place_ref, *refs):
    ones, grads, attns, mids = (refs[k * count : (k + 1) * count] for k in range(4))
    refs = refs[4 * count :]
    moms, outs, gram_ref = refs[:4], refs[4:16], refs[16]
    first = pl.program_id(0) == 0
    left = joined(ones)
    width = moms[0].shape[1]
    for k in range(3):
        right = jnp.concatenate([r[:, k * width : (k + 1) * width] for r in grads], axis=0)
        moved(dot(left, right, 0, 0), moms[k], *outs[3 * k : 3 * k + 3])
        add_gram(gram_ref, outs[3 * k + 2], True, place_ref[0] == k, first)
    moved(dot(joined(attns), joined(mids), 0, 0), moms[3], *outs[9:12])
    add_gram(gram_ref, outs[11], False, place_ref[0] == 3, first)


def attention_weights(place, ones, grads, attns, mids, moms, tile=256):
    share, width = moms[0].shape
    tile = min(tile, share)

    def cols(v):
        return pl.BlockSpec((v.shape[0], tile), lambda i: (0, i))

    def whole(v):
        return pl.BlockSpec(v.shape, lambda i: (0, 0))

    tall = pl.BlockSpec((tile, width), lambda i: (i, 0))
    wide = pl.BlockSpec((width, tile), lambda i: (0, i))
    gram, gram_shape = gram_spec(width)
    shapes = []
    for mom in moms:
        shapes += [jax.ShapeDtypeStruct(mom.shape, kind) for kind in (F32, F32, BF)]
    out = pl.pallas_call(
        functools.partial(attention_weights_kernel, len(ones)),
        grid=(share // tile,),
        in_specs=[smem()]
        + [cols(v) for v in ones]
        + [whole(v) for v in grads]
        + [whole(v) for v in attns]
        + [cols(v) for v in mids]
        + [tall, tall, tall, wide],
        out_specs=[tall] * 9 + [wide] * 3 + [gram],
        out_shape=shapes + [gram_shape],
        compiler_params=params(),
        cost_estimate=cost(8 * len(ones) * ones[0].shape[0] * share * width, 56 * share * width),
        name="attention_weights",
    )(place, *ones, *grads, *attns, *mids, *moms)
    return out[:3], out[3:6], out[6:9], out[9:12], out[12]


def mlp_weights_kernel(count, base, filled, place_ref, *refs):
    twos, hids, dgates, dups, dys = (refs[k * count : (k + 1) * count] for k in range(5))
    refs = refs[5 * count :]
    moms, refs = refs[:3], refs[3:]
    before, refs = (refs[9:12], refs[12:]) if filled else (None, refs)
    outs, grams = refs[:9], refs[9:]
    j, i = pl.program_id(0), pl.program_id(1)

    if filled:

        @pl.when(jnp.logical_and(i == 0, j == 0))
        def _():
            for gram_ref, old in zip(grams, before):
                gram_ref[...] = old[...]

    two = joined(twos)
    hit, first = base + j == place_ref[0], i == 0
    moved(dot(two, joined(dgates), 0, 0), moms[0], *outs[:3])
    add_gram(grams[0], outs[2], True, hit, first)
    moved(dot(two, joined(dups), 0, 0), moms[1], *outs[3:6])
    add_gram(grams[1], outs[5], True, hit, first)
    moved(dot(joined(hids), joined(dys), 0, 0), moms[2], *outs[6:9])
    add_gram(grams[2], outs[8], False, hit, first)


def mlp_weights(place, twos, trios, dys, moms, size, span, into, tile=512):
    share, width = moms[0].shape
    part, parts = span
    blocks = width // size // parts
    tile = min(tile, share)

    def cols(v):
        return pl.BlockSpec((v.shape[0], tile), lambda j, i: (0, i))

    def plane(v, k):
        return pl.BlockSpec((1, v.shape[1], size), lambda j, i: (k, 0, j))

    tall = pl.BlockSpec((tile, size), lambda j, i: (i, part * blocks + j))
    wide = pl.BlockSpec((size, tile), lambda j, i: (part * blocks + j, i))
    gram, gram_shape = gram_spec(size)
    shapes = []
    for mom in moms:
        shapes += [jax.ShapeDtypeStruct(mom.shape, kind) for kind in (F32, F32, BF)]
    in_specs = [smem()] + [cols(v) for v in twos]
    for k in range(3):
        in_specs += [plane(v, k) for v in trios]
    in_specs += [cols(v) for v in dys] + [tall, tall, wide]
    args = [place, *twos, *trios, *trios, *trios, *dys, *moms]
    aliases = {len(args) + k: k for k in range(9)}
    in_specs += [pl.BlockSpec(memory_space=pl.ANY)] * 9 + [gram] * 3
    args += [v for out in into for v in out[:3]] + [out[3] for out in into]
    tok = sum(v.shape[0] for v in twos)
    out = pl.pallas_call(
        functools.partial(mlp_weights_kernel, len(twos), part * blocks, True),
        grid=(blocks, share // tile),
        in_specs=in_specs,
        out_specs=[tall] * 6 + [wide] * 3 + [gram] * 3,
        out_shape=shapes + [gram_shape] * 3,
        input_output_aliases=aliases,
        compiler_params=params(),
        cost_estimate=cost(6 * tok * share * width // parts, 42 * share * width // parts),
        name="mlp_weights",
    )(*args)
    return [(*out[3 * k : 3 * k + 3], out[9 + k]) for k in range(3)]


def polynomial_kernel(a_ref, b_ref, out_ref, full_ref):
    size, half = full_ref.shape[0], full_ref.shape[0] // 2
    corner = a_ref[1] + b_ref[1]
    full_ref[:half, :half] = a_ref[0] + b_ref[0]
    full_ref[:half, half:] = corner
    full_ref[half:, :half] = corner.T
    full_ref[half:, half:] = a_ref[2] + b_ref[2]
    row = lax.broadcasted_iota(jnp.int32, (size, size), 0)
    column = lax.broadcasted_iota(jnp.int32, (size, size), 1)
    eye = row == column

    def split(full):
        only = jnp.where(eye, full, 0.0)
        return (
            jnp.where(eye, 0.0, full),
            jnp.sum(only, axis=1, keepdims=True),
            jnp.sum(only, axis=0, keepdims=True),
        )

    def times(left, right):
        loff, lcol, lrow = left
        roff, rcol, rrow = right
        full = dot(loff.astype(BF), roff.astype(BF)) + lcol * roff + loff * rrow
        off, dcol, drow = split(full)
        return off, dcol + lcol * rcol, drow + lrow * rrow

    def mix(coefs, first, second, shift):
        off = coefs[0] * first[0] + coefs[1] * second[0]
        dcol = coefs[0] * first[1] + coefs[1] * second[1] + shift
        drow = coefs[0] * first[2] + coefs[1] * second[2] + shift
        return off, dcol, drow

    gram = split(full_ref[...])
    norm = jnp.sqrt(jnp.sum(gram[2])) + 1e-07
    inverse = 1.0 / (norm * norm)
    gram = tuple(part * inverse for part in gram)
    total = None
    for step in range(NS_STEPS):
        square = times(gram, gram)
        factor = mix((COEF_B, COEF_C), gram, square, COEF_A)
        total = factor if total is None else times(factor, total)
        if step < NS_STEPS - 1:
            gram = times(factor, times(factor, gram))
    weight = -RATE / norm
    off = (total[0] * weight).astype(BF)
    out_ref[:half] = off[:half, :half]
    out_ref[half:size] = off[:half, half:]
    out_ref[size : size + half] = off[half:, half:]
    diagonal = total[2] * weight
    high = diagonal.astype(BF).astype(F32)
    low = diagonal - high
    line = lax.broadcasted_iota(jnp.int32, (16, half), 0)
    tail = jnp.zeros((16, half), F32)
    for k, part in enumerate((high[:, :half], high[:, half:], low[:, :half], low[:, half:])):
        tail = jnp.where(line == k, part, tail)
    out_ref[size + half :] = tail.astype(BF)


def polynomial(a, b):
    half = a.shape[1]
    size = 2 * half
    return pl.pallas_call(
        polynomial_kernel,
        in_specs=[pl.BlockSpec(memory_space=pltpu.VMEM)] * 2,
        out_specs=pl.BlockSpec(memory_space=pltpu.VMEM),
        out_shape=jax.ShapeDtypeStruct((3 * half + 16, half), BF),
        scratch_shapes=[pltpu.VMEM((size, size), F32)],
        compiler_params=params(),
        cost_estimate=cost(34 * size**3, 10 * size * size),
        name="polynomial",
    )(a, b)


def unpack(packed, factor_ref, column):
    half = packed.shape[1]
    corner = packed[half : 2 * half]
    factor_ref[:half, :half] = packed[:half]
    factor_ref[:half, half:] = corner
    factor_ref[half:, :half] = corner.astype(F32).T.astype(BF)
    factor_ref[half:, half:] = packed[2 * half : 3 * half]
    ends = packed[3 * half :].astype(F32)
    line = jnp.concatenate([ends[0:1] + ends[2:3], ends[1:2] + ends[3:4]], axis=1)
    if not column:
        return line
    size = 2 * half
    eye = lax.broadcasted_iota(jnp.int32, (size, size), 0) == lax.broadcasted_iota(
        jnp.int32, (size, size), 1
    )
    return jnp.sum(jnp.where(eye, line, 0.0), axis=1, keepdims=True)


def stepped(look_ref, w_ref, o_ref, factor, diagonal, by_columns):
    look = look_ref[...]
    step = dot(look, factor) if by_columns else dot(factor, look)
    o_ref[...] = w_ref[...].astype(F32) + (step + look.astype(F32) * diagonal)


def update_kernel(by_columns, me_ref, q_ref, l_ref, w_ref, o_ref, factor_ref, line_ref):
    @pl.when(pl.program_id(1) == 0)
    def _():
        line_ref[...] = unpack(q_ref[0], factor_ref, not by_columns)

    stepped(l_ref, w_ref, o_ref, factor_ref[...], line_ref[...], by_columns)


def update(factors, look, weight, by_columns, me):
    _, packed, half = factors.shape
    size = 2 * half
    height, width = weight.shape
    if by_columns:
        tile = min(1024, height)
        grid = (width // size, height // tile)
        spec = pl.BlockSpec((tile, size), lambda b, i, me_ref: (i, b))
    else:
        tile = min(1024, width)
        grid = (height // size, width // tile)
        spec = pl.BlockSpec((size, tile), lambda b, i, me_ref: (b, i))
    return pl.pallas_call(
        functools.partial(update_kernel, by_columns),
        grid_spec=pltpu.PrefetchScalarGridSpec(
            num_scalar_prefetch=1,
            grid=grid,
            in_specs=[
                pl.BlockSpec((1, packed, half), lambda b, i, me_ref: (b ^ me_ref[0], 0, 0)),
                spec,
                spec,
            ],
            out_specs=spec,
            scratch_shapes=[
                pltpu.VMEM((size, size), BF),
                pltpu.VMEM((1, size) if by_columns else (size, 1), F32),
            ],
        ),
        out_shape=jax.ShapeDtypeStruct(weight.shape, F32),
        compiler_params=params(),
        cost_estimate=cost(2 * size * height * width, 8 * height * width),
        name="update",
    )(me, factors, look, weight)


def attention_update_kernel(me_ref, *refs):
    qs, looks, weights, outs = refs[:4], refs[4:8], refs[8:12], refs[12:16]
    factor_ref, row_ref, column_ref = refs[16:]

    @pl.when(pl.program_id(0) == 0)
    def _():
        for k in range(3):
            row_ref[k] = unpack(qs[k][0], factor_ref.at[k], False)
        column_ref[...] = unpack(qs[3][0], factor_ref.at[3], True)

    for k in range(3):
        stepped(looks[k], weights[k], outs[k], factor_ref[k], row_ref[k], True)
    stepped(looks[3], weights[3], outs[3], factor_ref[3], column_ref[...], False)


def attention_update(factors, looks, weights, me, tile=256):
    _, packed, half = factors.shape
    size = 2 * half
    share, width = weights[0].shape
    tile = min(tile, share)
    tall = pl.BlockSpec((tile, width), lambda i, me_ref: (i, 0))
    wide = pl.BlockSpec((width, tile), lambda i, me_ref: (0, i))

    def factor(k):
        return pl.BlockSpec((1, packed, half), lambda i, me_ref: (me_ref[0] ^ k, 0, 0))

    specs = [tall, tall, tall, wide]
    return pl.pallas_call(
        attention_update_kernel,
        grid_spec=pltpu.PrefetchScalarGridSpec(
            num_scalar_prefetch=1,
            grid=(share // tile,),
            in_specs=[factor(k) for k in range(4)] + specs + specs,
            out_specs=specs,
            scratch_shapes=[
                pltpu.VMEM((4, size, size), BF),
                pltpu.VMEM((3, 1, size), F32),
                pltpu.VMEM((size, 1), F32),
            ],
        ),
        out_shape=[jax.ShapeDtypeStruct(w.shape, F32) for w in weights],
        compiler_params=params(),
        cost_estimate=cost(8 * size * share * width, 32 * share * width),
        name="attention_update",
    )(me, factors, factors, factors, factors, *looks, *weights)


def body(
    tokens,
    out_grad,
    segment_start,
    norm_attn,
    norm_mlp,
    w_query,
    w_key,
    w_value,
    w_out,
    w_gate,
    w_up,
    w_down,
    mom_query,
    mom_key,
    mom_value,
    mom_out,
    mom_gate,
    mom_up,
    mom_down,
):
    rows = tokens.shape[1]
    me = lax.axis_index("ctx")
    groups = lax.axis_size("fsdp")
    place = jnp.stack([me, me]).astype(jnp.int32)
    width = w_query.shape[1]
    depth = tokens.shape[2]
    low_in = tokens[0]
    inputs = low_in.astype(F32)
    gain_one, gain_two = norm_attn.astype(F32), norm_mlp.astype(F32)

    spread = f_scatter_cols(low_in)
    inv_one = lax.rsqrt(jnp.mean(inputs * inputs, axis=1, keepdims=True) + EPS)
    inv_spread = f_gather_rows(inv_one)
    scaled = (spread.astype(F32) * gain_one).astype(BF)
    one_spread = (spread.astype(F32) * inv_spread * gain_one).astype(BF)

    partial = [dot(scaled, w) for w in (w_query, w_key, w_value)]
    if pair():
        qkv = f_reduce_list(partial)
    else:
        qkv = jnp.concatenate([f_reduce_rows(part) for part in partial], axis=1)
    qkv = later(qkv * inv_one, inv_spread)
    dy_spread = f_scatter_cols(out_grad[0])
    one_two, dy_two = ctx_two(one_spread), ctx_two(dy_spread)

    starts = segment_start[0]
    chunks = [(me ^ j) * rows for j in range(lax.axis_size("ctx"))]
    key_start = jnp.concatenate([lax.dynamic_slice_in_dim(starts, o, rows) for o in chunks])
    key_index = jnp.concatenate([o + jnp.arange(rows, dtype=jnp.int32) for o in chunks])
    query_start, query_index = key_start[:rows], key_index[:rows]
    cosine, sine = rope_tables((query_index - query_start).astype(F32), width)
    marks = (query_index[:, None], query_start[:, None], key_index[None], key_start[None])

    query = rotate(qkv[:, :width], cosine, sine).astype(BF)
    kv_own = jnp.concatenate(
        [rotate(qkv[:, width : 2 * width], cosine, sine), qkv[:, 2 * width :]], axis=1
    ).astype(BF)
    kv = jnp.concatenate(ctx_parts(kv_own), axis=0)
    keys, values = kv[:, :width], kv[:, width:]
    query = later(query, dy_spread)
    attn = attention(query, keys, values, marks)
    attn_rows = f_gather_rows(attn)

    dhid = dot(dy_spread, w_down, 1, 1)
    attn_two = ctx_two(attn_rows)
    attn_rows = later(attn_rows, dhid)

    own_in = own_quarter(spread).astype(F32)
    own_inv = own_quarter(inv_spread)
    own_dy = own_quarter(dy_spread).astype(F32)

    middle = own_in + later(z_reduce(dot(attn_rows, w_out)), dy_two[1], attn_two[1])
    squares = f_all(jnp.sum(middle * middle, axis=1, keepdims=True))
    inv_two = lax.rsqrt(squares * (1.0 / depth) + EPS)
    own_two = (middle * inv_two * gain_two).astype(BF)
    if pair():
        dhid_got = swap(later(dhid.astype(BF), own_two), "fsdp", 1)
    else:
        dhid_got = dhid = lax.psum(dhid, "fsdp")
    two_spread = later(z_gather(own_two), dhid_got)
    two_two = ctx_two(two_spread)

    halves = 2
    count = w_gate.shape[1] // halves
    parts = [units(two_spread, w_gate, w_up, p, count) for p in range(halves)]
    if pair():
        got = [swap(sent, "fsdp", 1) for _, sent in parts]
        owns = [own for own, _ in parts]
    else:
        owns = [lax.psum(own, "fsdp") for own, _ in parts]
        got = owns
    owns[0] = later(owns[0], owns[1], two_two[1], one_two[1])
    trios, dx_two = [], None
    for p in range(halves):
        trio, dx_two = hidden_units(
            owns[p], got[p], dhid, dhid_got, w_gate, w_up, p, before=dx_two
        )
        trios.append(trio)

    trio_twos = [ctx_two(trio) for trio in trios]
    grad_two = z_reduce_slow(dx_two)
    trio_alls = [ctx_four(later(trio_twos[0], dx_two)), ctx_four(later(trio_twos[1], grad_two))]
    two_all, dy_all = ctx_four(later(two_two, dx_two)), ctx_four(later(dy_two, dx_two))
    scaled_two = middle * inv_two
    weighted = grad_two * gain_two
    mean = f_all(jnp.sum(weighted * scaled_two, axis=1, keepdims=True)) * (1.0 / depth)
    grad_middle = own_dy + inv_two * (weighted - scaled_two * mean)
    own_mid = later(grad_middle.astype(BF), trio_twos[0][1], trio_twos[1][1])
    span = (0, halves)
    gate_out = weight_grad(
        later(place, own_mid), two_all, trio_alls[0], mom_gate, width, True, (1024, 512), (None, 1),
        span=span,
    )
    mid_spread = z_gather_groups_slow(own_mid, gate_out)
    grad_attn = f_reduce_rows(dot(mid_spread, w_out, 1, 1)).astype(BF)

    dquery, dkeys, dvalues = attention_grad(query, keys, values, grad_attn, marks)
    dkv = jnp.concatenate([dkeys, dvalues], axis=1)
    up_out = weight_grad(
        later(place, dkv), two_all, trio_alls[0], mom_up, width, True, (1024, 512), (None, 2),
        span=span,
    )
    got_dkv = later(swap(dkv[2 * rows :], "ctx", 2), up_out)
    far = dkv[: 2 * rows].astype(F32) + got_dkv.astype(F32)
    near = far[:rows] + swap(far[rows:].astype(BF), "ctx", 1).astype(F32)
    dqkv = jnp.concatenate(
        [
            unrotate(dquery, cosine, sine),
            unrotate(near[:, :width], cosine, sine),
            near[:, width:],
        ],
        axis=1,
    ).astype(BF)
    dqkv_rows = f_gather_rows(dqkv)

    one_all = ctx_four(one_two)
    down_out = weight_grad(
        later(place, dqkv), trio_alls[0], dy_all, mom_down, width, False, (512, 1024), (0, None),
        span=span,
    )
    gate_out, up_out, down_out = mlp_weights(
        later(place, dqkv_rows), two_all, trio_alls[1], dy_all, (mom_gate, mom_up, mom_down),
        width, (1, halves), (gate_out, up_out, down_out),
    )
    g_gate, m_gate, l_gate, gram_gate = gate_out
    g_up, m_up, l_up, gram_up = up_out
    g_down, m_down, l_down, gram_down = down_out

    mid_all, attn_all = ctx_parts(mid_spread), ctx_four(attn_two)
    dqkv_all = ctx_parts(dqkv_rows)
    query_out, key_out, value_out, out_out, gram_attn = attention_weights(
        later(place, g_down), one_all, dqkv_all, attn_all, mid_all,
        (mom_query, mom_key, mom_value, mom_out),
    )
    g_query, m_query, l_query = query_out
    g_key, m_key, l_key = key_out
    g_value, m_value, l_value = value_out
    g_out, m_out, l_out = out_out

    trios, dqkv_rows = later((trios, dqkv_rows), down_out[3])
    out_part = sum(
        dot(trio[0], w_down[p * count : (p + 1) * count]) for p, trio in enumerate(trios)
    )
    result = f_gather_cols((middle + z_reduce(out_part)).astype(BF))
    result = z_gather_slow(result)

    dx_one = (
        dot(dqkv_rows[:, :width], w_query, 1, 1)
        + dot(dqkv_rows[:, width : 2 * width], w_key, 1, 1)
        + dot(dqkv_rows[:, 2 * width :], w_value, 1, 1)
    )
    grad_one = z_reduce(dx_one)
    scaled_one = own_in * own_inv
    weighted = grad_one * gain_one
    mean = f_all(jnp.sum(weighted * scaled_one, axis=1, keepdims=True)) * (1.0 / depth)
    input_grad = grad_middle + own_inv * (weighted - scaled_one * mean)
    input_grad = z_gather_slow(f_gather_cols(input_grad.astype(BF))).astype(F32)

    gain_parts = jnp.stack(
        [
            jnp.sum(dx_one * one_spread.astype(F32), axis=0),
            jnp.sum(dx_two * two_spread.astype(F32), axis=0),
        ]
    )
    gain_sums = all_sum(gain_parts, ("ctx", "tp"))
    grad_gain_one = gain_sums[0] / gain_one
    grad_gain_two = gain_sums[1] / gain_two

    if pair():
        even = lax.axis_index("fsdp") == 0
        kept = jnp.where(even, gram_down, gram_gate)
        sent = jnp.where(even, gram_gate, gram_down)
        both = later((kept, swap(sent, "fsdp", 1)), g_value, result, input_grad)
        q_own = polynomial(*both)
        got_attn = swap(gram_attn, "fsdp", 1)
        both = later((gram_up, swap(gram_up, "fsdp", 1)), q_own, gain_sums)
        q_up = polynomial(*both)
        q_other = swap(q_own, "fsdp", 1)
        q_down = ctx_two(jnp.where(even, q_own, q_other))
        q_gate = ctx_two(jnp.where(even, q_other, q_own))
        q_up = ctx_two(q_up)
        both = later((gram_attn, got_attn), q_up[0])
        q_attn = ctx_two(polynomial(*both))
    else:
        grams = lax.psum(jnp.stack([gram_down, gram_gate, gram_up, gram_attn]), "fsdp")
        none = jnp.zeros_like(gram_up)
        q_down, q_gate, q_up, q_attn = (ctx_two(polynomial(grams[k], none)) for k in range(4))
        got_attn = grams
    q_down, q_gate, q_up, q_attn = (
        jnp.stack(ctx_four(q)) for q in (q_down, q_gate, q_up, q_attn)
    )
    ctx_place = place[:1]
    new_down = update(q_down, l_down, w_down, False, ctx_place)
    new_gate = update(q_gate, l_gate, w_gate, True, ctx_place)
    new_up = update(q_up, l_up, w_up, True, ctx_place)

    new_query, new_key, new_value, new_out = attention_update(
        q_attn, (l_query, l_key, l_value, l_out), (w_query, w_key, w_value, w_out), ctx_place
    )

    return (
        result[None],
        input_grad[None],
        grad_gain_one,
        grad_gain_two,
        g_query,
        g_key,
        g_value,
        g_out,
        g_gate,
        g_up,
        g_down,
        m_query,
        m_key,
        m_value,
        m_out,
        m_gate,
        m_up,
        m_down,
        new_query,
        new_key,
        new_value,
        new_out,
        new_gate,
        new_up,
        new_down,
    )


def solution(mesh):
    act = P("fsdp", "ctx", None)
    col, row, vec = P("fsdp", "tp"), P("tp", "fsdp"), P("fsdp")
    seven = (col, col, col, row, col, col, row)
    in_specs = (act, act, P("fsdp", None), vec, vec) + seven + seven
    out_specs = (act, act, vec, vec) + seven + seven + seven
    return jax.shard_map(body, mesh=mesh, in_specs=in_specs, out_specs=out_specs, check_vma=False)
```

```python
import functools
import math

import jax
import jax.numpy as jnp
from jax import lax
from jax.experimental import pallas as pl
from jax.experimental.pallas import tpu as pltpu
from jax.sharding import PartitionSpec as P

HEAD_DIM = 64
NS_STEPS = 5
EPS = 1e-05
THETA = 130000.0
MOMENTUM = 0.95
COEF_A = 3.4445
COEF_B = -4.775
COEF_C = 2.0315
RATE = 0.5
BF = jnp.bfloat16
F32 = jnp.float32
VMEM_LIMIT = 56 * 1024 * 1024


def dot(left, right, ldim=1, rdim=0):
    return lax.dot_general(
        left, right, (((ldim,), (rdim,)), ((), ())), preferred_element_type=F32
    )


def params():
    return pltpu.CompilerParams(vmem_limit_bytes=VMEM_LIMIT)


def lasting(microseconds):
    return pl.CostEstimate(
        flops=0, bytes_accessed=int(microseconds * 3690000), transcendentals=0
    )


def swap(value, axis, bit):
    size = lax.axis_size(axis)
    return lax.ppermute(value, axis, [(i, i ^ bit) for i in range(size)])


def later(value, *others):
    return lax.optimization_barrier((value, others))[0]


def ctx_two(value):
    return [value, swap(value, "ctx", 2)]


def ctx_four(two):
    value, far = two
    return [value, swap(value, "ctx", 1), far, swap(far, "ctx", 1)]


def ctx_parts(value):
    return ctx_four(ctx_two(value))


def pair():
    return lax.axis_size("fsdp") == 2


def f_scatter_cols(value):
    size = lax.axis_size("fsdp")
    rows, width = value.shape
    part = width // size
    if size == 2:
        own = lax.axis_index("fsdp")
        mine = lax.dynamic_slice_in_dim(value, own * part, part, 1)
        other = lax.dynamic_slice_in_dim(value, (1 - own) * part, part, 1)
        return jnp.concatenate([mine, swap(other, "fsdp", 1)], axis=0)
    cut = jnp.swapaxes(value.reshape(rows, size, part), 0, 1)
    return lax.all_to_all(cut, "fsdp", 0, 0, tiled=True).reshape(size * rows, part)


def f_gather_cols(value):
    size = lax.axis_size("fsdp")
    rows = value.shape[0] // size
    if size == 2:
        own = lax.axis_index("fsdp")
        mine, other = value[:rows], swap(value[rows:], "fsdp", 1)
        return jnp.concatenate(
            [jnp.where(own == 0, mine, other), jnp.where(own == 0, other, mine)], axis=1
        )
    cut = lax.all_to_all(value.reshape(size, rows, -1), "fsdp", 0, 0, tiled=True)
    return jnp.swapaxes(cut, 0, 1).reshape(rows, -1)


def f_gather_rows(value):
    if pair():
        return jnp.concatenate([value, swap(value, "fsdp", 1)], axis=0)
    return lax.all_gather(value, "fsdp", axis=0, tiled=True)


def f_reduce_rows(value):
    size = lax.axis_size("fsdp")
    rows = value.shape[0] // size
    if size == 2:
        return value[:rows].astype(F32) + swap(value[rows:].astype(BF), "fsdp", 1).astype(F32)
    return lax.psum_scatter(value.astype(F32), "fsdp", scatter_dimension=0, tiled=True)


def flip(value):
    half = value.shape[0] // 2
    return jnp.concatenate([value[half:], value[:half]], axis=0)


def f_all(value):
    if pair():
        return value + flip(swap(value, "fsdp", 1))
    return lax.psum(value, "fsdp")


def f_reduce_list(parts):
    rows = parts[0].shape[0] // 2
    sent = jnp.concatenate([p[rows:].astype(BF) for p in parts], axis=1)
    return jnp.concatenate([p[:rows] for p in parts], axis=1) + swap(sent, "fsdp", 1).astype(F32)


def z_shift(value, k):
    size = lax.axis_size("tp")
    return lax.ppermute(value, "tp", [(i, (i + k) % size) for i in range(size)])


def z_shifts():
    size = lax.axis_size("tp")
    return sorted(range(1, size), key=lambda k: -min(k, size - k))


def by_quarter(value):
    size, groups = lax.axis_size("tp"), lax.axis_size("fsdp")
    rows, width = value.shape
    part = rows // (size * groups)
    cut = jnp.swapaxes(value.reshape(groups, size, part, width), 0, 1)
    return cut.reshape(size, groups * part, width)


def own_quarter(value):
    return lax.dynamic_index_in_dim(by_quarter(value), lax.axis_index("tp"), 0, keepdims=False)


def z_reduce(value):
    sent = by_quarter(value.astype(BF))
    return jnp.sum(lax.all_to_all(sent, "tp", 0, 0, tiled=True).astype(F32), axis=0)


def z_gather(value):
    size, groups = lax.axis_size("tp"), lax.axis_size("fsdp")
    rows, width = value.shape
    full = lax.all_gather(value, "tp", axis=0)
    full = jnp.swapaxes(full.reshape(size, groups, rows // groups, width), 0, 1)
    return full.reshape(size * rows, width)


def z_reduce_slow(value):
    size, me = lax.axis_size("tp"), lax.axis_index("tp")
    cut = by_quarter(value)
    total = lax.dynamic_index_in_dim(cut, me, 0, keepdims=False).astype(F32)
    for k in z_shifts():
        sent = lax.dynamic_index_in_dim(cut, (me + k) % size, 0, keepdims=False).astype(BF)
        total = total + z_shift(sent, k).astype(F32)
    return total


def z_gather_groups_slow(value, wait=()):
    size, groups = lax.axis_size("tp"), lax.axis_size("fsdp")
    rows, width = value.shape
    full = z_gather_slow(value, wait).reshape(size, groups, rows // groups, width)
    return jnp.swapaxes(full, 0, 1).reshape(size * rows, width)


def z_gather_slow(value, wait=()):
    size, me = lax.axis_size("tp"), lax.axis_index("tp")
    by_place = {k: later(z_shift(value, k), wait) for k in z_shifts()}
    by_place[0] = value
    ordered = []
    for at in range(size):
        chosen = value
        for k in z_shifts():
            chosen = jnp.where((me - k) % size == at, by_place[k], chosen)
        ordered.append(chosen)
    return jnp.concatenate(ordered, axis=0)


def all_sum(value, axes):
    for axis in axes:
        size = lax.axis_size(axis)
        if axis == "tp":
            value = value + sum(z_shift(value, k) for k in z_shifts())
        else:
            bit = 1
            while bit < size:
                value = value + swap(value, axis, bit)
                bit *= 2
    return value


def rope_tables(position, width):
    half = HEAD_DIM // 2
    freq = THETA ** (-(jnp.arange(half, dtype=F32) * 2.0 / HEAD_DIM))
    angle = position[:, None] * freq[None, :]
    repeat = width // half
    return jnp.tile(jnp.cos(angle), (1, repeat)), jnp.tile(jnp.sin(angle), (1, repeat))


def first_half(shape):
    lane = lax.broadcasted_iota(jnp.int32, shape, 1)
    return (lane & (HEAD_DIM - 1)) < HEAD_DIM // 2


def rotate(values, cosine, sine):
    half = HEAD_DIM // 2
    turned = jnp.where(
        first_half(values.shape), -jnp.roll(values, -half, 1), jnp.roll(values, half, 1)
    )
    return values * cosine + turned * sine


def unrotate(grads, cosine, sine):
    half = HEAD_DIM // 2
    scaled = grads * sine
    back = jnp.where(
        first_half(grads.shape), jnp.roll(scaled, -half, 1), -jnp.roll(scaled, half, 1)
    )
    return grads * cosine + back


def head_probs(query, keys, allowed, scale):
    scores = jnp.where(allowed, dot(query, keys, 1, 1) * scale, -1e30)
    top = jnp.max(scores, axis=1, keepdims=True)
    expo = jnp.exp(scores - top)
    return expo / jnp.sum(expo, axis=1, keepdims=True)


def attention_kernel(scale, q_ref, k_ref, v_ref, qi_ref, qs_ref, ki_ref, ks_ref, o_ref):
    allowed = (ks_ref[...] == qs_ref[...]) & (ki_ref[...] <= qi_ref[...])
    query, keys, values = q_ref[...], k_ref[...], v_ref[...]
    lane = lax.broadcasted_iota(jnp.int32, query.shape, 1)
    outs = []
    for head in range(2):
        mine = (lane >= HEAD_DIM) == (head == 1)
        prob = head_probs(jnp.where(mine, query, 0), keys, allowed, scale)
        outs.append(dot(prob.astype(BF), values))
    o_ref[...] = jnp.where(lane < HEAD_DIM, outs[0], outs[1]).astype(BF)


def attention_grad_kernel(
    scale, q_ref, k_ref, v_ref, g_ref, qi_ref, qs_ref, ki_ref, ks_ref, dq_ref, dk_ref, dv_ref
):
    allowed = (ks_ref[...] == qs_ref[...]) & (ki_ref[...] <= qi_ref[...])
    query, keys, values, grads = q_ref[...], k_ref[...], v_ref[...], g_ref[...]
    lane = lax.broadcasted_iota(jnp.int32, query.shape, 1)
    wide = lax.broadcasted_iota(jnp.int32, keys.shape, 1)
    dqs, dks, dvs = [], [], []
    for head in range(2):
        mine = (lane >= HEAD_DIM) == (head == 1)
        prob = head_probs(jnp.where(mine, query, 0), keys, allowed, scale)
        dprob = dot(jnp.where(mine, grads, 0), values, 1, 1)
        delta = jnp.sum(prob * dprob, axis=1, keepdims=True)
        dscore = (prob * (dprob - delta)).astype(BF)
        dqs.append(dot(dscore, keys))
        dks.append(dot(dscore, query, 0, 0))
        dvs.append(dot(prob.astype(BF), grads, 0, 0))
    low, wlow = lane < HEAD_DIM, wide < HEAD_DIM
    dq_ref[...] = jnp.where(low, dqs[0], dqs[1]) * scale
    dk_ref[...] = (jnp.where(wlow, dks[0], dks[1]) * scale).astype(BF)
    dv_ref[...] = jnp.where(wlow, dvs[0], dvs[1]).astype(BF)


def attention_specs(rows, keys):
    def col(n):
        return pl.BlockSpec((n, 2 * HEAD_DIM), lambda h: (0, h))

    def whole(shape):
        return pl.BlockSpec(shape, lambda h: (0, 0))

    marks = [whole((rows, 1)), whole((rows, 1)), whole((1, keys)), whole((1, keys))]
    return col, marks


def attention(query, keys, values, marks):
    rows, width = query.shape
    count = keys.shape[0]
    col, mark_specs = attention_specs(rows, count)
    return pl.pallas_call(
        functools.partial(attention_kernel, 1.0 / math.sqrt(HEAD_DIM)),
        grid=(width // (2 * HEAD_DIM),),
        in_specs=[col(rows), col(count), col(count)] + mark_specs,
        out_specs=col(rows),
        out_shape=jax.ShapeDtypeStruct((rows, width), BF),
        compiler_params=params(),
        cost_estimate=lasting(5.5),
        name="attention",
    )(query, keys, values, *marks)


def attention_grad(query, keys, values, grads, marks):
    rows, width = query.shape
    count = keys.shape[0]
    col, mark_specs = attention_specs(rows, count)
    return pl.pallas_call(
        functools.partial(attention_grad_kernel, 1.0 / math.sqrt(HEAD_DIM)),
        grid=(width // (2 * HEAD_DIM),),
        in_specs=[col(rows), col(count), col(count), col(rows)] + mark_specs,
        out_specs=[col(rows), col(count), col(count)],
        out_shape=[
            jax.ShapeDtypeStruct((rows, width), F32),
            jax.ShapeDtypeStruct((count, width), BF),
            jax.ShapeDtypeStruct((count, width), BF),
        ],
        compiler_params=params(),
        cost_estimate=lasting(7),
        name="attention_grad",
    )(query, keys, values, grads, *marks)


def smem():
    return pl.BlockSpec(memory_space=pltpu.SMEM)


def units_kernel(x_ref, wg_ref, wu_ref, own_ref, sent_ref):
    for k, w_ref in enumerate((wg_ref, wu_ref)):
        part = dot(x_ref[...], w_ref[...])
        own_ref[k] = part
        sent_ref[k] = part.astype(BF)


def units(x, wgate, wup, at, count, tile=512):
    rows, depth = x.shape
    steps = count // tile
    weight = pl.BlockSpec((depth, tile), lambda n: (0, at * steps + n))
    out = pl.BlockSpec((2, rows, tile), lambda n: (0, 0, n))
    return pl.pallas_call(
        units_kernel,
        grid=(steps,),
        in_specs=[pl.BlockSpec((rows, depth), lambda n: (0, 0)), weight, weight],
        out_specs=[out, out],
        out_shape=[
            jax.ShapeDtypeStruct((2, rows, count), F32),
            jax.ShapeDtypeStruct((2, rows, count), BF),
        ],
        compiler_params=params(),
        cost_estimate=lasting(4.5),
        name="units",
    )(x, wgate, wup)


def hidden_kernel(paired, first, own_ref, got_ref, dh_ref, dgot_ref, wg_ref, wu_ref, *refs):
    if first:
        out_ref, acc_ref = refs
    else:
        before_ref, out_ref, acc_ref = refs
    half = dh_ref.shape[0] // 2

    def total(own, got):
        if not paired:
            return own
        got = got.astype(F32)
        return own + jnp.concatenate([got[half:], got[:half]], axis=0)

    gate = total(own_ref[0], got_ref[0])
    upper = total(own_ref[1], got_ref[1])
    dhid = total(dh_ref[...], dgot_ref[...])
    sigma = jax.nn.sigmoid(gate)
    silu = gate * sigma
    dgate = (dhid * upper * sigma * (1.0 + gate * (1.0 - sigma))).astype(BF)
    dup = (dhid * silu).astype(BF)
    out_ref[0] = (silu * upper).astype(BF)
    out_ref[1] = dgate
    out_ref[2] = dup
    grad = dot(dgate, wg_ref[...], 1, 1) + dot(dup, wu_ref[...], 1, 1)

    @pl.when(pl.program_id(0) == 0)
    def _():
        acc_ref[...] = grad if first else grad + before_ref[...]

    @pl.when(pl.program_id(0) > 0)
    def _():
        acc_ref[...] += grad


def hidden_units(own, got, dhid, dgot, wgate, wup, at, before=None, tile=512):
    _, rows, count = own.shape
    depth = wgate.shape[0]
    steps = count // tile
    weight = pl.BlockSpec((depth, tile), lambda n: (0, at * steps + n))
    trio = pl.BlockSpec((2, rows, tile), lambda n: (0, 0, n))
    lanes = pl.BlockSpec((rows, tile), lambda n: (0, at * steps + n))
    total = pl.BlockSpec((rows, depth), lambda n: (0, 0))
    args = [own, got, dhid, dgot, wgate, wup] + ([] if before is None else [before])
    return pl.pallas_call(
        functools.partial(hidden_kernel, pair(), before is None),
        grid=(steps,),
        in_specs=[trio, trio, lanes, lanes, weight, weight] + [total] * (len(args) - 6),
        out_specs=[pl.BlockSpec((3, rows, tile), lambda n: (0, 0, n)), total],
        out_shape=[
            jax.ShapeDtypeStruct((3, rows, count), BF),
            jax.ShapeDtypeStruct((rows, depth), F32),
        ],
        compiler_params=params(),
        cost_estimate=lasting(6),
        name="hidden_units",
    )(*args)


def joined(parts):
    return jnp.concatenate([r[...].reshape(r.shape[-2:]) for r in parts], axis=0)


def moved(total, mom_ref, g_ref, m_ref, l_ref):
    mom = MOMENTUM * mom_ref[...] + total
    g_ref[...] = total
    m_ref[...] = mom
    l_ref[...] = (total + MOMENTUM * mom).astype(BF)


def add_gram(gram_ref, look_ref, by_columns, hit, first):
    half = gram_ref.shape[1]

    def three():
        if by_columns:
            low, high = look_ref[:, :half], look_ref[:, half:]
        else:
            low, high = look_ref[:half, :], look_ref[half:, :]
        dim = 0 if by_columns else 1
        return [dot(x, y, dim, dim) for x, y in ((low, low), (low, high), (high, high))]

    @pl.when(jnp.logical_and(hit, first))
    def _():
        for k, value in enumerate(three()):
            gram_ref[k] = value

    @pl.when(jnp.logical_and(hit, jnp.logical_not(first)))
    def _():
        for k, value in enumerate(three()):
            gram_ref[k] += value


def gram_spec(size):
    half = size // 2
    return (
        pl.BlockSpec((3, half, half), lambda *at: (0, 0, 0)),
        jax.ShapeDtypeStruct((3, half, half), F32),
    )


def weight_grad_kernel(nl, nr, by_columns, base, filled, place_ref, *refs):
    lefts, rights = refs[:nl], refs[nl : nl + nr]
    mom_ref, g_ref, m_ref, l_ref, gram_ref = refs[nl + nr], *refs[-4:]
    tall, wide = g_ref.shape
    moved(dot(joined(lefts), joined(rights), 0, 0), mom_ref, g_ref, m_ref, l_ref)
    i, j = pl.program_id(0), pl.program_id(1)
    outer, inner = (j, i) if by_columns else (i, j)
    size = 2 * gram_ref.shape[1]
    count = (wide if by_columns else tall) // size

    if filled:

        @pl.when(jnp.logical_and(i == 0, j == 0))
        def _():
            gram_ref[...] = refs[nl + nr + 4][...]

    for k in range(count):
        at = pl.ds(k * size, size)
        look = l_ref.at[:, at] if by_columns else l_ref.at[at, :]
        add_gram(gram_ref, look, by_columns, base + outer * count + k == place_ref[0], inner == 0)


def weight_grad(
    place, lefts, rights, mom, size, by_columns, tile, planes=(None, None), span=None, into=None
):
    height, width = mom.shape
    part, parts = span or (0, 1)
    tm, tn = min(tile[0], height), min(tile[1], width)
    grid = [height // tm, width // tn]
    axis = 1 if by_columns else 0
    grid[axis] //= parts
    start = [0, 0]
    start[axis] = part * grid[axis]
    out = pl.BlockSpec((tm, tn), lambda i, j: (start[0] + i, start[1] + j))
    tok = sum(v.shape[-2] for v in lefts)

    def specs(values, plane, lanes, place_of):
        if plane is None:
            return [pl.BlockSpec((v.shape[0], lanes), lambda i, j: (0, place_of(i, j))) for v in values]
        return [
            pl.BlockSpec((1, v.shape[1], lanes), lambda i, j: (plane, 0, place_of(i, j)))
            for v in values
        ]

    whole_gram, gram_shape = gram_spec(size)
    in_specs = [smem()]
    in_specs += specs(lefts, planes[0], tm, lambda i, j: i)
    in_specs += specs(rights, planes[1], tn, lambda i, j: j)
    in_specs += [out]
    args = [place, *lefts, *rights, mom]
    aliases = {}
    if into is not None:
        aliases = {len(args) + k: k for k in range(3)}
        in_specs += [pl.BlockSpec(memory_space=pl.ANY)] * 3 + [whole_gram]
        args += list(into)
    blocks = (width if by_columns else height) // size // parts
    return pl.pallas_call(
        functools.partial(
            weight_grad_kernel, len(lefts), len(rights), by_columns, part * blocks, into is not None
        ),
        grid=tuple(grid),
        in_specs=in_specs,
        out_specs=[out, out, out, whole_gram],
        out_shape=[
            jax.ShapeDtypeStruct((height, width), F32),
            jax.ShapeDtypeStruct((height, width), F32),
            jax.ShapeDtypeStruct((height, width), BF),
            gram_shape,
        ],
        input_output_aliases=aliases,
        compiler_params=params(),
        cost_estimate=lasting(9),
        name="weight_grad",
    )(*args)


def attention_weights_kernel(count, place_ref, *refs):
    ones, grads, attns, mids = (refs[k * count : (k + 1) * count] for k in range(4))
    refs = refs[4 * count :]
    moms, outs, gram_ref = refs[:4], refs[4:16], refs[16]
    first = pl.program_id(0) == 0
    left = joined(ones)
    width = moms[0].shape[1]
    for k in range(3):
        right = jnp.concatenate([r[:, k * width : (k + 1) * width] for r in grads], axis=0)
        moved(dot(left, right, 0, 0), moms[k], *outs[3 * k : 3 * k + 3])
        add_gram(gram_ref, outs[3 * k + 2], True, place_ref[0] == k, first)
    moved(dot(joined(attns), joined(mids), 0, 0), moms[3], *outs[9:12])
    add_gram(gram_ref, outs[11], False, place_ref[0] == 3, first)


def attention_weights(place, ones, grads, attns, mids, moms, tile=256):
    share, width = moms[0].shape
    tile = min(tile, share)

    def cols(v):
        return pl.BlockSpec((v.shape[0], tile), lambda i: (0, i))

    def whole(v):
        return pl.BlockSpec(v.shape, lambda i: (0, 0))

    tall = pl.BlockSpec((tile, width), lambda i: (i, 0))
    wide = pl.BlockSpec((width, tile), lambda i: (0, i))
    gram, gram_shape = gram_spec(width)
    shapes = []
    for mom in moms:
        shapes += [jax.ShapeDtypeStruct(mom.shape, kind) for kind in (F32, F32, BF)]
    out = pl.pallas_call(
        functools.partial(attention_weights_kernel, len(ones)),
        grid=(share // tile,),
        in_specs=[smem()]
        + [cols(v) for v in ones]
        + [whole(v) for v in grads]
        + [whole(v) for v in attns]
        + [cols(v) for v in mids]
        + [tall, tall, tall, wide],
        out_specs=[tall] * 9 + [wide] * 3 + [gram],
        out_shape=shapes + [gram_shape],
        compiler_params=params(),
        cost_estimate=lasting(18),
        name="attention_weights",
    )(place, *ones, *grads, *attns, *mids, *moms)
    return out[:3], out[3:6], out[6:9], out[9:12], out[12]


def mlp_weights_kernel(count, base, filled, place_ref, *refs):
    twos, hids, dgates, dups, dys = (refs[k * count : (k + 1) * count] for k in range(5))
    refs = refs[5 * count :]
    moms, refs = refs[:3], refs[3:]
    before, refs = (refs[9:12], refs[12:]) if filled else (None, refs)
    outs, grams = refs[:9], refs[9:]
    j, i = pl.program_id(0), pl.program_id(1)

    if filled:

        @pl.when(jnp.logical_and(i == 0, j == 0))
        def _():
            for gram_ref, old in zip(grams, before):
                gram_ref[...] = old[...]

    two = joined(twos)
    hit, first = base + j == place_ref[0], i == 0
    moved(dot(two, joined(dgates), 0, 0), moms[0], *outs[:3])
    add_gram(grams[0], outs[2], True, hit, first)
    moved(dot(two, joined(dups), 0, 0), moms[1], *outs[3:6])
    add_gram(grams[1], outs[5], True, hit, first)
    moved(dot(joined(hids), joined(dys), 0, 0), moms[2], *outs[6:9])
    add_gram(grams[2], outs[8], False, hit, first)


def mlp_weights(place, twos, trios, dys, moms, size, span, into, tile=512):
    share, width = moms[0].shape
    part, parts = span
    blocks = width // size // parts
    tile = min(tile, share)

    def cols(v):
        return pl.BlockSpec((v.shape[0], tile), lambda j, i: (0, i))

    def plane(v, k):
        return pl.BlockSpec((1, v.shape[1], size), lambda j, i: (k, 0, j))

    tall = pl.BlockSpec((tile, size), lambda j, i: (i, part * blocks + j))
    wide = pl.BlockSpec((size, tile), lambda j, i: (part * blocks + j, i))
    gram, gram_shape = gram_spec(size)
    shapes = []
    for mom in moms:
        shapes += [jax.ShapeDtypeStruct(mom.shape, kind) for kind in (F32, F32, BF)]
    in_specs = [smem()] + [cols(v) for v in twos]
    for k in range(3):
        in_specs += [plane(v, k) for v in trios]
    in_specs += [cols(v) for v in dys] + [tall, tall, wide]
    args = [place, *twos, *trios, *trios, *trios, *dys, *moms]
    aliases = {len(args) + k: k for k in range(9)}
    in_specs += [pl.BlockSpec(memory_space=pl.ANY)] * 9 + [gram] * 3
    args += [v for out in into for v in out[:3]] + [out[3] for out in into]
    out = pl.pallas_call(
        functools.partial(mlp_weights_kernel, len(twos), part * blocks, True),
        grid=(blocks, share // tile),
        in_specs=in_specs,
        out_specs=[tall] * 6 + [wide] * 3 + [gram] * 3,
        out_shape=shapes + [gram_shape] * 3,
        input_output_aliases=aliases,
        compiler_params=params(),
        cost_estimate=lasting(24),
        name="mlp_weights",
    )(*args)
    return [(*out[3 * k : 3 * k + 3], out[9 + k]) for k in range(3)]


def polynomial_kernel(a_ref, b_ref, out_ref, full_ref):
    size, half = full_ref.shape[0], full_ref.shape[0] // 2
    corner = a_ref[1] + b_ref[1]
    full_ref[:half, :half] = a_ref[0] + b_ref[0]
    full_ref[:half, half:] = corner
    full_ref[half:, :half] = corner.T
    full_ref[half:, half:] = a_ref[2] + b_ref[2]
    row = lax.broadcasted_iota(jnp.int32, (size, size), 0)
    column = lax.broadcasted_iota(jnp.int32, (size, size), 1)
    eye = row == column

    def split(full):
        only = jnp.where(eye, full, 0.0)
        return (
            jnp.where(eye, 0.0, full),
            jnp.sum(only, axis=1, keepdims=True),
            jnp.sum(only, axis=0, keepdims=True),
        )

    def times(left, right):
        loff, lcol, lrow = left
        roff, rcol, rrow = right
        full = dot(loff.astype(BF), roff.astype(BF)) + lcol * roff + loff * rrow
        off, dcol, drow = split(full)
        return off, dcol + lcol * rcol, drow + lrow * rrow

    def mix(coefs, first, second, shift):
        off = coefs[0] * first[0] + coefs[1] * second[0]
        dcol = coefs[0] * first[1] + coefs[1] * second[1] + shift
        drow = coefs[0] * first[2] + coefs[1] * second[2] + shift
        return off, dcol, drow

    gram = split(full_ref[...])
    norm = jnp.sqrt(jnp.sum(gram[2])) + 1e-07
    inverse = 1.0 / (norm * norm)
    gram = tuple(part * inverse for part in gram)
    total = None
    for step in range(NS_STEPS):
        square = times(gram, gram)
        factor = mix((COEF_B, COEF_C), gram, square, COEF_A)
        total = factor if total is None else times(factor, total)
        if step < NS_STEPS - 1:
            gram = times(factor, times(factor, gram))
    weight = -RATE / norm
    off = (total[0] * weight).astype(BF)
    out_ref[:half] = off[:half, :half]
    out_ref[half:size] = off[:half, half:]
    out_ref[size : size + half] = off[half:, half:]
    diagonal = total[2] * weight
    high = diagonal.astype(BF).astype(F32)
    low = diagonal - high
    line = lax.broadcasted_iota(jnp.int32, (16, half), 0)
    tail = jnp.zeros((16, half), F32)
    for k, part in enumerate((high[:, :half], high[:, half:], low[:, :half], low[:, half:])):
        tail = jnp.where(line == k, part, tail)
    out_ref[size + half :] = tail.astype(BF)


def polynomial(a, b):
    half = a.shape[1]
    size = 2 * half
    return pl.pallas_call(
        polynomial_kernel,
        in_specs=[pl.BlockSpec(memory_space=pltpu.VMEM)] * 2,
        out_specs=pl.BlockSpec(memory_space=pltpu.VMEM),
        out_shape=jax.ShapeDtypeStruct((3 * half + 16, half), BF),
        scratch_shapes=[pltpu.VMEM((size, size), F32)],
        compiler_params=params(),
        cost_estimate=lasting(10),
        name="polynomial",
    )(a, b)


def unpack(packed, factor_ref, column):
    half = packed.shape[1]
    corner = packed[half : 2 * half]
    factor_ref[:half, :half] = packed[:half]
    factor_ref[:half, half:] = corner
    factor_ref[half:, :half] = corner.astype(F32).T.astype(BF)
    factor_ref[half:, half:] = packed[2 * half : 3 * half]
    ends = packed[3 * half :].astype(F32)
    line = jnp.concatenate([ends[0:1] + ends[2:3], ends[1:2] + ends[3:4]], axis=1)
    if not column:
        return line
    size = 2 * half
    eye = lax.broadcasted_iota(jnp.int32, (size, size), 0) == lax.broadcasted_iota(
        jnp.int32, (size, size), 1
    )
    return jnp.sum(jnp.where(eye, line, 0.0), axis=1, keepdims=True)


def stepped(look_ref, w_ref, o_ref, factor, diagonal, by_columns):
    look = look_ref[...]
    step = dot(look, factor) if by_columns else dot(factor, look)
    o_ref[...] = w_ref[...].astype(F32) + (step + look.astype(F32) * diagonal)


def update_kernel(by_columns, me_ref, q_ref, l_ref, w_ref, o_ref, factor_ref, line_ref):
    @pl.when(pl.program_id(1) == 0)
    def _():
        line_ref[...] = unpack(q_ref[0], factor_ref, not by_columns)

    stepped(l_ref, w_ref, o_ref, factor_ref[...], line_ref[...], by_columns)


def update(factors, look, weight, by_columns, me):
    _, packed, half = factors.shape
    size = 2 * half
    height, width = weight.shape
    if by_columns:
        tile = min(1024, height)
        grid = (width // size, height // tile)
        spec = pl.BlockSpec((tile, size), lambda b, i, me_ref: (i, b))
    else:
        tile = min(1024, width)
        grid = (height // size, width // tile)
        spec = pl.BlockSpec((size, tile), lambda b, i, me_ref: (b, i))
    return pl.pallas_call(
        functools.partial(update_kernel, by_columns),
        grid_spec=pltpu.PrefetchScalarGridSpec(
            num_scalar_prefetch=1,
            grid=grid,
            in_specs=[
                pl.BlockSpec((1, packed, half), lambda b, i, me_ref: (b ^ me_ref[0], 0, 0)),
                spec,
                spec,
            ],
            out_specs=spec,
            scratch_shapes=[
                pltpu.VMEM((size, size), BF),
                pltpu.VMEM((1, size) if by_columns else (size, 1), F32),
            ],
        ),
        out_shape=jax.ShapeDtypeStruct(weight.shape, F32),
        compiler_params=params(),
        cost_estimate=lasting(9),
        name="update",
    )(me, factors, look, weight)


def attention_update_kernel(me_ref, *refs):
    qs, looks, weights, outs = refs[:4], refs[4:8], refs[8:12], refs[12:16]
    factor_ref, row_ref, column_ref = refs[16:]

    @pl.when(pl.program_id(0) == 0)
    def _():
        for k in range(3):
            row_ref[k] = unpack(qs[k][0], factor_ref.at[k], False)
        column_ref[...] = unpack(qs[3][0], factor_ref.at[3], True)

    for k in range(3):
        stepped(looks[k], weights[k], outs[k], factor_ref[k], row_ref[k], True)
    stepped(looks[3], weights[3], outs[3], factor_ref[3], column_ref[...], False)


def attention_update(factors, looks, weights, me, tile=256):
    _, packed, half = factors.shape
    size = 2 * half
    share, width = weights[0].shape
    tile = min(tile, share)
    tall = pl.BlockSpec((tile, width), lambda i, me_ref: (i, 0))
    wide = pl.BlockSpec((width, tile), lambda i, me_ref: (0, i))

    def factor(k):
        return pl.BlockSpec((1, packed, half), lambda i, me_ref: (me_ref[0] ^ k, 0, 0))

    specs = [tall, tall, tall, wide]
    return pl.pallas_call(
        attention_update_kernel,
        grid_spec=pltpu.PrefetchScalarGridSpec(
            num_scalar_prefetch=1,
            grid=(share // tile,),
            in_specs=[factor(k) for k in range(4)] + specs + specs,
            out_specs=specs,
            scratch_shapes=[
                pltpu.VMEM((4, size, size), BF),
                pltpu.VMEM((3, 1, size), F32),
                pltpu.VMEM((size, 1), F32),
            ],
        ),
        out_shape=[jax.ShapeDtypeStruct(w.shape, F32) for w in weights],
        compiler_params=params(),
        cost_estimate=lasting(9),
        name="attention_update",
    )(me, factors, factors, factors, factors, *looks, *weights)


def body(
    tokens,
    out_grad,
    segment_start,
    norm_attn,
    norm_mlp,
    w_query,
    w_key,
    w_value,
    w_out,
    w_gate,
    w_up,
    w_down,
    mom_query,
    mom_key,
    mom_value,
    mom_out,
    mom_gate,
    mom_up,
    mom_down,
):
    rows = tokens.shape[1]
    me = lax.axis_index("ctx")
    groups = lax.axis_size("fsdp")
    place = jnp.stack([me, me]).astype(jnp.int32)
    width = w_query.shape[1]
    depth = tokens.shape[2]
    low_in = tokens[0]
    inputs = low_in.astype(F32)
    gain_one, gain_two = norm_attn.astype(F32), norm_mlp.astype(F32)

    spread = f_scatter_cols(low_in)
    inv_one = lax.rsqrt(jnp.mean(inputs * inputs, axis=1, keepdims=True) + EPS)
    inv_spread = f_gather_rows(inv_one)
    scaled = (spread.astype(F32) * gain_one).astype(BF)
    one_spread = (spread.astype(F32) * inv_spread * gain_one).astype(BF)

    partial = [dot(scaled, w) for w in (w_query, w_key, w_value)]
    if pair():
        qkv = f_reduce_list(partial)
    else:
        qkv = jnp.concatenate([f_reduce_rows(part) for part in partial], axis=1)
    qkv = later(qkv * inv_one, inv_spread)
    dy_spread = f_scatter_cols(out_grad[0])
    one_two, dy_two = ctx_two(one_spread), ctx_two(dy_spread)

    starts = segment_start[0]
    chunks = [(me ^ j) * rows for j in range(lax.axis_size("ctx"))]
    key_start = jnp.concatenate([lax.dynamic_slice_in_dim(starts, o, rows) for o in chunks])
    key_index = jnp.concatenate([o + jnp.arange(rows, dtype=jnp.int32) for o in chunks])
    query_start, query_index = key_start[:rows], key_index[:rows]
    cosine, sine = rope_tables((query_index - query_start).astype(F32), width)
    marks = (query_index[:, None], query_start[:, None], key_index[None], key_start[None])

    query = rotate(qkv[:, :width], cosine, sine).astype(BF)
    kv_own = jnp.concatenate(
        [rotate(qkv[:, width : 2 * width], cosine, sine), qkv[:, 2 * width :]], axis=1
    ).astype(BF)
    kv = jnp.concatenate(ctx_parts(kv_own), axis=0)
    keys, values = kv[:, :width], kv[:, width:]
    query = later(query, dy_spread)
    attn = attention(query, keys, values, marks)
    attn_rows = f_gather_rows(attn)

    dhid = dot(dy_spread, w_down, 1, 1)
    attn_two = ctx_two(attn_rows)
    attn_rows = later(attn_rows, dhid)

    own_in = own_quarter(spread).astype(F32)
    own_inv = own_quarter(inv_spread)
    own_dy = own_quarter(dy_spread).astype(F32)

    middle = own_in + later(z_reduce(dot(attn_rows, w_out)), dy_two[1], attn_two[1])
    squares = f_all(jnp.sum(middle * middle, axis=1, keepdims=True))
    inv_two = lax.rsqrt(squares * (1.0 / depth) + EPS)
    own_two = (middle * inv_two * gain_two).astype(BF)
    if pair():
        dhid_got = swap(later(dhid.astype(BF), own_two), "fsdp", 1)
    else:
        dhid_got = dhid = lax.psum(dhid, "fsdp")
    two_spread = later(z_gather(own_two), dhid_got)
    two_two = ctx_two(two_spread)

    halves = 2
    count = w_gate.shape[1] // halves
    parts = [units(two_spread, w_gate, w_up, p, count) for p in range(halves)]
    if pair():
        got = [swap(sent, "fsdp", 1) for _, sent in parts]
        owns = [own for own, _ in parts]
    else:
        owns = [lax.psum(own, "fsdp") for own, _ in parts]
        got = owns
    owns[0] = later(owns[0], owns[1], two_two[1], one_two[1])
    trios, dx_two = [], None
    for p in range(halves):
        trio, dx_two = hidden_units(
            owns[p], got[p], dhid, dhid_got, w_gate, w_up, p, before=dx_two
        )
        trios.append(trio)

    trio_twos = [ctx_two(trio) for trio in trios]
    grad_two = z_reduce_slow(dx_two)
    trio_alls = [ctx_four(later(two, grad_two)) for two in trio_twos]
    two_all, dy_all = ctx_four(later(two_two, grad_two)), ctx_four(later(dy_two, grad_two))
    scaled_two = middle * inv_two
    weighted = grad_two * gain_two
    mean = f_all(jnp.sum(weighted * scaled_two, axis=1, keepdims=True)) * (1.0 / depth)
    grad_middle = own_dy + inv_two * (weighted - scaled_two * mean)
    own_mid = later(grad_middle.astype(BF), trio_twos[0][1], trio_twos[1][1])
    span = (0, halves)
    gate_out = weight_grad(
        later(place, own_mid), two_all, trio_alls[0], mom_gate, width, True, (1024, 512), (None, 1),
        span=span,
    )
    mid_spread = z_gather_groups_slow(own_mid, gate_out)
    out_part = sum(
        dot(trio[0], w_down[p * count : (p + 1) * count]) for p, trio in enumerate(trios)
    ).astype(BF)
    out_sum = z_reduce(out_part)
    grad_attn = later(f_reduce_rows(dot(mid_spread, w_out, 1, 1)).astype(BF), out_part)

    dquery, dkeys, dvalues = attention_grad(query, keys, values, grad_attn, marks)
    dkv = jnp.concatenate([dkeys, dvalues], axis=1)
    up_out = weight_grad(
        later(place, dkv), two_all, trio_alls[0], mom_up, width, True, (1024, 512), (None, 2),
        span=span,
    )
    got_dkv = later(swap(dkv[2 * rows :], "ctx", 2), up_out)
    far = dkv[: 2 * rows].astype(F32) + got_dkv.astype(F32)
    near = far[:rows] + swap(far[rows:].astype(BF), "ctx", 1).astype(F32)
    dqkv = jnp.concatenate(
        [
            unrotate(dquery, cosine, sine),
            unrotate(near[:, :width], cosine, sine),
            near[:, width:],
        ],
        axis=1,
    ).astype(BF)
    mid_two = ctx_two(mid_spread)
    down_out = weight_grad(
        later(place, dqkv), trio_alls[0], dy_all, mom_down, width, False, (512, 1024), (0, None),
        span=span,
    )
    dqkv_rows = later(f_gather_rows(dqkv), mid_two[1], down_out)
    dqkv_two = ctx_two(dqkv_rows)
    dx_one = (
        dot(dqkv_rows[:, :width], w_query, 1, 1)
        + dot(dqkv_rows[:, width : 2 * width], w_key, 1, 1)
        + dot(dqkv_rows[:, 2 * width :], w_value, 1, 1)
    )
    gain_parts = jnp.stack(
        [
            jnp.sum(dx_one * one_spread.astype(F32), axis=0),
            jnp.sum(dx_two * two_spread.astype(F32), axis=0),
        ]
    )
    grad_one = z_reduce(dx_one)

    one_all = ctx_four(one_two)
    gate_out, up_out, down_out = mlp_weights(
        later(place, dqkv_rows, out_sum, gain_parts), two_all, trio_alls[1], dy_all, (mom_gate, mom_up, mom_down),
        width, (1, halves), (gate_out, up_out, down_out),
    )
    g_gate, m_gate, l_gate, gram_gate = gate_out
    g_up, m_up, l_up, gram_up = up_out
    g_down, m_down, l_down, gram_down = down_out

    mid_all, attn_all = ctx_four(later(mid_two, dqkv_rows)), ctx_four(attn_two)
    dqkv_all = ctx_four(later(dqkv_two, g_down))
    gain_sums = all_sum(gain_parts, ("ctx",))
    query_out, key_out, value_out, out_out, gram_attn = attention_weights(
        later(place, g_down, grad_one, gain_sums), one_all, dqkv_all, attn_all, mid_all,
        (mom_query, mom_key, mom_value, mom_out),
    )
    g_query, m_query, l_query = query_out
    g_key, m_key, l_key = key_out
    g_value, m_value, l_value = value_out
    g_out, m_out, l_out = out_out

    out_sum, grad_one, gain_sums = later((out_sum, grad_one, gain_sums), g_value)
    result = f_gather_cols((middle + out_sum).astype(BF))
    scaled_one = own_in * own_inv
    weighted = grad_one * gain_one
    mean = f_all(jnp.sum(weighted * scaled_one, axis=1, keepdims=True)) * (1.0 / depth)
    input_grad = grad_middle + own_inv * (weighted - scaled_one * mean)
    input_grad = f_gather_cols(input_grad.astype(BF))
    result_cols, input_cols = result, input_grad
    result = z_gather_slow(result)
    input_grad = z_gather_slow(input_grad).astype(F32)

    gain_sums = all_sum(gain_sums, ("tp",))
    grad_gain_one = gain_sums[0] / gain_one
    grad_gain_two = gain_sums[1] / gain_two

    if pair():
        even = lax.axis_index("fsdp") == 0
        kept = jnp.where(even, gram_down, gram_gate)
        sent = jnp.where(even, gram_gate, gram_down)
        both = later((kept, swap(sent, "fsdp", 1)), g_value)
        q_own = polynomial(*both)
        got_attn = swap(gram_attn, "fsdp", 1)
        both = later((gram_up, swap(gram_up, "fsdp", 1)), q_own)
        q_up = polynomial(*both)
        q_other = swap(q_own, "fsdp", 1)
        q_down = ctx_two(jnp.where(even, q_own, q_other))
        q_gate = ctx_two(jnp.where(even, q_other, q_own))
        q_up = ctx_two(q_up)
        both = later((gram_attn, got_attn), q_up[0], mean, result_cols)
        q_attn = ctx_two(polynomial(*both))
    else:
        grams = lax.psum(jnp.stack([gram_down, gram_gate, gram_up, gram_attn]), "fsdp")
        none = jnp.zeros_like(gram_up)
        q_down, q_gate, q_up, q_attn = (ctx_two(polynomial(grams[k], none)) for k in range(4))
        got_attn = grams
    q_down, q_gate, q_up, q_attn = (
        jnp.stack(ctx_four(q)) for q in (q_down, q_gate, q_up, q_attn)
    )
    ctx_place = place[:1]
    new_down = update(q_down, l_down, w_down, False, later(ctx_place, input_cols))
    new_gate = update(q_gate, l_gate, w_gate, True, later(ctx_place, new_down, result))
    turn = later(ctx_place, new_gate, input_grad, gain_sums)
    new_up = update(q_up, l_up, w_up, True, turn)

    new_query, new_key, new_value, new_out = attention_update(
        q_attn, (l_query, l_key, l_value, l_out), (w_query, w_key, w_value, w_out), later(ctx_place, new_up)
    )

    return (
        result[None],
        input_grad[None],
        grad_gain_one,
        grad_gain_two,
        g_query,
        g_key,
        g_value,
        g_out,
        g_gate,
        g_up,
        g_down,
        m_query,
        m_key,
        m_value,
        m_out,
        m_gate,
        m_up,
        m_down,
        new_query,
        new_key,
        new_value,
        new_out,
        new_gate,
        new_up,
        new_down,
    )


def solution(mesh):
    act = P("fsdp", "ctx", None)
    col, row, vec = P("fsdp", "tp"), P("tp", "fsdp"), P("fsdp")
    seven = (col, col, col, row, col, col, row)
    in_specs = (act, act, P("fsdp", None), vec, vec) + seven + seven
    out_specs = (act, act, vec, vec) + seven + seven + seven
    return jax.shard_map(body, mesh=mesh, in_specs=in_specs, out_specs=out_specs, check_vma=False)
```

```python
import functools
import math

import jax
import jax.numpy as jnp
from jax import lax
from jax.experimental import pallas as pl
from jax.experimental.pallas import tpu as pltpu
from jax.sharding import PartitionSpec as P

HEAD_DIM = 64
NS_STEPS = 5
EPS = 1e-05
THETA = 130000.0
MOMENTUM = 0.95
COEF_A = 3.4445
COEF_B = -4.775
COEF_C = 2.0315
RATE = 0.5
BF = jnp.bfloat16
F32 = jnp.float32
VMEM_LIMIT = 56 * 1024 * 1024


def dot(left, right, ldim=1, rdim=0):
    return lax.dot_general(
        left, right, (((ldim,), (rdim,)), ((), ())), preferred_element_type=F32
    )


def params():
    return pltpu.CompilerParams(vmem_limit_bytes=VMEM_LIMIT)


def lasting(microseconds):
    return pl.CostEstimate(
        flops=0, bytes_accessed=int(microseconds * 3690000), transcendentals=0
    )


def swap(value, axis, bit):
    size = lax.axis_size(axis)
    return lax.ppermute(value, axis, [(i, i ^ bit) for i in range(size)])


def later(value, *others):
    return lax.optimization_barrier((value, others))[0]


def ctx_two(value):
    return [value, swap(value, "ctx", 2)]


def ctx_four(two):
    value, far = two
    return [value, swap(value, "ctx", 1), far, swap(far, "ctx", 1)]


def ctx_parts(value):
    return ctx_four(ctx_two(value))


def pair():
    return lax.axis_size("fsdp") == 2


def f_scatter_cols(value):
    size = lax.axis_size("fsdp")
    rows, width = value.shape
    part = width // size
    if size == 2:
        own = lax.axis_index("fsdp")
        mine = lax.dynamic_slice_in_dim(value, own * part, part, 1)
        other = lax.dynamic_slice_in_dim(value, (1 - own) * part, part, 1)
        return jnp.concatenate([mine, swap(other, "fsdp", 1)], axis=0)
    cut = jnp.swapaxes(value.reshape(rows, size, part), 0, 1)
    return lax.all_to_all(cut, "fsdp", 0, 0, tiled=True).reshape(size * rows, part)


def f_gather_cols(value):
    size = lax.axis_size("fsdp")
    rows = value.shape[0] // size
    if size == 2:
        own = lax.axis_index("fsdp")
        mine, other = value[:rows], swap(value[rows:], "fsdp", 1)
        return jnp.concatenate(
            [jnp.where(own == 0, mine, other), jnp.where(own == 0, other, mine)], axis=1
        )
    cut = lax.all_to_all(value.reshape(size, rows, -1), "fsdp", 0, 0, tiled=True)
    return jnp.swapaxes(cut, 0, 1).reshape(rows, -1)


def f_gather_rows(value):
    if pair():
        return jnp.concatenate([value, swap(value, "fsdp", 1)], axis=0)
    return lax.all_gather(value, "fsdp", axis=0, tiled=True)


def f_reduce_rows(value):
    size = lax.axis_size("fsdp")
    rows = value.shape[0] // size
    if size == 2:
        return value[:rows].astype(F32) + swap(value[rows:].astype(BF), "fsdp", 1).astype(F32)
    return lax.psum_scatter(value.astype(F32), "fsdp", scatter_dimension=0, tiled=True)


def flip(value):
    half = value.shape[0] // 2
    return jnp.concatenate([value[half:], value[:half]], axis=0)


def f_all(value):
    if pair():
        return value + flip(swap(value, "fsdp", 1))
    return lax.psum(value, "fsdp")


def f_reduce_list(parts):
    rows = parts[0].shape[0] // 2
    sent = jnp.concatenate([p[rows:].astype(BF) for p in parts], axis=1)
    return jnp.concatenate([p[:rows] for p in parts], axis=1) + swap(sent, "fsdp", 1).astype(F32)


def z_shift(value, k):
    size = lax.axis_size("tp")
    return lax.ppermute(value, "tp", [(i, (i + k) % size) for i in range(size)])


def z_shifts():
    size = lax.axis_size("tp")
    return sorted(range(1, size), key=lambda k: -min(k, size - k))


def by_quarter(value):
    size, groups = lax.axis_size("tp"), lax.axis_size("fsdp")
    rows, width = value.shape
    part = rows // (size * groups)
    cut = jnp.swapaxes(value.reshape(groups, size, part, width), 0, 1)
    return cut.reshape(size, groups * part, width)


def own_quarter(value):
    return lax.dynamic_index_in_dim(by_quarter(value), lax.axis_index("tp"), 0, keepdims=False)


def z_reduce(value):
    sent = by_quarter(value.astype(BF))
    return jnp.sum(lax.all_to_all(sent, "tp", 0, 0, tiled=True).astype(F32), axis=0)


def z_gather(value):
    size, groups = lax.axis_size("tp"), lax.axis_size("fsdp")
    rows, width = value.shape
    full = lax.all_gather(value, "tp", axis=0)
    full = jnp.swapaxes(full.reshape(size, groups, rows // groups, width), 0, 1)
    return full.reshape(size * rows, width)


def z_reduce_slow(value):
    size, me = lax.axis_size("tp"), lax.axis_index("tp")
    cut = by_quarter(value)
    total = lax.dynamic_index_in_dim(cut, me, 0, keepdims=False).astype(F32)
    for k in z_shifts():
        sent = lax.dynamic_index_in_dim(cut, (me + k) % size, 0, keepdims=False).astype(BF)
        total = total + z_shift(sent, k).astype(F32)
    return total


def z_gather_groups_slow(value, wait=()):
    size, groups = lax.axis_size("tp"), lax.axis_size("fsdp")
    rows, width = value.shape
    full = z_gather_slow(value, wait).reshape(size, groups, rows // groups, width)
    return jnp.swapaxes(full, 0, 1).reshape(size * rows, width)


def z_gather_slow(value, wait=()):
    size, me = lax.axis_size("tp"), lax.axis_index("tp")
    by_place = {k: later(z_shift(value, k), wait) for k in z_shifts()}
    by_place[0] = value
    ordered = []
    for at in range(size):
        chosen = value
        for k in z_shifts():
            chosen = jnp.where((me - k) % size == at, by_place[k], chosen)
        ordered.append(chosen)
    return jnp.concatenate(ordered, axis=0)


def all_sum(value, axes):
    for axis in axes:
        size = lax.axis_size(axis)
        if axis == "tp":
            value = value + sum(z_shift(value, k) for k in z_shifts())
        else:
            bit = 1
            while bit < size:
                value = value + swap(value, axis, bit)
                bit *= 2
    return value


def rope_tables(position, width):
    half = HEAD_DIM // 2
    freq = THETA ** (-(jnp.arange(half, dtype=F32) * 2.0 / HEAD_DIM))
    angle = position[:, None] * freq[None, :]
    repeat = width // half
    return jnp.tile(jnp.cos(angle), (1, repeat)), jnp.tile(jnp.sin(angle), (1, repeat))


def first_half(shape):
    lane = lax.broadcasted_iota(jnp.int32, shape, 1)
    return (lane & (HEAD_DIM - 1)) < HEAD_DIM // 2


def rotate(values, cosine, sine):
    half = HEAD_DIM // 2
    turned = jnp.where(
        first_half(values.shape), -jnp.roll(values, -half, 1), jnp.roll(values, half, 1)
    )
    return values * cosine + turned * sine


def unrotate(grads, cosine, sine):
    half = HEAD_DIM // 2
    scaled = grads * sine
    back = jnp.where(
        first_half(grads.shape), jnp.roll(scaled, -half, 1), -jnp.roll(scaled, half, 1)
    )
    return grads * cosine + back


def head_probs(query, keys, allowed, scale):
    scores = jnp.where(allowed, dot(query, keys, 1, 1) * scale, -1e30)
    top = jnp.max(scores, axis=1, keepdims=True)
    expo = jnp.exp(scores - top)
    return expo / jnp.sum(expo, axis=1, keepdims=True)


def attention_kernel(scale, q_ref, k_ref, v_ref, qi_ref, qs_ref, ki_ref, ks_ref, o_ref):
    allowed = (ks_ref[...] == qs_ref[...]) & (ki_ref[...] <= qi_ref[...])
    query, keys, values = q_ref[...], k_ref[...], v_ref[...]
    lane = lax.broadcasted_iota(jnp.int32, query.shape, 1)
    outs = []
    for head in range(2):
        mine = (lane >= HEAD_DIM) == (head == 1)
        prob = head_probs(jnp.where(mine, query, 0), keys, allowed, scale)
        outs.append(dot(prob.astype(BF), values))
    o_ref[...] = jnp.where(lane < HEAD_DIM, outs[0], outs[1]).astype(BF)


def attention_grad_kernel(
    scale, q_ref, k_ref, v_ref, g_ref, qi_ref, qs_ref, ki_ref, ks_ref, dq_ref, dk_ref, dv_ref
):
    allowed = (ks_ref[...] == qs_ref[...]) & (ki_ref[...] <= qi_ref[...])
    query, keys, values, grads = q_ref[...], k_ref[...], v_ref[...], g_ref[...]
    lane = lax.broadcasted_iota(jnp.int32, query.shape, 1)
    wide = lax.broadcasted_iota(jnp.int32, keys.shape, 1)
    dqs, dks, dvs = [], [], []
    for head in range(2):
        mine = (lane >= HEAD_DIM) == (head == 1)
        prob = head_probs(jnp.where(mine, query, 0), keys, allowed, scale)
        dprob = dot(jnp.where(mine, grads, 0), values, 1, 1)
        delta = jnp.sum(prob * dprob, axis=1, keepdims=True)
        dscore = (prob * (dprob - delta)).astype(BF)
        dqs.append(dot(dscore, keys))
        dks.append(dot(dscore, query, 0, 0))
        dvs.append(dot(prob.astype(BF), grads, 0, 0))
    low, wlow = lane < HEAD_DIM, wide < HEAD_DIM
    dq_ref[...] = jnp.where(low, dqs[0], dqs[1]) * scale
    dk_ref[...] = (jnp.where(wlow, dks[0], dks[1]) * scale).astype(BF)
    dv_ref[...] = jnp.where(wlow, dvs[0], dvs[1]).astype(BF)


def attention_specs(rows, keys):
    def col(n):
        return pl.BlockSpec((n, 2 * HEAD_DIM), lambda h: (0, h))

    def whole(shape):
        return pl.BlockSpec(shape, lambda h: (0, 0))

    marks = [whole((rows, 1)), whole((rows, 1)), whole((1, keys)), whole((1, keys))]
    return col, marks


def attention(query, keys, values, marks):
    rows, width = query.shape
    count = keys.shape[0]
    col, mark_specs = attention_specs(rows, count)
    return pl.pallas_call(
        functools.partial(attention_kernel, 1.0 / math.sqrt(HEAD_DIM)),
        grid=(width // (2 * HEAD_DIM),),
        in_specs=[col(rows), col(count), col(count)] + mark_specs,
        out_specs=col(rows),
        out_shape=jax.ShapeDtypeStruct((rows, width), BF),
        compiler_params=params(),
        cost_estimate=lasting(5.5),
        name="attention",
    )(query, keys, values, *marks)


def attention_grad(query, keys, values, grads, marks):
    rows, width = query.shape
    count = keys.shape[0]
    col, mark_specs = attention_specs(rows, count)
    return pl.pallas_call(
        functools.partial(attention_grad_kernel, 1.0 / math.sqrt(HEAD_DIM)),
        grid=(width // (2 * HEAD_DIM),),
        in_specs=[col(rows), col(count), col(count), col(rows)] + mark_specs,
        out_specs=[col(rows), col(count), col(count)],
        out_shape=[
            jax.ShapeDtypeStruct((rows, width), F32),
            jax.ShapeDtypeStruct((count, width), BF),
            jax.ShapeDtypeStruct((count, width), BF),
        ],
        compiler_params=params(),
        cost_estimate=lasting(7),
        name="attention_grad",
    )(query, keys, values, grads, *marks)


def smem():
    return pl.BlockSpec(memory_space=pltpu.SMEM)


def units_kernel(x_ref, wg_ref, wu_ref, own_ref, sent_ref):
    for k, w_ref in enumerate((wg_ref, wu_ref)):
        part = dot(x_ref[...], w_ref[...])
        own_ref[k] = part
        sent_ref[k] = part.astype(BF)


def units(x, wgate, wup, at, count, tile=512):
    rows, depth = x.shape
    steps = count // tile
    weight = pl.BlockSpec((depth, tile), lambda n: (0, at * steps + n))
    out = pl.BlockSpec((2, rows, tile), lambda n: (0, 0, n))
    return pl.pallas_call(
        units_kernel,
        grid=(steps,),
        in_specs=[pl.BlockSpec((rows, depth), lambda n: (0, 0)), weight, weight],
        out_specs=[out, out],
        out_shape=[
            jax.ShapeDtypeStruct((2, rows, count), F32),
            jax.ShapeDtypeStruct((2, rows, count), BF),
        ],
        compiler_params=params(),
        cost_estimate=lasting(4.5),
        name="units",
    )(x, wgate, wup)


def hidden_kernel(paired, first, own_ref, got_ref, dh_ref, dgot_ref, wg_ref, wu_ref, *refs):
    if first:
        out_ref, acc_ref = refs
    else:
        before_ref, out_ref, acc_ref = refs
    half = dh_ref.shape[0] // 2

    def total(own, got):
        if not paired:
            return own
        got = got.astype(F32)
        return own + jnp.concatenate([got[half:], got[:half]], axis=0)

    gate = total(own_ref[0], got_ref[0])
    upper = total(own_ref[1], got_ref[1])
    dhid = total(dh_ref[...], dgot_ref[...])
    sigma = jax.nn.sigmoid(gate)
    silu = gate * sigma
    dgate = (dhid * upper * sigma * (1.0 + gate * (1.0 - sigma))).astype(BF)
    dup = (dhid * silu).astype(BF)
    out_ref[0] = (silu * upper).astype(BF)
    out_ref[1] = dgate
    out_ref[2] = dup
    grad = dot(dgate, wg_ref[...], 1, 1) + dot(dup, wu_ref[...], 1, 1)

    @pl.when(pl.program_id(0) == 0)
    def _():
        acc_ref[...] = grad if first else grad + before_ref[...]

    @pl.when(pl.program_id(0) > 0)
    def _():
        acc_ref[...] += grad


def hidden_units(own, got, dhid, dgot, wgate, wup, at, before=None, tile=512):
    _, rows, count = own.shape
    depth = wgate.shape[0]
    steps = count // tile
    weight = pl.BlockSpec((depth, tile), lambda n: (0, at * steps + n))
    trio = pl.BlockSpec((2, rows, tile), lambda n: (0, 0, n))
    lanes = pl.BlockSpec((rows, tile), lambda n: (0, at * steps + n))
    total = pl.BlockSpec((rows, depth), lambda n: (0, 0))
    args = [own, got, dhid, dgot, wgate, wup] + ([] if before is None else [before])
    return pl.pallas_call(
        functools.partial(hidden_kernel, pair(), before is None),
        grid=(steps,),
        in_specs=[trio, trio, lanes, lanes, weight, weight] + [total] * (len(args) - 6),
        out_specs=[pl.BlockSpec((3, rows, tile), lambda n: (0, 0, n)), total],
        out_shape=[
            jax.ShapeDtypeStruct((3, rows, count), BF),
            jax.ShapeDtypeStruct((rows, depth), F32),
        ],
        compiler_params=params(),
        cost_estimate=lasting(6),
        name="hidden_units",
    )(*args)


def joined(parts):
    return jnp.concatenate([r[...].reshape(r.shape[-2:]) for r in parts], axis=0)


def moved(total, mom_ref, g_ref, m_ref, l_ref):
    mom = MOMENTUM * mom_ref[...] + total
    g_ref[...] = total
    m_ref[...] = mom
    l_ref[...] = (total + MOMENTUM * mom).astype(BF)


def add_gram(gram_ref, look_ref, by_columns, hit, first):
    half = gram_ref.shape[1]

    def three():
        if by_columns:
            low, high = look_ref[:, :half], look_ref[:, half:]
        else:
            low, high = look_ref[:half, :], look_ref[half:, :]
        dim = 0 if by_columns else 1
        return [dot(x, y, dim, dim) for x, y in ((low, low), (low, high), (high, high))]

    @pl.when(jnp.logical_and(hit, first))
    def _():
        for k, value in enumerate(three()):
            gram_ref[k] = value

    @pl.when(jnp.logical_and(hit, jnp.logical_not(first)))
    def _():
        for k, value in enumerate(three()):
            gram_ref[k] += value


def gram_spec(size):
    half = size // 2
    return (
        pl.BlockSpec((3, half, half), lambda *at: (0, 0, 0)),
        jax.ShapeDtypeStruct((3, half, half), F32),
    )


def weight_grad_kernel(nl, nr, by_columns, base, filled, place_ref, *refs):
    lefts, rights = refs[:nl], refs[nl : nl + nr]
    mom_ref, g_ref, m_ref, l_ref, gram_ref = refs[nl + nr], *refs[-4:]
    tall, wide = g_ref.shape
    moved(dot(joined(lefts), joined(rights), 0, 0), mom_ref, g_ref, m_ref, l_ref)
    i, j = pl.program_id(0), pl.program_id(1)
    outer, inner = (j, i) if by_columns else (i, j)
    size = 2 * gram_ref.shape[1]
    count = (wide if by_columns else tall) // size

    if filled:

        @pl.when(jnp.logical_and(i == 0, j == 0))
        def _():
            gram_ref[...] = refs[nl + nr + 4][...]

    for k in range(count):
        at = pl.ds(k * size, size)
        look = l_ref.at[:, at] if by_columns else l_ref.at[at, :]
        add_gram(gram_ref, look, by_columns, base + outer * count + k == place_ref[0], inner == 0)


def weight_grad(
    place, lefts, rights, mom, size, by_columns, tile, planes=(None, None), span=None, into=None
):
    height, width = mom.shape
    part, parts = span or (0, 1)
    tm, tn = min(tile[0], height), min(tile[1], width)
    grid = [height // tm, width // tn]
    axis = 1 if by_columns else 0
    grid[axis] //= parts
    start = [0, 0]
    start[axis] = part * grid[axis]
    out = pl.BlockSpec((tm, tn), lambda i, j: (start[0] + i, start[1] + j))
    tok = sum(v.shape[-2] for v in lefts)

    def specs(values, plane, lanes, place_of):
        if plane is None:
            return [pl.BlockSpec((v.shape[0], lanes), lambda i, j: (0, place_of(i, j))) for v in values]
        return [
            pl.BlockSpec((1, v.shape[1], lanes), lambda i, j: (plane, 0, place_of(i, j)))
            for v in values
        ]

    whole_gram, gram_shape = gram_spec(size)
    in_specs = [smem()]
    in_specs += specs(lefts, planes[0], tm, lambda i, j: i)
    in_specs += specs(rights, planes[1], tn, lambda i, j: j)
    in_specs += [out]
    args = [place, *lefts, *rights, mom]
    aliases = {}
    if into is not None:
        aliases = {len(args) + k: k for k in range(3)}
        in_specs += [pl.BlockSpec(memory_space=pl.ANY)] * 3 + [whole_gram]
        args += list(into)
    blocks = (width if by_columns else height) // size // parts
    return pl.pallas_call(
        functools.partial(
            weight_grad_kernel, len(lefts), len(rights), by_columns, part * blocks, into is not None
        ),
        grid=tuple(grid),
        in_specs=in_specs,
        out_specs=[out, out, out, whole_gram],
        out_shape=[
            jax.ShapeDtypeStruct((height, width), F32),
            jax.ShapeDtypeStruct((height, width), F32),
            jax.ShapeDtypeStruct((height, width), BF),
            gram_shape,
        ],
        input_output_aliases=aliases,
        compiler_params=params(),
        cost_estimate=lasting(9),
        name="weight_grad",
    )(*args)


def attention_weights_kernel(count, place_ref, *refs):
    ones, grads, attns, mids = (refs[k * count : (k + 1) * count] for k in range(4))
    refs = refs[4 * count :]
    moms, outs, gram_ref = refs[:4], refs[4:16], refs[16]
    first = pl.program_id(0) == 0
    left = joined(ones)
    width = moms[0].shape[1]
    for k in range(3):
        right = jnp.concatenate([r[:, k * width : (k + 1) * width] for r in grads], axis=0)
        moved(dot(left, right, 0, 0), moms[k], *outs[3 * k : 3 * k + 3])
        add_gram(gram_ref, outs[3 * k + 2], True, place_ref[0] == k, first)
    moved(dot(joined(attns), joined(mids), 0, 0), moms[3], *outs[9:12])
    add_gram(gram_ref, outs[11], False, place_ref[0] == 3, first)


def attention_weights(place, ones, grads, attns, mids, moms, tile=256):
    share, width = moms[0].shape
    tile = min(tile, share)

    def cols(v):
        return pl.BlockSpec((v.shape[0], tile), lambda i: (0, i))

    def whole(v):
        return pl.BlockSpec(v.shape, lambda i: (0, 0))

    tall = pl.BlockSpec((tile, width), lambda i: (i, 0))
    wide = pl.BlockSpec((width, tile), lambda i: (0, i))
    gram, gram_shape = gram_spec(width)
    shapes = []
    for mom in moms:
        shapes += [jax.ShapeDtypeStruct(mom.shape, kind) for kind in (F32, F32, BF)]
    out = pl.pallas_call(
        functools.partial(attention_weights_kernel, len(ones)),
        grid=(share // tile,),
        in_specs=[smem()]
        + [cols(v) for v in ones]
        + [whole(v) for v in grads]
        + [whole(v) for v in attns]
        + [cols(v) for v in mids]
        + [tall, tall, tall, wide],
        out_specs=[tall] * 9 + [wide] * 3 + [gram],
        out_shape=shapes + [gram_shape],
        compiler_params=params(),
        cost_estimate=lasting(18),
        name="attention_weights",
    )(place, *ones, *grads, *attns, *mids, *moms)
    return out[:3], out[3:6], out[6:9], out[9:12], out[12]


def mlp_weights_kernel(count, base, filled, place_ref, *refs):
    twos, hids, dgates, dups, dys = (refs[k * count : (k + 1) * count] for k in range(5))
    refs = refs[5 * count :]
    moms, refs = refs[:3], refs[3:]
    before, refs = (refs[9:12], refs[12:]) if filled else (None, refs)
    outs, grams = refs[:9], refs[9:]
    j, i = pl.program_id(0), pl.program_id(1)

    if filled:

        @pl.when(jnp.logical_and(i == 0, j == 0))
        def _():
            for gram_ref, old in zip(grams, before):
                gram_ref[...] = old[...]

    two = joined(twos)
    hit, first = base + j == place_ref[0], i == 0
    moved(dot(two, joined(dgates), 0, 0), moms[0], *outs[:3])
    add_gram(grams[0], outs[2], True, hit, first)
    moved(dot(two, joined(dups), 0, 0), moms[1], *outs[3:6])
    add_gram(grams[1], outs[5], True, hit, first)
    moved(dot(joined(hids), joined(dys), 0, 0), moms[2], *outs[6:9])
    add_gram(grams[2], outs[8], False, hit, first)


def mlp_weights(place, twos, trios, dys, moms, size, span, into, tile=512):
    share, width = moms[0].shape
    part, parts = span
    blocks = width // size // parts
    tile = min(tile, share)

    def cols(v):
        return pl.BlockSpec((v.shape[0], tile), lambda j, i: (0, i))

    def plane(v, k):
        return pl.BlockSpec((1, v.shape[1], size), lambda j, i: (k, 0, j))

    tall = pl.BlockSpec((tile, size), lambda j, i: (i, part * blocks + j))
    wide = pl.BlockSpec((size, tile), lambda j, i: (part * blocks + j, i))
    gram, gram_shape = gram_spec(size)
    shapes = []
    for mom in moms:
        shapes += [jax.ShapeDtypeStruct(mom.shape, kind) for kind in (F32, F32, BF)]
    in_specs = [smem()] + [cols(v) for v in twos]
    for k in range(3):
        in_specs += [plane(v, k) for v in trios]
    in_specs += [cols(v) for v in dys] + [tall, tall, wide]
    args = [place, *twos, *trios, *trios, *trios, *dys, *moms]
    aliases = {len(args) + k: k for k in range(9)}
    in_specs += [pl.BlockSpec(memory_space=pl.ANY)] * 9 + [gram] * 3
    args += [v for out in into for v in out[:3]] + [out[3] for out in into]
    out = pl.pallas_call(
        functools.partial(mlp_weights_kernel, len(twos), part * blocks, True),
        grid=(blocks, share // tile),
        in_specs=in_specs,
        out_specs=[tall] * 6 + [wide] * 3 + [gram] * 3,
        out_shape=shapes + [gram_shape] * 3,
        input_output_aliases=aliases,
        compiler_params=params(),
        cost_estimate=lasting(24),
        name="mlp_weights",
    )(*args)
    return [(*out[3 * k : 3 * k + 3], out[9 + k]) for k in range(3)]


def polynomial_kernel(a_ref, b_ref, out_ref, full_ref):
    size, half = full_ref.shape[0], full_ref.shape[0] // 2
    corner = a_ref[1] + b_ref[1]
    full_ref[:half, :half] = a_ref[0] + b_ref[0]
    full_ref[:half, half:] = corner
    full_ref[half:, :half] = corner.T
    full_ref[half:, half:] = a_ref[2] + b_ref[2]
    row = lax.broadcasted_iota(jnp.int32, (size, size), 0)
    column = lax.broadcasted_iota(jnp.int32, (size, size), 1)
    eye = row == column

    def split(full):
        only = jnp.where(eye, full, 0.0)
        return (
            jnp.where(eye, 0.0, full),
            jnp.sum(only, axis=1, keepdims=True),
            jnp.sum(only, axis=0, keepdims=True),
        )

    def times(left, right):
        loff, lcol, lrow = left
        roff, rcol, rrow = right
        full = dot(loff.astype(BF), roff.astype(BF)) + lcol * roff + loff * rrow
        off, dcol, drow = split(full)
        return off, dcol + lcol * rcol, drow + lrow * rrow

    def mix(coefs, first, second, shift):
        off = coefs[0] * first[0] + coefs[1] * second[0]
        dcol = coefs[0] * first[1] + coefs[1] * second[1] + shift
        drow = coefs[0] * first[2] + coefs[1] * second[2] + shift
        return off, dcol, drow

    gram = split(full_ref[...])
    norm = jnp.sqrt(jnp.sum(gram[2])) + 1e-07
    inverse = 1.0 / (norm * norm)
    gram = tuple(part * inverse for part in gram)
    total = None
    for step in range(NS_STEPS):
        square = times(gram, gram)
        factor = mix((COEF_B, COEF_C), gram, square, COEF_A)
        total = factor if total is None else times(factor, total)
        if step < NS_STEPS - 1:
            gram = times(factor, times(factor, gram))
    weight = -RATE / norm
    off = (total[0] * weight).astype(BF)
    out_ref[:half] = off[:half, :half]
    out_ref[half:size] = off[:half, half:]
    out_ref[size : size + half] = off[half:, half:]
    diagonal = total[2] * weight
    high = diagonal.astype(BF).astype(F32)
    low = diagonal - high
    line = lax.broadcasted_iota(jnp.int32, (16, half), 0)
    tail = jnp.zeros((16, half), F32)
    for k, part in enumerate((high[:, :half], high[:, half:], low[:, :half], low[:, half:])):
        tail = jnp.where(line == k, part, tail)
    out_ref[size + half :] = tail.astype(BF)


def polynomial(a, b):
    half = a.shape[1]
    size = 2 * half
    return pl.pallas_call(
        polynomial_kernel,
        in_specs=[pl.BlockSpec(memory_space=pltpu.VMEM)] * 2,
        out_specs=pl.BlockSpec(memory_space=pltpu.VMEM),
        out_shape=jax.ShapeDtypeStruct((3 * half + 16, half), BF),
        scratch_shapes=[pltpu.VMEM((size, size), F32)],
        compiler_params=params(),
        cost_estimate=lasting(10),
        name="polynomial",
    )(a, b)


def unpack(packed, factor_ref, column):
    half = packed.shape[1]
    corner = packed[half : 2 * half]
    factor_ref[:half, :half] = packed[:half]
    factor_ref[:half, half:] = corner
    factor_ref[half:, :half] = corner.astype(F32).T.astype(BF)
    factor_ref[half:, half:] = packed[2 * half : 3 * half]
    ends = packed[3 * half :].astype(F32)
    line = jnp.concatenate([ends[0:1] + ends[2:3], ends[1:2] + ends[3:4]], axis=1)
    if not column:
        return line
    size = 2 * half
    eye = lax.broadcasted_iota(jnp.int32, (size, size), 0) == lax.broadcasted_iota(
        jnp.int32, (size, size), 1
    )
    return jnp.sum(jnp.where(eye, line, 0.0), axis=1, keepdims=True)


def stepped(look_ref, w_ref, o_ref, factor, diagonal, by_columns):
    look = look_ref[...]
    step = dot(look, factor) if by_columns else dot(factor, look)
    o_ref[...] = w_ref[...].astype(F32) + (step + look.astype(F32) * diagonal)


def update_kernel(by_columns, me_ref, q_ref, l_ref, w_ref, o_ref, factor_ref, line_ref):
    @pl.when(pl.program_id(1) == 0)
    def _():
        line_ref[...] = unpack(q_ref[0], factor_ref, not by_columns)

    stepped(l_ref, w_ref, o_ref, factor_ref[...], line_ref[...], by_columns)


def update(factors, look, weight, by_columns, me):
    _, packed, half = factors.shape
    size = 2 * half
    height, width = weight.shape
    if by_columns:
        tile = min(1024, height)
        grid = (width // size, height // tile)
        spec = pl.BlockSpec((tile, size), lambda b, i, me_ref: (i, b))
    else:
        tile = min(1024, width)
        grid = (height // size, width // tile)
        spec = pl.BlockSpec((size, tile), lambda b, i, me_ref: (b, i))
    return pl.pallas_call(
        functools.partial(update_kernel, by_columns),
        grid_spec=pltpu.PrefetchScalarGridSpec(
            num_scalar_prefetch=1,
            grid=grid,
            in_specs=[
                pl.BlockSpec((1, packed, half), lambda b, i, me_ref: (b ^ me_ref[0], 0, 0)),
                spec,
                spec,
            ],
            out_specs=spec,
            scratch_shapes=[
                pltpu.VMEM((size, size), BF),
                pltpu.VMEM((1, size) if by_columns else (size, 1), F32),
            ],
        ),
        out_shape=jax.ShapeDtypeStruct(weight.shape, F32),
        compiler_params=params(),
        cost_estimate=lasting(9),
        name="update",
    )(me, factors, look, weight)


def attention_update_kernel(me_ref, *refs):
    qs, looks, weights, outs = refs[:4], refs[4:8], refs[8:12], refs[12:16]
    factor_ref, row_ref, column_ref = refs[16:]

    @pl.when(pl.program_id(0) == 0)
    def _():
        for k in range(3):
            row_ref[k] = unpack(qs[k][0], factor_ref.at[k], False)
        column_ref[...] = unpack(qs[3][0], factor_ref.at[3], True)

    for k in range(3):
        stepped(looks[k], weights[k], outs[k], factor_ref[k], row_ref[k], True)
    stepped(looks[3], weights[3], outs[3], factor_ref[3], column_ref[...], False)


def attention_update(factors, looks, weights, me, tile=256):
    _, packed, half = factors.shape
    size = 2 * half
    share, width = weights[0].shape
    tile = min(tile, share)
    tall = pl.BlockSpec((tile, width), lambda i, me_ref: (i, 0))
    wide = pl.BlockSpec((width, tile), lambda i, me_ref: (0, i))

    def factor(k):
        return pl.BlockSpec((1, packed, half), lambda i, me_ref: (me_ref[0] ^ k, 0, 0))

    specs = [tall, tall, tall, wide]
    return pl.pallas_call(
        attention_update_kernel,
        grid_spec=pltpu.PrefetchScalarGridSpec(
            num_scalar_prefetch=1,
            grid=(share // tile,),
            in_specs=[factor(k) for k in range(4)] + specs + specs,
            out_specs=specs,
            scratch_shapes=[
                pltpu.VMEM((4, size, size), BF),
                pltpu.VMEM((3, 1, size), F32),
                pltpu.VMEM((size, 1), F32),
            ],
        ),
        out_shape=[jax.ShapeDtypeStruct(w.shape, F32) for w in weights],
        compiler_params=params(),
        cost_estimate=lasting(9),
        name="attention_update",
    )(me, factors, factors, factors, factors, *looks, *weights)


def body(
    tokens,
    out_grad,
    segment_start,
    norm_attn,
    norm_mlp,
    w_query,
    w_key,
    w_value,
    w_out,
    w_gate,
    w_up,
    w_down,
    mom_query,
    mom_key,
    mom_value,
    mom_out,
    mom_gate,
    mom_up,
    mom_down,
):
    rows = tokens.shape[1]
    me = lax.axis_index("ctx")
    groups = lax.axis_size("fsdp")
    place = jnp.stack([me, me]).astype(jnp.int32)
    width = w_query.shape[1]
    depth = tokens.shape[2]
    low_in = tokens[0]
    inputs = low_in.astype(F32)
    gain_one, gain_two = norm_attn.astype(F32), norm_mlp.astype(F32)

    spread = f_scatter_cols(low_in)
    inv_one = lax.rsqrt(jnp.mean(inputs * inputs, axis=1, keepdims=True) + EPS)
    inv_spread = f_gather_rows(inv_one)
    scaled = (spread.astype(F32) * gain_one).astype(BF)
    one_spread = (spread.astype(F32) * inv_spread * gain_one).astype(BF)

    partial = [dot(scaled, w) for w in (w_query, w_key, w_value)]
    if pair():
        qkv = f_reduce_list(partial)
    else:
        qkv = jnp.concatenate([f_reduce_rows(part) for part in partial], axis=1)
    qkv = later(qkv * inv_one, inv_spread)
    dy_spread = f_scatter_cols(out_grad[0])
    one_two, dy_two = ctx_two(one_spread), ctx_two(dy_spread)

    starts = segment_start[0]
    chunks = [(me ^ j) * rows for j in range(lax.axis_size("ctx"))]
    key_start = jnp.concatenate([lax.dynamic_slice_in_dim(starts, o, rows) for o in chunks])
    key_index = jnp.concatenate([o + jnp.arange(rows, dtype=jnp.int32) for o in chunks])
    query_start, query_index = key_start[:rows], key_index[:rows]
    cosine, sine = rope_tables((query_index - query_start).astype(F32), width)
    marks = (query_index[:, None], query_start[:, None], key_index[None], key_start[None])

    query = rotate(qkv[:, :width], cosine, sine).astype(BF)
    kv_own = jnp.concatenate(
        [rotate(qkv[:, width : 2 * width], cosine, sine), qkv[:, 2 * width :]], axis=1
    ).astype(BF)
    kv = jnp.concatenate(ctx_parts(kv_own), axis=0)
    keys, values = kv[:, :width], kv[:, width:]
    query = later(query, dy_spread)
    attn = attention(query, keys, values, marks)
    attn_rows = f_gather_rows(attn)

    dhid = dot(dy_spread, w_down, 1, 1)
    attn_two = ctx_two(attn_rows)
    attn_rows = later(attn_rows, dhid)

    own_in = own_quarter(spread).astype(F32)
    own_inv = own_quarter(inv_spread)
    own_dy = own_quarter(dy_spread).astype(F32)

    middle = own_in + later(z_reduce(dot(attn_rows, w_out)), dy_two[1], attn_two[1])
    squares = f_all(jnp.sum(middle * middle, axis=1, keepdims=True))
    inv_two = lax.rsqrt(squares * (1.0 / depth) + EPS)
    own_two = (middle * inv_two * gain_two).astype(BF)
    if pair():
        dhid_got = swap(later(dhid.astype(BF), own_two), "fsdp", 1)
    else:
        dhid_got = dhid = lax.psum(dhid, "fsdp")
    two_spread = later(z_gather(own_two), dhid_got)
    two_two = ctx_two(two_spread)

    halves = 2
    count = w_gate.shape[1] // halves
    parts = [units(two_spread, w_gate, w_up, p, count) for p in range(halves)]
    if pair():
        got = [swap(sent, "fsdp", 1) for _, sent in parts]
        owns = [own for own, _ in parts]
    else:
        owns = [lax.psum(own, "fsdp") for own, _ in parts]
        got = owns
    owns[0] = later(owns[0], owns[1], two_two[1], one_two[1])
    trios, dx_two = [], None
    for p in range(halves):
        trio, dx_two = hidden_units(
            owns[p], got[p], dhid, dhid_got, w_gate, w_up, p, before=dx_two
        )
        trios.append(trio)

    trio_twos = [ctx_two(trio) for trio in trios]
    grad_two = z_reduce_slow(dx_two)
    trio_alls = [ctx_four(later(two, grad_two)) for two in trio_twos]
    two_all, dy_all = ctx_four(later(two_two, grad_two)), ctx_four(later(dy_two, grad_two))
    scaled_two = middle * inv_two
    weighted = grad_two * gain_two
    mean = f_all(jnp.sum(weighted * scaled_two, axis=1, keepdims=True)) * (1.0 / depth)
    grad_middle = own_dy + inv_two * (weighted - scaled_two * mean)
    own_mid = later(grad_middle.astype(BF), trio_twos[0][1], trio_twos[1][1])
    span = (0, halves)
    gate_out = weight_grad(
        later(place, own_mid), two_all, trio_alls[0], mom_gate, width, True, (1024, 512), (None, 1),
        span=span,
    )
    mid_spread = z_gather_groups_slow(own_mid, gate_out)
    out_part = sum(
        dot(trio[0], w_down[p * count : (p + 1) * count]) for p, trio in enumerate(trios)
    ).astype(BF)
    out_sum = z_reduce(out_part)
    grad_attn = later(f_reduce_rows(dot(mid_spread, w_out, 1, 1)).astype(BF), out_part)

    dquery, dkeys, dvalues = attention_grad(query, keys, values, grad_attn, marks)
    dkv = jnp.concatenate([dkeys, dvalues], axis=1)
    up_out = weight_grad(
        later(place, dkv), two_all, trio_alls[0], mom_up, width, True, (1024, 512), (None, 2),
        span=span,
    )
    got_dkv = later(swap(dkv[2 * rows :], "ctx", 2), up_out)
    far = dkv[: 2 * rows].astype(F32) + got_dkv.astype(F32)
    near = far[:rows] + swap(far[rows:].astype(BF), "ctx", 1).astype(F32)
    dqkv = jnp.concatenate(
        [
            unrotate(dquery, cosine, sine),
            unrotate(near[:, :width], cosine, sine),
            near[:, width:],
        ],
        axis=1,
    ).astype(BF)
    mid_two = ctx_two(mid_spread)
    down_out = weight_grad(
        later(place, dqkv), trio_alls[0], dy_all, mom_down, width, False, (512, 1024), (0, None),
        span=span,
    )
    dqkv_rows = later(f_gather_rows(dqkv), mid_two[1], down_out)
    dqkv_two = ctx_two(dqkv_rows)
    dx_one = (
        dot(dqkv_rows[:, :width], w_query, 1, 1)
        + dot(dqkv_rows[:, width : 2 * width], w_key, 1, 1)
        + dot(dqkv_rows[:, 2 * width :], w_value, 1, 1)
    )
    gain_parts = jnp.stack(
        [
            jnp.sum(dx_one * one_spread.astype(F32), axis=0),
            jnp.sum(dx_two * two_spread.astype(F32), axis=0),
        ]
    )
    grad_one = z_reduce(dx_one)

    one_all = ctx_four(one_two)
    gate_out, up_out, down_out = mlp_weights(
        later(place, dqkv_rows, out_sum, gain_parts), two_all, trio_alls[1], dy_all, (mom_gate, mom_up, mom_down),
        width, (1, halves), (gate_out, up_out, down_out),
    )
    g_gate, m_gate, l_gate, gram_gate = gate_out
    g_up, m_up, l_up, gram_up = up_out
    g_down, m_down, l_down, gram_down = down_out

    mid_all, attn_all = ctx_four(later(mid_two, dqkv_rows)), ctx_four(attn_two)
    dqkv_all = ctx_four(later(dqkv_two, g_down))
    gain_sums = all_sum(gain_parts, ("ctx",))
    query_out, key_out, value_out, out_out, gram_attn = attention_weights(
        later(place, g_down, grad_one, gain_sums), one_all, dqkv_all, attn_all, mid_all,
        (mom_query, mom_key, mom_value, mom_out),
    )
    g_query, m_query, l_query = query_out
    g_key, m_key, l_key = key_out
    g_value, m_value, l_value = value_out
    g_out, m_out, l_out = out_out

    out_sum, grad_one, gain_sums = later((out_sum, grad_one, gain_sums), g_value)
    result = middle + out_sum
    scaled_one = own_in * own_inv
    weighted = grad_one * gain_one
    mean = f_all(jnp.sum(weighted * scaled_one, axis=1, keepdims=True)) * (1.0 / depth)
    input_grad = grad_middle + own_inv * (weighted - scaled_one * mean)
    finals = jnp.concatenate([result, input_grad], axis=1).astype(BF)

    gain_sums = all_sum(gain_sums, ("tp",))
    grad_gain_one = gain_sums[0] / gain_one
    grad_gain_two = gain_sums[1] / gain_two

    if pair():
        even = lax.axis_index("fsdp") == 0
        kept = jnp.where(even, gram_down, gram_gate)
        sent = jnp.where(even, gram_gate, gram_down)
        both = later((kept, swap(sent, "fsdp", 1)), g_value)
        q_own = polynomial(*both)
        got_attn = swap(gram_attn, "fsdp", 1)
        both = later((gram_up, swap(gram_up, "fsdp", 1)), q_own, mean)
        q_up = polynomial(*both)
        q_other = swap(q_own, "fsdp", 1)
        two = [jnp.where(even, q_own, q_other), jnp.where(even, q_other, q_own)]
        q_two = ctx_two(jnp.stack(two))
        q_up = ctx_two(q_up)
        both = later((gram_attn, got_attn), q_up[0])
        q_attn = ctx_two(polynomial(*both))
    else:
        grams = lax.psum(jnp.stack([gram_down, gram_gate, gram_up, gram_attn]), "fsdp")
        none = jnp.zeros_like(gram_up)
        q_down, q_gate, q_up, q_attn = (polynomial(grams[k], none) for k in range(4))
        q_two = ctx_two(jnp.stack([q_down, q_gate]))
        q_up, q_attn = ctx_two(q_up), ctx_two(q_attn)
        got_attn = grams
    share = w_query.shape[0]
    finals = f_gather_cols(later(finals, got_attn))
    q_two, q_up, q_attn = (jnp.stack(ctx_four(q)) for q in (q_two, q_up, q_attn))
    q_down, q_gate = q_two[:, 0], q_two[:, 1]
    ctx_place = place[:1]
    new_down = update(q_down, l_down, w_down, False, ctx_place)
    new_gate = update(q_gate, l_gate, w_gate, True, later(ctx_place, new_down))
    finals = z_gather_slow(later(finals, q_attn[0]), new_gate)
    result, input_grad = (
        jnp.concatenate(
            [finals[:, (2 * g + k) * share : (2 * g + k + 1) * share] for g in range(groups)], axis=1
        )
        for k in range(2)
    )
    input_grad = input_grad.astype(F32)
    turn = later(ctx_place, new_gate, finals, gain_sums)
    new_up = update(q_up, l_up, w_up, True, turn)

    new_query, new_key, new_value, new_out = attention_update(
        q_attn, (l_query, l_key, l_value, l_out), (w_query, w_key, w_value, w_out), later(ctx_place, new_up)
    )

    return (
        result[None],
        input_grad[None],
        grad_gain_one,
        grad_gain_two,
        g_query,
        g_key,
        g_value,
        g_out,
        g_gate,
        g_up,
        g_down,
        m_query,
        m_key,
        m_value,
        m_out,
        m_gate,
        m_up,
        m_down,
        new_query,
        new_key,
        new_value,
        new_out,
        new_gate,
        new_up,
        new_down,
    )


def solution(mesh):
    act = P("fsdp", "ctx", None)
    col, row, vec = P("fsdp", "tp"), P("tp", "fsdp"), P("fsdp")
    seven = (col, col, col, row, col, col, row)
    in_specs = (act, act, P("fsdp", None), vec, vec) + seven + seven
    out_specs = (act, act, vec, vec) + seven + seven + seven
    return jax.shard_map(body, mesh=mesh, in_specs=in_specs, out_specs=out_specs, check_vma=False)
```

```python
import functools
import math

import jax
import jax.numpy as jnp
from jax import lax
from jax.experimental import pallas as pl
from jax.experimental.pallas import tpu as pltpu
from jax.sharding import PartitionSpec as P

HEAD_DIM = 64
NS_STEPS = 5
EPS = 1e-05
THETA = 130000.0
MOMENTUM = 0.95
COEF_A = 3.4445
COEF_B = -4.775
COEF_C = 2.0315
RATE = 0.5
BF = jnp.bfloat16
F32 = jnp.float32
VMEM_LIMIT = 56 * 1024 * 1024


def dot(left, right, ldim=1, rdim=0):
    return lax.dot_general(
        left, right, (((ldim,), (rdim,)), ((), ())), preferred_element_type=F32
    )


def params():
    return pltpu.CompilerParams(vmem_limit_bytes=VMEM_LIMIT)


def lasting(microseconds):
    return pl.CostEstimate(
        flops=0, bytes_accessed=int(microseconds * 3690000), transcendentals=0
    )


def swap(value, axis, bit):
    size = lax.axis_size(axis)
    return lax.ppermute(value, axis, [(i, i ^ bit) for i in range(size)])


def later(value, *others):
    return lax.optimization_barrier((value, others))[0]


def ctx_two(value):
    return [value, swap(value, "ctx", 2)]


def ctx_four(two):
    value, far = two
    return [value, swap(value, "ctx", 1), far, swap(far, "ctx", 1)]


def ctx_parts(value):
    return ctx_four(ctx_two(value))


def pair():
    return lax.axis_size("fsdp") == 2


def f_scatter_cols(value):
    size = lax.axis_size("fsdp")
    rows, width = value.shape
    part = width // size
    if size == 2:
        own = lax.axis_index("fsdp")
        mine = lax.dynamic_slice_in_dim(value, own * part, part, 1)
        other = lax.dynamic_slice_in_dim(value, (1 - own) * part, part, 1)
        return jnp.concatenate([mine, swap(other, "fsdp", 1)], axis=0)
    cut = jnp.swapaxes(value.reshape(rows, size, part), 0, 1)
    return lax.all_to_all(cut, "fsdp", 0, 0, tiled=True).reshape(size * rows, part)


def f_gather_cols(value):
    size = lax.axis_size("fsdp")
    rows = value.shape[0] // size
    if size == 2:
        own = lax.axis_index("fsdp")
        mine, other = value[:rows], swap(value[rows:], "fsdp", 1)
        return jnp.concatenate(
            [jnp.where(own == 0, mine, other), jnp.where(own == 0, other, mine)], axis=1
        )
    cut = lax.all_to_all(value.reshape(size, rows, -1), "fsdp", 0, 0, tiled=True)
    return jnp.swapaxes(cut, 0, 1).reshape(rows, -1)


def f_gather_rows(value):
    if pair():
        return jnp.concatenate([value, swap(value, "fsdp", 1)], axis=0)
    return lax.all_gather(value, "fsdp", axis=0, tiled=True)


def f_reduce_rows(value):
    size = lax.axis_size("fsdp")
    rows = value.shape[0] // size
    if size == 2:
        return value[:rows].astype(F32) + swap(value[rows:].astype(BF), "fsdp", 1).astype(F32)
    return lax.psum_scatter(value.astype(F32), "fsdp", scatter_dimension=0, tiled=True)


def flip(value):
    half = value.shape[0] // 2
    return jnp.concatenate([value[half:], value[:half]], axis=0)


def f_all(value):
    if pair():
        return value + flip(swap(value, "fsdp", 1))
    return lax.psum(value, "fsdp")


def f_reduce_list(parts):
    rows = parts[0].shape[0] // 2
    sent = jnp.concatenate([p[rows:].astype(BF) for p in parts], axis=1)
    return jnp.concatenate([p[:rows] for p in parts], axis=1) + swap(sent, "fsdp", 1).astype(F32)


def z_shift(value, k):
    size = lax.axis_size("tp")
    return lax.ppermute(value, "tp", [(i, (i + k) % size) for i in range(size)])


def z_shifts():
    size = lax.axis_size("tp")
    return sorted(range(1, size), key=lambda k: -min(k, size - k))


def by_quarter(value):
    size, groups = lax.axis_size("tp"), lax.axis_size("fsdp")
    rows, width = value.shape
    part = rows // (size * groups)
    cut = jnp.swapaxes(value.reshape(groups, size, part, width), 0, 1)
    return cut.reshape(size, groups * part, width)


def own_quarter(value):
    return lax.dynamic_index_in_dim(by_quarter(value), lax.axis_index("tp"), 0, keepdims=False)


def z_reduce(value):
    sent = by_quarter(value.astype(BF))
    return jnp.sum(lax.all_to_all(sent, "tp", 0, 0, tiled=True).astype(F32), axis=0)


def z_gather(value):
    size, groups = lax.axis_size("tp"), lax.axis_size("fsdp")
    rows, width = value.shape
    full = lax.all_gather(value, "tp", axis=0)
    full = jnp.swapaxes(full.reshape(size, groups, rows // groups, width), 0, 1)
    return full.reshape(size * rows, width)


def z_reduce_slow(value):
    size, me = lax.axis_size("tp"), lax.axis_index("tp")
    cut = by_quarter(value)
    total = lax.dynamic_index_in_dim(cut, me, 0, keepdims=False).astype(F32)
    for k in z_shifts():
        sent = lax.dynamic_index_in_dim(cut, (me + k) % size, 0, keepdims=False).astype(BF)
        total = total + z_shift(sent, k).astype(F32)
    return total


def z_gather_groups_slow(value, wait=()):
    size, groups = lax.axis_size("tp"), lax.axis_size("fsdp")
    rows, width = value.shape
    full = z_gather_slow(value, wait).reshape(size, groups, rows // groups, width)
    return jnp.swapaxes(full, 0, 1).reshape(size * rows, width)


def z_gather_slow(value, wait=()):
    size, me = lax.axis_size("tp"), lax.axis_index("tp")
    by_place = {k: later(z_shift(value, k), wait) for k in z_shifts()}
    by_place[0] = value
    ordered = []
    for at in range(size):
        chosen = value
        for k in z_shifts():
            chosen = jnp.where((me - k) % size == at, by_place[k], chosen)
        ordered.append(chosen)
    return jnp.concatenate(ordered, axis=0)


def all_sum(value, axes):
    for axis in axes:
        size = lax.axis_size(axis)
        if axis == "tp":
            value = value + sum(z_shift(value, k) for k in z_shifts())
        else:
            bit = 1
            while bit < size:
                value = value + swap(value, axis, bit)
                bit *= 2
    return value


def rope_tables(position, width):
    half = HEAD_DIM // 2
    freq = THETA ** (-(jnp.arange(half, dtype=F32) * 2.0 / HEAD_DIM))
    angle = position[:, None] * freq[None, :]
    repeat = width // half
    return jnp.tile(jnp.cos(angle), (1, repeat)), jnp.tile(jnp.sin(angle), (1, repeat))


def first_half(shape):
    lane = lax.broadcasted_iota(jnp.int32, shape, 1)
    return (lane & (HEAD_DIM - 1)) < HEAD_DIM // 2


def rotate(values, cosine, sine):
    half = HEAD_DIM // 2
    turned = jnp.where(
        first_half(values.shape), -jnp.roll(values, -half, 1), jnp.roll(values, half, 1)
    )
    return values * cosine + turned * sine


def unrotate(grads, cosine, sine):
    half = HEAD_DIM // 2
    scaled = grads * sine
    back = jnp.where(
        first_half(grads.shape), jnp.roll(scaled, -half, 1), -jnp.roll(scaled, half, 1)
    )
    return grads * cosine + back


def head_probs(query, keys, allowed, scale):
    scores = jnp.where(allowed, dot(query, keys, 1, 1) * scale, -1e30)
    top = jnp.max(scores, axis=1, keepdims=True)
    expo = jnp.exp(scores - top)
    return expo / jnp.sum(expo, axis=1, keepdims=True)


def attention_kernel(scale, q_ref, k_ref, v_ref, qi_ref, qs_ref, ki_ref, ks_ref, o_ref):
    allowed = (ks_ref[...] == qs_ref[...]) & (ki_ref[...] <= qi_ref[...])
    query, keys, values = q_ref[...], k_ref[...], v_ref[...]
    lane = lax.broadcasted_iota(jnp.int32, query.shape, 1)
    outs = []
    for head in range(2):
        mine = (lane >= HEAD_DIM) == (head == 1)
        prob = head_probs(jnp.where(mine, query, 0), keys, allowed, scale)
        outs.append(dot(prob.astype(BF), values))
    o_ref[...] = jnp.where(lane < HEAD_DIM, outs[0], outs[1]).astype(BF)


def attention_grad_kernel(
    scale, q_ref, k_ref, v_ref, g_ref, qi_ref, qs_ref, ki_ref, ks_ref, dq_ref, dk_ref, dv_ref
):
    allowed = (ks_ref[...] == qs_ref[...]) & (ki_ref[...] <= qi_ref[...])
    query, keys, values, grads = q_ref[...], k_ref[...], v_ref[...], g_ref[...]
    lane = lax.broadcasted_iota(jnp.int32, query.shape, 1)
    wide = lax.broadcasted_iota(jnp.int32, keys.shape, 1)
    dqs, dks, dvs = [], [], []
    for head in range(2):
        mine = (lane >= HEAD_DIM) == (head == 1)
        prob = head_probs(jnp.where(mine, query, 0), keys, allowed, scale)
        dprob = dot(jnp.where(mine, grads, 0), values, 1, 1)
        delta = jnp.sum(prob * dprob, axis=1, keepdims=True)
        dscore = (prob * (dprob - delta)).astype(BF)
        dqs.append(dot(dscore, keys))
        dks.append(dot(dscore, query, 0, 0))
        dvs.append(dot(prob.astype(BF), grads, 0, 0))
    low, wlow = lane < HEAD_DIM, wide < HEAD_DIM
    dq_ref[...] = jnp.where(low, dqs[0], dqs[1]) * scale
    dk_ref[...] = (jnp.where(wlow, dks[0], dks[1]) * scale).astype(BF)
    dv_ref[...] = jnp.where(wlow, dvs[0], dvs[1]).astype(BF)


def attention_specs(rows, keys):
    def col(n):
        return pl.BlockSpec((n, 2 * HEAD_DIM), lambda h: (0, h))

    def whole(shape):
        return pl.BlockSpec(shape, lambda h: (0, 0))

    marks = [whole((rows, 1)), whole((rows, 1)), whole((1, keys)), whole((1, keys))]
    return col, marks


def attention(query, keys, values, marks):
    rows, width = query.shape
    count = keys.shape[0]
    col, mark_specs = attention_specs(rows, count)
    return pl.pallas_call(
        functools.partial(attention_kernel, 1.0 / math.sqrt(HEAD_DIM)),
        grid=(width // (2 * HEAD_DIM),),
        in_specs=[col(rows), col(count), col(count)] + mark_specs,
        out_specs=col(rows),
        out_shape=jax.ShapeDtypeStruct((rows, width), BF),
        compiler_params=params(),
        cost_estimate=lasting(5.5),
        name="attention",
    )(query, keys, values, *marks)


def attention_grad(query, keys, values, grads, marks):
    rows, width = query.shape
    count = keys.shape[0]
    col, mark_specs = attention_specs(rows, count)
    return pl.pallas_call(
        functools.partial(attention_grad_kernel, 1.0 / math.sqrt(HEAD_DIM)),
        grid=(width // (2 * HEAD_DIM),),
        in_specs=[col(rows), col(count), col(count), col(rows)] + mark_specs,
        out_specs=[col(rows), col(count), col(count)],
        out_shape=[
            jax.ShapeDtypeStruct((rows, width), F32),
            jax.ShapeDtypeStruct((count, width), BF),
            jax.ShapeDtypeStruct((count, width), BF),
        ],
        compiler_params=params(),
        cost_estimate=lasting(7),
        name="attention_grad",
    )(query, keys, values, grads, *marks)


def smem():
    return pl.BlockSpec(memory_space=pltpu.SMEM)


def units_kernel(x_ref, wg_ref, wu_ref, own_ref, sent_ref):
    for k, w_ref in enumerate((wg_ref, wu_ref)):
        part = dot(x_ref[...], w_ref[...])
        own_ref[k] = part
        sent_ref[k] = part.astype(BF)


def units(x, wgate, wup, at, count, tile=512):
    rows, depth = x.shape
    steps = count // tile
    weight = pl.BlockSpec((depth, tile), lambda n: (0, at * steps + n))
    out = pl.BlockSpec((2, rows, tile), lambda n: (0, 0, n))
    return pl.pallas_call(
        units_kernel,
        grid=(steps,),
        in_specs=[pl.BlockSpec((rows, depth), lambda n: (0, 0)), weight, weight],
        out_specs=[out, out],
        out_shape=[
            jax.ShapeDtypeStruct((2, rows, count), F32),
            jax.ShapeDtypeStruct((2, rows, count), BF),
        ],
        compiler_params=params(),
        cost_estimate=lasting(4.5),
        name="units",
    )(x, wgate, wup)


def hidden_kernel(paired, first, own_ref, got_ref, dh_ref, dgot_ref, wg_ref, wu_ref, *refs):
    if first:
        out_ref, acc_ref = refs
    else:
        before_ref, out_ref, acc_ref = refs
    half = dh_ref.shape[0] // 2

    def total(own, got):
        if not paired:
            return own
        got = got.astype(F32)
        return own + jnp.concatenate([got[half:], got[:half]], axis=0)

    gate = total(own_ref[0], got_ref[0])
    upper = total(own_ref[1], got_ref[1])
    dhid = total(dh_ref[...], dgot_ref[...])
    sigma = jax.nn.sigmoid(gate)
    silu = gate * sigma
    dgate = (dhid * upper * sigma * (1.0 + gate * (1.0 - sigma))).astype(BF)
    dup = (dhid * silu).astype(BF)
    out_ref[0] = (silu * upper).astype(BF)
    out_ref[1] = dgate
    out_ref[2] = dup
    grad = dot(dgate, wg_ref[...], 1, 1) + dot(dup, wu_ref[...], 1, 1)

    @pl.when(pl.program_id(0) == 0)
    def _():
        acc_ref[...] = grad if first else grad + before_ref[...]

    @pl.when(pl.program_id(0) > 0)
    def _():
        acc_ref[...] += grad


def hidden_units(own, got, dhid, dgot, wgate, wup, at, before=None, tile=512):
    _, rows, count = own.shape
    depth = wgate.shape[0]
    steps = count // tile
    weight = pl.BlockSpec((depth, tile), lambda n: (0, at * steps + n))
    trio = pl.BlockSpec((2, rows, tile), lambda n: (0, 0, n))
    lanes = pl.BlockSpec((rows, tile), lambda n: (0, at * steps + n))
    total = pl.BlockSpec((rows, depth), lambda n: (0, 0))
    args = [own, got, dhid, dgot, wgate, wup] + ([] if before is None else [before])
    return pl.pallas_call(
        functools.partial(hidden_kernel, pair(), before is None),
        grid=(steps,),
        in_specs=[trio, trio, lanes, lanes, weight, weight] + [total] * (len(args) - 6),
        out_specs=[pl.BlockSpec((3, rows, tile), lambda n: (0, 0, n)), total],
        out_shape=[
            jax.ShapeDtypeStruct((3, rows, count), BF),
            jax.ShapeDtypeStruct((rows, depth), F32),
        ],
        compiler_params=params(),
        cost_estimate=lasting(6),
        name="hidden_units",
    )(*args)


def joined(parts):
    return jnp.concatenate([r[...].reshape(r.shape[-2:]) for r in parts], axis=0)


def moved(total, mom_ref, g_ref, m_ref, l_ref):
    mom = MOMENTUM * mom_ref[...] + total
    g_ref[...] = total
    m_ref[...] = mom
    l_ref[...] = (total + MOMENTUM * mom).astype(BF)


def add_gram(gram_ref, look_ref, by_columns, hit, first):
    half = gram_ref.shape[1]

    def three():
        if by_columns:
            low, high = look_ref[:, :half], look_ref[:, half:]
        else:
            low, high = look_ref[:half, :], look_ref[half:, :]
        dim = 0 if by_columns else 1
        return [dot(x, y, dim, dim) for x, y in ((low, low), (low, high), (high, high))]

    @pl.when(jnp.logical_and(hit, first))
    def _():
        for k, value in enumerate(three()):
            gram_ref[k] = value

    @pl.when(jnp.logical_and(hit, jnp.logical_not(first)))
    def _():
        for k, value in enumerate(three()):
            gram_ref[k] += value


def gram_spec(size):
    half = size // 2
    return (
        pl.BlockSpec((3, half, half), lambda *at: (0, 0, 0)),
        jax.ShapeDtypeStruct((3, half, half), F32),
    )


def weight_grad_kernel(nl, nr, by_columns, base, filled, place_ref, *refs):
    lefts, rights = refs[:nl], refs[nl : nl + nr]
    mom_ref, g_ref, m_ref, l_ref, gram_ref = refs[nl + nr], *refs[-4:]
    tall, wide = g_ref.shape
    moved(dot(joined(lefts), joined(rights), 0, 0), mom_ref, g_ref, m_ref, l_ref)
    i, j = pl.program_id(0), pl.program_id(1)
    outer, inner = (j, i) if by_columns else (i, j)
    size = 2 * gram_ref.shape[1]
    count = (wide if by_columns else tall) // size

    if filled:

        @pl.when(jnp.logical_and(i == 0, j == 0))
        def _():
            gram_ref[...] = refs[nl + nr + 4][...]

    for k in range(count):
        at = pl.ds(k * size, size)
        look = l_ref.at[:, at] if by_columns else l_ref.at[at, :]
        add_gram(gram_ref, look, by_columns, base + outer * count + k == place_ref[0], inner == 0)


def weight_grad(
    place, lefts, rights, mom, size, by_columns, tile, planes=(None, None), span=None, into=None
):
    height, width = mom.shape
    part, parts = span or (0, 1)
    tm, tn = min(tile[0], height), min(tile[1], width)
    grid = [height // tm, width // tn]
    axis = 1 if by_columns else 0
    grid[axis] //= parts
    start = [0, 0]
    start[axis] = part * grid[axis]
    out = pl.BlockSpec((tm, tn), lambda i, j: (start[0] + i, start[1] + j))
    tok = sum(v.shape[-2] for v in lefts)

    def specs(values, plane, lanes, place_of):
        if plane is None:
            return [pl.BlockSpec((v.shape[0], lanes), lambda i, j: (0, place_of(i, j))) for v in values]
        return [
            pl.BlockSpec((1, v.shape[1], lanes), lambda i, j: (plane, 0, place_of(i, j)))
            for v in values
        ]

    whole_gram, gram_shape = gram_spec(size)
    in_specs = [smem()]
    in_specs += specs(lefts, planes[0], tm, lambda i, j: i)
    in_specs += specs(rights, planes[1], tn, lambda i, j: j)
    in_specs += [out]
    args = [place, *lefts, *rights, mom]
    aliases = {}
    if into is not None:
        aliases = {len(args) + k: k for k in range(3)}
        in_specs += [pl.BlockSpec(memory_space=pl.ANY)] * 3 + [whole_gram]
        args += list(into)
    blocks = (width if by_columns else height) // size // parts
    return pl.pallas_call(
        functools.partial(
            weight_grad_kernel, len(lefts), len(rights), by_columns, part * blocks, into is not None
        ),
        grid=tuple(grid),
        in_specs=in_specs,
        out_specs=[out, out, out, whole_gram],
        out_shape=[
            jax.ShapeDtypeStruct((height, width), F32),
            jax.ShapeDtypeStruct((height, width), F32),
            jax.ShapeDtypeStruct((height, width), BF),
            gram_shape,
        ],
        input_output_aliases=aliases,
        compiler_params=params(),
        cost_estimate=lasting(9),
        name="weight_grad",
    )(*args)


def attention_weights_kernel(count, place_ref, *refs):
    ones, grads, attns, mids = (refs[k * count : (k + 1) * count] for k in range(4))
    refs = refs[4 * count :]
    moms, outs, gram_ref = refs[:4], refs[4:16], refs[16]
    first = pl.program_id(0) == 0
    left = joined(ones)
    width = moms[0].shape[1]
    for k in range(3):
        right = jnp.concatenate([r[:, k * width : (k + 1) * width] for r in grads], axis=0)
        moved(dot(left, right, 0, 0), moms[k], *outs[3 * k : 3 * k + 3])
        add_gram(gram_ref, outs[3 * k + 2], True, place_ref[0] == k, first)
    moved(dot(joined(attns), joined(mids), 0, 0), moms[3], *outs[9:12])
    add_gram(gram_ref, outs[11], False, place_ref[0] == 3, first)


def attention_weights(place, ones, grads, attns, mids, moms, tile=256):
    share, width = moms[0].shape
    tile = min(tile, share)

    def cols(v):
        return pl.BlockSpec((v.shape[0], tile), lambda i: (0, i))

    def whole(v):
        return pl.BlockSpec(v.shape, lambda i: (0, 0))

    tall = pl.BlockSpec((tile, width), lambda i: (i, 0))
    wide = pl.BlockSpec((width, tile), lambda i: (0, i))
    gram, gram_shape = gram_spec(width)
    shapes = []
    for mom in moms:
        shapes += [jax.ShapeDtypeStruct(mom.shape, kind) for kind in (F32, F32, BF)]
    out = pl.pallas_call(
        functools.partial(attention_weights_kernel, len(ones)),
        grid=(share // tile,),
        in_specs=[smem()]
        + [cols(v) for v in ones]
        + [whole(v) for v in grads]
        + [whole(v) for v in attns]
        + [cols(v) for v in mids]
        + [tall, tall, tall, wide],
        out_specs=[tall] * 9 + [wide] * 3 + [gram],
        out_shape=shapes + [gram_shape],
        compiler_params=params(),
        cost_estimate=lasting(18),
        name="attention_weights",
    )(place, *ones, *grads, *attns, *mids, *moms)
    return out[:3], out[3:6], out[6:9], out[9:12], out[12]


def mlp_weights_kernel(count, base, filled, place_ref, *refs):
    twos, hids, dgates, dups, dys = (refs[k * count : (k + 1) * count] for k in range(5))
    refs = refs[5 * count :]
    moms, refs = refs[:3], refs[3:]
    before, refs = (refs[9:12], refs[12:]) if filled else (None, refs)
    outs, grams = refs[:9], refs[9:]
    j, i = pl.program_id(0), pl.program_id(1)

    if filled:

        @pl.when(jnp.logical_and(i == 0, j == 0))
        def _():
            for gram_ref, old in zip(grams, before):
                gram_ref[...] = old[...]

    two = joined(twos)
    hit, first = base + j == place_ref[0], i == 0
    moved(dot(two, joined(dgates), 0, 0), moms[0], *outs[:3])
    add_gram(grams[0], outs[2], True, hit, first)
    moved(dot(two, joined(dups), 0, 0), moms[1], *outs[3:6])
    add_gram(grams[1], outs[5], True, hit, first)
    moved(dot(joined(hids), joined(dys), 0, 0), moms[2], *outs[6:9])
    add_gram(grams[2], outs[8], False, hit, first)


def mlp_weights(place, twos, trios, dys, moms, size, span, into, tile=512):
    share, width = moms[0].shape
    part, parts = span
    blocks = width // size // parts
    tile = min(tile, share)

    def cols(v):
        return pl.BlockSpec((v.shape[0], tile), lambda j, i: (0, i))

    def plane(v, k):
        return pl.BlockSpec((1, v.shape[1], size), lambda j, i: (k, 0, j))

    tall = pl.BlockSpec((tile, size), lambda j, i: (i, part * blocks + j))
    wide = pl.BlockSpec((size, tile), lambda j, i: (part * blocks + j, i))
    gram, gram_shape = gram_spec(size)
    shapes = []
    for mom in moms:
        shapes += [jax.ShapeDtypeStruct(mom.shape, kind) for kind in (F32, F32, BF)]
    in_specs = [smem()] + [cols(v) for v in twos]
    for k in range(3):
        in_specs += [plane(v, k) for v in trios]
    in_specs += [cols(v) for v in dys] + [tall, tall, wide]
    args = [place, *twos, *trios, *trios, *trios, *dys, *moms]
    aliases = {len(args) + k: k for k in range(9)}
    in_specs += [pl.BlockSpec(memory_space=pl.ANY)] * 9 + [gram] * 3
    args += [v for out in into for v in out[:3]] + [out[3] for out in into]
    out = pl.pallas_call(
        functools.partial(mlp_weights_kernel, len(twos), part * blocks, True),
        grid=(blocks, share // tile),
        in_specs=in_specs,
        out_specs=[tall] * 6 + [wide] * 3 + [gram] * 3,
        out_shape=shapes + [gram_shape] * 3,
        input_output_aliases=aliases,
        compiler_params=params(),
        cost_estimate=lasting(24),
        name="mlp_weights",
    )(*args)
    return [(*out[3 * k : 3 * k + 3], out[9 + k]) for k in range(3)]


def polynomial_kernel(a_ref, b_ref, out_ref, full_ref):
    size, half = full_ref.shape[0], full_ref.shape[0] // 2
    corner = a_ref[1] + b_ref[1]
    full_ref[:half, :half] = a_ref[0] + b_ref[0]
    full_ref[:half, half:] = corner
    full_ref[half:, :half] = corner.T
    full_ref[half:, half:] = a_ref[2] + b_ref[2]
    row = lax.broadcasted_iota(jnp.int32, (size, size), 0)
    column = lax.broadcasted_iota(jnp.int32, (size, size), 1)
    eye = row == column

    def split(full):
        only = jnp.where(eye, full, 0.0)
        return (
            jnp.where(eye, 0.0, full),
            jnp.sum(only, axis=1, keepdims=True),
            jnp.sum(only, axis=0, keepdims=True),
        )

    def times(left, right):
        loff, lcol, lrow = left
        roff, rcol, rrow = right
        full = dot(loff.astype(BF), roff.astype(BF)) + lcol * roff + loff * rrow
        off, dcol, drow = split(full)
        return off, dcol + lcol * rcol, drow + lrow * rrow

    def mix(coefs, first, second, shift):
        off = coefs[0] * first[0] + coefs[1] * second[0]
        dcol = coefs[0] * first[1] + coefs[1] * second[1] + shift
        drow = coefs[0] * first[2] + coefs[1] * second[2] + shift
        return off, dcol, drow

    gram = split(full_ref[...])
    norm = jnp.sqrt(jnp.sum(gram[2])) + 1e-07
    inverse = 1.0 / (norm * norm)
    gram = tuple(part * inverse for part in gram)
    total = None
    for step in range(NS_STEPS):
        square = times(gram, gram)
        factor = mix((COEF_B, COEF_C), gram, square, COEF_A)
        total = factor if total is None else times(factor, total)
        if step < NS_STEPS - 1:
            gram = times(factor, times(factor, gram))
    weight = -RATE / norm
    off = (total[0] * weight).astype(BF)
    out_ref[:half] = off[:half, :half]
    out_ref[half:size] = off[:half, half:]
    out_ref[size : size + half] = off[half:, half:]
    diagonal = total[2] * weight
    high = diagonal.astype(BF).astype(F32)
    low = diagonal - high
    line = lax.broadcasted_iota(jnp.int32, (16, half), 0)
    tail = jnp.zeros((16, half), F32)
    for k, part in enumerate((high[:, :half], high[:, half:], low[:, :half], low[:, half:])):
        tail = jnp.where(line == k, part, tail)
    out_ref[size + half :] = tail.astype(BF)


def polynomial(a, b):
    half = a.shape[1]
    size = 2 * half
    return pl.pallas_call(
        polynomial_kernel,
        in_specs=[pl.BlockSpec(memory_space=pltpu.VMEM)] * 2,
        out_specs=pl.BlockSpec(memory_space=pltpu.VMEM),
        out_shape=jax.ShapeDtypeStruct((3 * half + 16, half), BF),
        scratch_shapes=[pltpu.VMEM((size, size), F32)],
        compiler_params=params(),
        cost_estimate=lasting(10),
        name="polynomial",
    )(a, b)


def unpack(packed, factor_ref, column):
    half = packed.shape[1]
    corner = packed[half : 2 * half]
    factor_ref[:half, :half] = packed[:half]
    factor_ref[:half, half:] = corner
    factor_ref[half:, :half] = corner.astype(F32).T.astype(BF)
    factor_ref[half:, half:] = packed[2 * half : 3 * half]
    ends = packed[3 * half :].astype(F32)
    line = jnp.concatenate([ends[0:1] + ends[2:3], ends[1:2] + ends[3:4]], axis=1)
    if not column:
        return line
    size = 2 * half
    eye = lax.broadcasted_iota(jnp.int32, (size, size), 0) == lax.broadcasted_iota(
        jnp.int32, (size, size), 1
    )
    return jnp.sum(jnp.where(eye, line, 0.0), axis=1, keepdims=True)


def stepped(look_ref, w_ref, o_ref, factor, diagonal, by_columns):
    look = look_ref[...]
    step = dot(look, factor) if by_columns else dot(factor, look)
    o_ref[...] = w_ref[...].astype(F32) + (step + look.astype(F32) * diagonal)


def update_kernel(by_columns, me_ref, q_ref, l_ref, w_ref, o_ref, factor_ref, line_ref):
    @pl.when(pl.program_id(1) == 0)
    def _():
        line_ref[...] = unpack(q_ref[0], factor_ref, not by_columns)

    stepped(l_ref, w_ref, o_ref, factor_ref[...], line_ref[...], by_columns)


def update(factors, look, weight, by_columns, me):
    _, packed, half = factors.shape
    size = 2 * half
    height, width = weight.shape
    if by_columns:
        tile = min(1024, height)
        grid = (width // size, height // tile)
        spec = pl.BlockSpec((tile, size), lambda b, i, me_ref: (i, b))
    else:
        tile = min(1024, width)
        grid = (height // size, width // tile)
        spec = pl.BlockSpec((size, tile), lambda b, i, me_ref: (b, i))
    return pl.pallas_call(
        functools.partial(update_kernel, by_columns),
        grid_spec=pltpu.PrefetchScalarGridSpec(
            num_scalar_prefetch=1,
            grid=grid,
            in_specs=[
                pl.BlockSpec((1, packed, half), lambda b, i, me_ref: (b ^ me_ref[0], 0, 0)),
                spec,
                spec,
            ],
            out_specs=spec,
            scratch_shapes=[
                pltpu.VMEM((size, size), BF),
                pltpu.VMEM((1, size) if by_columns else (size, 1), F32),
            ],
        ),
        out_shape=jax.ShapeDtypeStruct(weight.shape, F32),
        compiler_params=params(),
        cost_estimate=lasting(9),
        name="update",
    )(me, factors, look, weight)


def attention_update_kernel(me_ref, *refs):
    qs, looks, weights, outs = refs[:4], refs[4:8], refs[8:12], refs[12:16]
    factor_ref, row_ref, column_ref = refs[16:]

    @pl.when(pl.program_id(0) == 0)
    def _():
        for k in range(3):
            row_ref[k] = unpack(qs[k][0], factor_ref.at[k], False)
        column_ref[...] = unpack(qs[3][0], factor_ref.at[3], True)

    for k in range(3):
        stepped(looks[k], weights[k], outs[k], factor_ref[k], row_ref[k], True)
    stepped(looks[3], weights[3], outs[3], factor_ref[3], column_ref[...], False)


def attention_update(factors, looks, weights, me, tile=256):
    _, packed, half = factors.shape
    size = 2 * half
    share, width = weights[0].shape
    tile = min(tile, share)
    tall = pl.BlockSpec((tile, width), lambda i, me_ref: (i, 0))
    wide = pl.BlockSpec((width, tile), lambda i, me_ref: (0, i))

    def factor(k):
        return pl.BlockSpec((1, packed, half), lambda i, me_ref: (me_ref[0] ^ k, 0, 0))

    specs = [tall, tall, tall, wide]
    return pl.pallas_call(
        attention_update_kernel,
        grid_spec=pltpu.PrefetchScalarGridSpec(
            num_scalar_prefetch=1,
            grid=(share // tile,),
            in_specs=[factor(k) for k in range(4)] + specs + specs,
            out_specs=specs,
            scratch_shapes=[
                pltpu.VMEM((4, size, size), BF),
                pltpu.VMEM((3, 1, size), F32),
                pltpu.VMEM((size, 1), F32),
            ],
        ),
        out_shape=[jax.ShapeDtypeStruct(w.shape, F32) for w in weights],
        compiler_params=params(),
        cost_estimate=lasting(9),
        name="attention_update",
    )(me, factors, factors, factors, factors, *looks, *weights)


def body(
    tokens,
    out_grad,
    segment_start,
    norm_attn,
    norm_mlp,
    w_query,
    w_key,
    w_value,
    w_out,
    w_gate,
    w_up,
    w_down,
    mom_query,
    mom_key,
    mom_value,
    mom_out,
    mom_gate,
    mom_up,
    mom_down,
):
    rows = tokens.shape[1]
    me = lax.axis_index("ctx")
    groups = lax.axis_size("fsdp")
    place = jnp.stack([me, me]).astype(jnp.int32)
    width = w_query.shape[1]
    depth = tokens.shape[2]
    low_in = tokens[0]
    inputs = low_in.astype(F32)
    gain_one, gain_two = norm_attn.astype(F32), norm_mlp.astype(F32)

    spread = f_scatter_cols(low_in)
    inv_one = lax.rsqrt(jnp.mean(inputs * inputs, axis=1, keepdims=True) + EPS)
    inv_spread = f_gather_rows(inv_one)
    scaled = (spread.astype(F32) * gain_one).astype(BF)
    one_spread = (spread.astype(F32) * inv_spread * gain_one).astype(BF)

    partial = [dot(scaled, w) for w in (w_query, w_key, w_value)]
    if pair():
        qkv = f_reduce_list(partial)
    else:
        qkv = jnp.concatenate([f_reduce_rows(part) for part in partial], axis=1)
    qkv = later(qkv * inv_one, inv_spread)
    dy_spread = f_scatter_cols(out_grad[0])
    one_two, dy_two = ctx_two(one_spread), ctx_two(dy_spread)

    starts = segment_start[0]
    chunks = [(me ^ j) * rows for j in range(lax.axis_size("ctx"))]
    key_start = jnp.concatenate([lax.dynamic_slice_in_dim(starts, o, rows) for o in chunks])
    key_index = jnp.concatenate([o + jnp.arange(rows, dtype=jnp.int32) for o in chunks])
    query_start, query_index = key_start[:rows], key_index[:rows]
    cosine, sine = rope_tables((query_index - query_start).astype(F32), width)
    marks = (query_index[:, None], query_start[:, None], key_index[None], key_start[None])

    query = rotate(qkv[:, :width], cosine, sine).astype(BF)
    kv_own = jnp.concatenate(
        [rotate(qkv[:, width : 2 * width], cosine, sine), qkv[:, 2 * width :]], axis=1
    ).astype(BF)
    kv = jnp.concatenate(ctx_parts(kv_own), axis=0)
    keys, values = kv[:, :width], kv[:, width:]
    query = later(query, dy_spread)
    attn = attention(query, keys, values, marks)
    attn_rows = f_gather_rows(attn)

    dhid = dot(dy_spread, w_down, 1, 1)
    attn_two = ctx_two(attn_rows)
    attn_rows = later(attn_rows, dhid)

    own_in = own_quarter(spread).astype(F32)
    own_inv = own_quarter(inv_spread)
    own_dy = own_quarter(dy_spread).astype(F32)

    middle = own_in + later(z_reduce(dot(attn_rows, w_out)), dy_two[1], attn_two[1])
    squares = f_all(jnp.sum(middle * middle, axis=1, keepdims=True))
    inv_two = lax.rsqrt(squares * (1.0 / depth) + EPS)
    own_two = (middle * inv_two * gain_two).astype(BF)
    if pair():
        dhid_got = swap(later(dhid.astype(BF), own_two), "fsdp", 1)
    else:
        dhid_got = dhid = lax.psum(dhid, "fsdp")
    two_spread = later(z_gather(own_two), dhid_got)
    two_two = ctx_two(two_spread)

    halves = 2
    count = w_gate.shape[1] // halves
    parts = [units(two_spread, w_gate, w_up, p, count) for p in range(halves)]
    if pair():
        got = [swap(sent, "fsdp", 1) for _, sent in parts]
        owns = [own for own, _ in parts]
    else:
        owns = [lax.psum(own, "fsdp") for own, _ in parts]
        got = owns
    owns[0] = later(owns[0], owns[1], two_two[1], one_two[1])
    trios, dx_two = [], None
    for p in range(halves):
        trio, dx_two = hidden_units(
            owns[p], got[p], dhid, dhid_got, w_gate, w_up, p, before=dx_two
        )
        trios.append(trio)

    trio_twos = [ctx_two(trio) for trio in trios]
    grad_two = z_reduce_slow(dx_two)
    trio_alls = [ctx_four(later(two, grad_two)) for two in trio_twos]
    two_all, dy_all = ctx_four(later(two_two, grad_two)), ctx_four(later(dy_two, grad_two))
    scaled_two = middle * inv_two
    weighted = grad_two * gain_two
    mean = f_all(jnp.sum(weighted * scaled_two, axis=1, keepdims=True)) * (1.0 / depth)
    grad_middle = own_dy + inv_two * (weighted - scaled_two * mean)
    own_mid = later(grad_middle.astype(BF), trio_twos[0][1], trio_twos[1][1])
    span = (0, halves)
    gate_out = weight_grad(
        later(place, own_mid), two_all, trio_alls[0], mom_gate, width, True, (1024, 512), (None, 1),
        span=span,
    )
    mid_spread = z_gather_groups_slow(own_mid, gate_out)
    out_part = sum(
        dot(trio[0], w_down[p * count : (p + 1) * count]) for p, trio in enumerate(trios)
    ).astype(BF)
    out_sum = z_reduce(out_part)
    grad_attn = later(f_reduce_rows(dot(mid_spread, w_out, 1, 1)).astype(BF), out_part)

    dquery, dkeys, dvalues = attention_grad(query, keys, values, grad_attn, marks)
    dkv = jnp.concatenate([dkeys, dvalues], axis=1)
    up_out = weight_grad(
        later(place, dkv), two_all, trio_alls[0], mom_up, width, True, (1024, 512), (None, 2),
        span=span,
    )
    got_dkv = later(swap(dkv[2 * rows :], "ctx", 2), up_out)
    far = dkv[: 2 * rows].astype(F32) + got_dkv.astype(F32)
    near = far[:rows] + swap(far[rows:].astype(BF), "ctx", 1).astype(F32)
    dqkv = jnp.concatenate(
        [
            unrotate(dquery, cosine, sine),
            unrotate(near[:, :width], cosine, sine),
            near[:, width:],
        ],
        axis=1,
    ).astype(BF)
    mid_two = ctx_two(mid_spread)
    down_out = weight_grad(
        later(place, dqkv), trio_alls[0], dy_all, mom_down, width, False, (512, 1024), (0, None),
        span=span,
    )
    dqkv_rows = later(f_gather_rows(dqkv), mid_two[1], down_out)
    dqkv_two = ctx_two(dqkv_rows)
    dx_one = (
        dot(dqkv_rows[:, :width], w_query, 1, 1)
        + dot(dqkv_rows[:, width : 2 * width], w_key, 1, 1)
        + dot(dqkv_rows[:, 2 * width :], w_value, 1, 1)
    )
    gain_parts = jnp.stack(
        [
            jnp.sum(dx_one * one_spread.astype(F32), axis=0),
            jnp.sum(dx_two * two_spread.astype(F32), axis=0),
        ]
    )
    grad_one = z_reduce(dx_one)

    one_all = ctx_four(one_two)
    gate_out, up_out, down_out = mlp_weights(
        later(place, dqkv_rows, out_sum, gain_parts), two_all, trio_alls[1], dy_all, (mom_gate, mom_up, mom_down),
        width, (1, halves), (gate_out, up_out, down_out),
    )
    g_gate, m_gate, l_gate, gram_gate = gate_out
    g_up, m_up, l_up, gram_up = up_out
    g_down, m_down, l_down, gram_down = down_out

    mid_all, attn_all = ctx_four(later(mid_two, dqkv_rows)), ctx_four(attn_two)
    dqkv_all = ctx_four(later(dqkv_two, g_down))
    gain_sums = all_sum(gain_parts, ("ctx",))
    query_out, key_out, value_out, out_out, gram_attn = attention_weights(
        later(place, g_down, grad_one, gain_sums), one_all, dqkv_all, attn_all, mid_all,
        (mom_query, mom_key, mom_value, mom_out),
    )
    g_query, m_query, l_query = query_out
    g_key, m_key, l_key = key_out
    g_value, m_value, l_value = value_out
    g_out, m_out, l_out = out_out

    out_sum, grad_one, gain_sums = later((out_sum, grad_one, gain_sums), g_value)
    result = middle + out_sum
    scaled_one = own_in * own_inv
    weighted = grad_one * gain_one
    mean = f_all(jnp.sum(weighted * scaled_one, axis=1, keepdims=True)) * (1.0 / depth)
    input_grad = grad_middle + own_inv * (weighted - scaled_one * mean)
    finals = jnp.concatenate([result, input_grad], axis=1).astype(BF)

    gain_sums = all_sum(gain_sums, ("tp",))
    grad_gain_one = gain_sums[0] / gain_one
    grad_gain_two = gain_sums[1] / gain_two

    if pair():
        even = lax.axis_index("fsdp") == 0
        kept = jnp.where(even, gram_down, gram_gate)
        sent = jnp.where(even, gram_gate, gram_down)
        both = later((kept, swap(sent, "fsdp", 1)), g_value)
        q_own = polynomial(*both)
        got_attn = swap(gram_attn, "fsdp", 1)
        both = later((gram_up, swap(gram_up, "fsdp", 1)), q_own, mean)
        q_up = polynomial(*both)
        q_other = swap(q_own, "fsdp", 1)
        two = [jnp.where(even, q_own, q_other), jnp.where(even, q_other, q_own)]
        q_two = ctx_two(jnp.stack(two))
        q_up = ctx_two(q_up)
        both = later((gram_attn, got_attn), q_up[0])
        q_attn = ctx_two(polynomial(*both))
    else:
        grams = lax.psum(jnp.stack([gram_down, gram_gate, gram_up, gram_attn]), "fsdp")
        none = jnp.zeros_like(gram_up)
        q_down, q_gate, q_up, q_attn = (polynomial(grams[k], none) for k in range(4))
        q_two = ctx_two(jnp.stack([q_down, q_gate]))
        q_up, q_attn = ctx_two(q_up), ctx_two(q_attn)
        got_attn = grams
    share = w_query.shape[0]
    finals = f_gather_cols(later(finals, got_attn))
    q_two, q_up = later((q_two, q_up), q_attn[0])
    q_two, q_up, q_attn = (jnp.stack(ctx_four(q)) for q in (q_two, q_up, q_attn))
    q_down, q_gate = q_two[:, 0], q_two[:, 1]
    ctx_place = place[:1]
    new_down = update(q_down, l_down, w_down, False, ctx_place)
    new_gate = update(q_gate, l_gate, w_gate, True, later(ctx_place, new_down))
    finals = z_gather_slow(later(finals, q_attn[0]), new_gate)
    result, input_grad = (
        jnp.concatenate(
            [finals[:, (2 * g + k) * share : (2 * g + k + 1) * share] for g in range(groups)], axis=1
        )
        for k in range(2)
    )
    input_grad = input_grad.astype(F32)
    turn = later(ctx_place, new_gate, finals, gain_sums)
    new_up = update(q_up, l_up, w_up, True, turn)

    new_query, new_key, new_value, new_out = attention_update(
        q_attn, (l_query, l_key, l_value, l_out), (w_query, w_key, w_value, w_out), later(ctx_place, new_up)
    )

    return (
        result[None],
        input_grad[None],
        grad_gain_one,
        grad_gain_two,
        g_query,
        g_key,
        g_value,
        g_out,
        g_gate,
        g_up,
        g_down,
        m_query,
        m_key,
        m_value,
        m_out,
        m_gate,
        m_up,
        m_down,
        new_query,
        new_key,
        new_value,
        new_out,
        new_gate,
        new_up,
        new_down,
    )


def solution(mesh):
    act = P("fsdp", "ctx", None)
    col, row, vec = P("fsdp", "tp"), P("tp", "fsdp"), P("fsdp")
    seven = (col, col, col, row, col, col, row)
    in_specs = (act, act, P("fsdp", None), vec, vec) + seven + seven
    out_specs = (act, act, vec, vec) + seven + seven + seven
    return jax.shard_map(body, mesh=mesh, in_specs=in_specs, out_specs=out_specs, check_vma=False)
```
